32 devices in a mesh: groups: 2 (over y), dev: 4 (over z), view: 2 (over x), chip: 2 (over core).
Axes of the slice: x: 2, y: 2, z: 4, core: 2. Of those that a mesh axis runs over, the one named last changes fastest.
Arguments:
- params: float32 [58, 32768], P(None, ('groups', 'dev')), parts along dimension 1
- cameras: float32 [4, 2, 4], P(('groups', 'view')), parts along dimension 0
- view_basis: float32 [4, 16], P(('groups', 'view')), parts along dimension 0, may hold values from -0.6 to 0.6
- tile_lists: int32 [2, 8, 2, 16], P('view', ('groups', 'dev'), 'chip'), parts along dimension 1, may hold values from 0 to 127, as said below
- margin_blocks: int32 [2, 8, 2, 16, 256], P('view', ('groups', 'dev'), 'chip'), parts along dimension 1, may hold values from 0 to 3839, as said below
- depth_orders: int32 [2, 8, 2, 16, 256], P('view', ('groups', 'dev'), 'chip'), parts along dimension 1, may hold values from 0 to 255, as said below
- tile_counts: int32 [2, 8, 2, 16], P('view', ('groups', 'dev'), 'chip'), parts along dimension 1, may hold values from 0 to 256, as said below
- requests: int32 [2, 4, 2, 8, 960], P('view', None, 'chip', ('groups', 'dev')), parts along dimension 3, may hold values from 0 to 4095, as said below
- target: float32 [2, 8, 2, 16, 3, 256], P('view', ('groups', 'dev'), 'chip'), parts along dimension 1, may hold values from -3 to 3
Outputs:
- grads: float32 [58, 32768], P(None, ('groups', 'dev', 'view', 'chip')), parts along dimension 1
- images: float32 [2, 8, 2, 16, 3, 256], P('view', ('groups', 'dev'), 'chip'), parts along dimension 1
The draws below stay inside these ranges and needn't reach their ends.
There are 2 independent parts, one for each index of `groups`. The reference program is written for one: setup_inputs(seed, part) draws one part's arguments, and reference() takes and returns one part's arrays. A program takes and returns all parts, laid end to end along the dimension named above; each array names one. Nothing has to cross between parts.
Inputs may be any that keep to these rules, and one draw needn't show every extreme that they name: `tile_lists`: each view's tiles are a permutation of 0 .. 127, 16 to a device. `margin_blocks`: every live entry names a slot that no other live entry of the same device names; a tile's live Gaussians lie near it on the image; dead entries hold 0. `depth_orders`: each row is a permutation of 0 .. 255 whose first tile_counts entries are the live entries of the block. `tile_counts`: live entries come first in depth order; some tile of every draw is full. `requests`: local Gaussian indices; slots that no live entry of the receiving device names hold 0; for some receiving device some shard fills all 960 slots.
All inputs are finite; a program needn't handle non-finite values.
Results may differ from the reference program's by a relative error of at most 0.0003.
Values sent between devices are 32-bit elements; how exact they have to be, the bound alone decides.
No kernel may reach another device: no remote copies, remote signals or barrier semaphores. Data moves between devices by JAX's collectives and lax.ppermute only.
A program may use at most 64 MiB of HBM per device.

```python
from functools import partial
import jax
import jax.numpy as jnp
from jax import lax

SIDE = 16
PIXELS = 256
COEFS = 16
GPT = 128
SPILL = 32
K = 256
TILES_DEV = 16
TW = 16
VIEWS = 2
TILES_VIEW = 128
G_DEV = 4096
GAUSS = 16384
CAP = 960
N_DEV = 4
N_CHIP = 2


def anchor_layout(key):
    return jax.random.permutation(jax.random.fold_in(key, 901), GAUSS).astype(jnp.int32)


def pair_layout(key):
    placing = anchor_layout(key)
    holder = jnp.zeros((GAUSS,), jnp.int32).at[placing].set(jnp.arange(GAUSS, dtype=jnp.int32))
    tile_rows = TILES_VIEW // TW
    tile = jnp.arange(TILES_VIEW, dtype=jnp.int32)
    column = tile % TW
    row_index = tile // TW
    entry = jnp.arange(K, dtype=jnp.int32)
    own = entry < GPT
    side = jnp.clip((entry - GPT) // SPILL, 0, 3)
    within = (entry - GPT) % SPILL
    step_x = jnp.array([-1, 1, 0, 0], jnp.int32)[side]
    step_y = jnp.array([0, 0, -1, 1], jnp.int32)[side]
    spill_code = jnp.array([1, 0, 3, 2], jnp.int32)[side]
    near_x = column[:, None] + jnp.where(own, 0, step_x)[None, :]
    near_y = row_index[:, None] + jnp.where(own, 0, step_y)[None, :]
    inside = (near_x >= 0) & (near_x < TW) & (near_y >= 0) & (near_y < tile_rows)
    source_tile = jnp.clip(near_y, 0, tile_rows - 1) * TW + jnp.clip(near_x, 0, TW - 1)
    anchor_rank = jnp.where(own, entry, spill_code * SPILL + within)[None, :]
    tile_ids = holder[source_tile * GPT + anchor_rank]
    lists = jnp.stack([jax.random.permutation(jax.random.fold_in(key, 910 + view), TILES_VIEW).astype(jnp.int32) for view in range(VIEWS)])
    lists = lists.reshape(VIEWS, N_DEV, N_CHIP, TILES_DEV)
    receivers = VIEWS * N_DEV * N_CHIP
    pair_ids = tile_ids[lists].reshape(receivers, TILES_DEV * K)
    pair_valid = inside[lists].reshape(receivers, TILES_DEV * K)
    source = pair_ids // G_DEV
    local = pair_ids % G_DEV

    def ranks(inputs):
        shard_of, valid_of = inputs
        onehot = ((shard_of[:, None] == jnp.arange(N_DEV, dtype=jnp.int32)[None, :]) & valid_of[:, None]).astype(jnp.int32)
        before = jnp.cumsum(onehot, axis=0) - onehot
        return jnp.sum(before * onehot, axis=1)
    rank_in = lax.map(ranks, (source, pair_valid))
    keep = pair_valid & (rank_in < CAP)
    slot = source * CAP + rank_in

    def fill(slot_of, keep_of, local_of):
        target_slot = jnp.where(keep_of, slot_of, N_DEV * CAP)
        return jnp.zeros((N_DEV * CAP,), jnp.int32).at[target_slot].set(local_of, mode='drop')
    requests = jax.vmap(fill)(slot, keep, local).reshape(VIEWS, N_DEV, N_CHIP, N_DEV, CAP)
    blocks = jnp.where(keep, slot, 0).reshape(VIEWS, N_DEV, N_CHIP, TILES_DEV, K)
    keep_tiles = keep.reshape(VIEWS, N_DEV, N_CHIP, TILES_DEV, K)
    counts = jnp.sum(keep_tiles.astype(jnp.int32), axis=4)
    scores = jax.random.randint(jax.random.fold_in(key, 930), keep_tiles.shape, 0, 4096) * K + entry
    scores = jnp.where(keep_tiles, scores, 4096 * K * 2 + entry)
    orders = jnp.argsort(scores, axis=4, stable=True).astype(jnp.int32)
    return (lists, blocks, orders, counts, requests)


def draw_tile_lists(key, part):
    return pair_layout(key)[0]


def draw_margin_blocks(key, part):
    return pair_layout(key)[1]


def draw_depth_orders(key, part):
    return pair_layout(key)[2]


def draw_tile_counts(key, part):
    return pair_layout(key)[3]


def draw_requests(key, part):
    return pair_layout(key)[4]


def draw_params(key, part):
    placing = anchor_layout(key)
    key = jax.random.fold_in(key, 5)
    keys = jax.random.split(key, 7)
    tile = placing // GPT
    anchor_rank = placing % GPT
    direction = jnp.where(anchor_rank < 4 * SPILL, anchor_rank // SPILL, 4)
    column = (tile % TW).astype(jnp.float32)
    row_index = (tile // TW).astype(jnp.float32)
    low_x = jnp.array([-0.1, 0.85, 0.15, 0.15, 0.15], jnp.float32)[direction]
    high_x = jnp.array([0.15, 1.1, 0.85, 0.85, 0.85], jnp.float32)[direction]
    low_y = jnp.array([0.15, 0.15, -0.1, 0.85, 0.15], jnp.float32)[direction]
    high_y = jnp.array([0.85, 0.85, 0.15, 1.1, 0.85], jnp.float32)[direction]
    spread_x = jax.random.uniform(keys[0], (GAUSS,), jnp.float32)
    spread_y = jax.random.uniform(keys[1], (GAUSS,), jnp.float32)
    place_x = column + low_x + (high_x - low_x) * spread_x
    place_y = row_index + low_y + (high_y - low_y) * spread_y
    height = jax.random.uniform(keys[2], (GAUSS,), jnp.float32, -0.5, 0.5)
    diagonal = jnp.exp(jax.random.uniform(keys[3], (3, GAUSS), jnp.float32, jnp.log(0.08), jnp.log(0.3)))
    offdiag = jax.random.uniform(keys[4], (3, GAUSS), jnp.float32, -0.08, 0.08)
    logit = jax.random.uniform(keys[5], (GAUSS,), jnp.float32, -3.0, 0.0)
    harmonics = 0.3 * jnp.clip(jax.random.normal(keys[6], (3 * COEFS, GAUSS), jnp.float32), -5.0, 5.0)
    geometry = jnp.stack([place_x, place_y, height, diagonal[0], offdiag[0], diagonal[1], offdiag[1], offdiag[2], diagonal[2], logit])
    return jnp.concatenate([geometry, harmonics], axis=0).astype(jnp.float32)


def draw_cameras(key, part):
    key = jax.random.fold_in(key, 11)
    noise = jax.random.uniform(key, (VIEWS, 2, 4), jnp.float32, -1.0, 1.0)
    base = jnp.array([[SIDE, 0.0, 0.0, 0.0], [0.0, SIDE, 0.0, 0.0]], jnp.float32)
    spread = jnp.array([[0.03, 0.03, 3.0, 2.0], [0.03, 0.03, 3.0, 2.0]], jnp.float32)
    return (base[None] + spread[None] * noise).astype(jnp.float32)


def level_of(key, extent, cuts, least, top_value):
    loudness = 1.0
    for dim, parts in cuts:
        draws = jax.random.uniform(jax.random.fold_in(jax.random.fold_in(key, 6), dim), (parts,), jnp.float32, least / len(cuts), top_value / len(cuts))
        loudness = loudness * jnp.repeat(jnp.exp(draws), extent[dim] // parts).reshape((-1,) + (1,) * (len(extent) - 1 - dim))
    return loudness


def centred(own_key, shape, deviation, bound, shards=(), held_as=jnp.bfloat16):
    gain = level_of(own_key, shape, shards, -0.22, 0.18) if shards else 1.0
    drawn = jax.random.normal(own_key, shape, jnp.float32) * deviation * gain
    return jnp.minimum(jnp.maximum(drawn, -bound), bound).astype(held_as)


def setup_inputs(seed: int = 0, part: int = 0) -> dict:
    key_of = jax.random.split(jax.random.key(seed), 10)
    own_keys = jax.random.split(jax.random.fold_in(key_of[9], part), 10)
    return {
        "params": draw_params(jax.random.fold_in(jax.random.fold_in(key_of[9], part), 71), part),
        "cameras": draw_cameras(jax.random.fold_in(jax.random.fold_in(key_of[9], part), 71), part),
        "view_basis": jnp.clip(jax.random.uniform(own_keys[2], (VIEWS, COEFS), jnp.float32, -0.6, 0.6) * level_of(own_keys[2], (VIEWS, COEFS), ((0, 2),), -0.4, 0.0), -0.6, 0.6),
        "tile_lists": draw_tile_lists(jax.random.fold_in(jax.random.fold_in(key_of[9], part), 71), part),
        "margin_blocks": draw_margin_blocks(jax.random.fold_in(jax.random.fold_in(key_of[9], part), 71), part),
        "depth_orders": draw_depth_orders(jax.random.fold_in(jax.random.fold_in(key_of[9], part), 71), part),
        "tile_counts": draw_tile_counts(jax.random.fold_in(jax.random.fold_in(key_of[9], part), 71), part),
        "requests": draw_requests(jax.random.fold_in(jax.random.fold_in(key_of[9], part), 71), part),
        "target": centred(own_keys[8], (VIEWS, N_DEV, N_CHIP, TILES_DEV, 3, PIXELS), 0.5, 3.0, ((0, 2), (1, 4), (2, 2)), jnp.float32),
    }


dilation = 0.3

def project(columns, camera, basis):
    highest = lax.Precision.HIGHEST
    linear = camera[:, 0:3]
    means = jnp.dot(linear, columns[0:3], precision=highest) + camera[:, 3][:, None]
    diag_x = columns[3]
    cross_yx = columns[4]
    diag_y = columns[5]
    cross_zx = columns[6]
    cross_zy = columns[7]
    diag_z = columns[8]
    world_xx = diag_x * diag_x
    world_xy = diag_x * cross_yx
    world_xz = diag_x * cross_zx
    world_yy = cross_yx * cross_yx + diag_y * diag_y
    world_yz = cross_yx * cross_zx + diag_y * cross_zy
    world_zz = cross_zx * cross_zx + cross_zy * cross_zy + diag_z * diag_z
    world = jnp.stack([jnp.stack([world_xx, world_xy, world_xz]), jnp.stack([world_xy, world_yy, world_yz]), jnp.stack([world_xz, world_yz, world_zz])])
    halfway = jnp.einsum('ij,jkn->ikn', linear, world, precision=highest)
    screen = jnp.einsum('ikn,lk->iln', halfway, linear, precision=highest)
    upper = screen[0, 0] + dilation
    cross = screen[0, 1]
    lower = screen[1, 1] + dilation
    determinant = upper * lower - cross * cross
    opacity = jax.nn.sigmoid(columns[9])
    harmonics = columns[10:].reshape(3, basis.shape[0], columns.shape[1])
    colour = jnp.einsum('k,ckn->cn', basis, harmonics, precision=highest) + 0.5
    shape_rows = jnp.stack([lower / determinant, -cross / determinant, upper / determinant, opacity])
    return jnp.concatenate([means, shape_rows, colour], axis=0)

def tile_pixels(tile_id):
    within = jnp.arange(PIXELS, dtype=jnp.int32)
    column = tile_id % TW * SIDE + within % SIDE
    row_index = tile_id // TW * SIDE + within // SIDE
    return (column.astype(jnp.float32) + 0.5, row_index.astype(jnp.float32) + 0.5)

def render(values, live_mask, across, downward):
    offset_x = across[None, :] - values[0][:, None]
    offset_y = downward[None, :] - values[1][:, None]
    quadric = 0.5 * (values[2][:, None] * offset_x * offset_x + 2.0 * values[3][:, None] * offset_x * offset_y + values[4][:, None] * offset_y * offset_y)
    alpha = (live_mask * values[5])[:, None] * jnp.exp(-quadric)
    logs = jnp.log1p(-alpha)
    before = jnp.exp(jnp.cumsum(logs, axis=0) - logs)
    return jnp.dot(values[6:9], before * alpha, precision=lax.Precision.HIGHEST)

def tile_step(features_all, slot_ids, ordering, live_count, tile_id, target_tile):
    ordered = jnp.take(slot_ids, ordering)
    live_mask = (jnp.arange(ordering.shape[0], dtype=jnp.int32) < live_count).astype(jnp.float32)
    gathered = jnp.take(features_all, ordered, axis=1)
    across, downward = tile_pixels(tile_id)
    image, pullback = jax.vjp(lambda values: render(values, live_mask, across, downward), gathered)
    cotangent = pullback(image - target_tile)[0]
    return (image, cotangent, ordered)

def reference(params, cameras, view_basis, tile_lists, margin_blocks, depth_orders, tile_counts, requests, target):
    grads = jnp.zeros(params.shape, jnp.float32)
    images = []
    many = N_DEV * N_CHIP * TILES_DEV
    for view in range(VIEWS):
        camera = cameras[view]
        basis = view_basis[view]
        features_all = project(params, camera, basis)
        shard_start = (jnp.arange(N_DEV, dtype=jnp.int32) * G_DEV)[None, None, :, None]
        global_ids = (requests[view] + shard_start).reshape(N_DEV, N_CHIP, 1, N_DEV * CAP)
        global_ids = jnp.broadcast_to(global_ids, (N_DEV, N_CHIP, TILES_DEV, N_DEV * CAP))
        entry_ids = jnp.take_along_axis(global_ids, margin_blocks[view], axis=3)
        grouped = (entry_ids.reshape(many // 4, 4, K), depth_orders[view].reshape(many // 4, 4, K), tile_counts[view].reshape(many // 4, 4), tile_lists[view].reshape(many // 4, 4), target[view].reshape(many // 4, 4, 3, PIXELS))

        def four_tiles(inputs):
            return jax.vmap(partial(tile_step, features_all))(*inputs)
        image, cotangent, ordered = lax.map(four_tiles, grouped)
        images.append(image.reshape(N_DEV, N_CHIP, TILES_DEV, 3, PIXELS))
        feature_grad = jax.ops.segment_sum(jnp.swapaxes(cotangent.reshape(many, 9, K), 1, 2).reshape(many * K, 9), ordered.reshape(many * K), GAUSS).T
        pullback = jax.vjp(lambda columns: project(columns, camera, basis), params)[1]
        grads = grads + pullback(feature_grad)[0]
    return (grads, jnp.stack(images))
```

```python
from functools import partial

import jax
import jax.numpy as jnp
from jax import lax
from jax.experimental import pallas as pl
from jax.experimental.pallas import tpu as pltpu
from jax.sharding import PartitionSpec as P

SIDE = 16
TW = 16
LANES = 128
LOG2E = 1.4426950408889634
LN2 = 0.6931471805599453
DILATION = 0.3
DEAD = -1e30
F32 = jnp.float32
BF16 = jnp.bfloat16
FEATS = 9


def lane_take(row, index):
    return jnp.take_along_axis(row, index, axis=1, mode="promise_in_bounds")


def split2(x):
    hi = x.astype(BF16)
    return hi, (x - hi.astype(F32)).astype(BF16)


def dot(a, b, ca, cb):
    return lax.dot_general(a, b, (((ca,), (cb,)), ((), ())), preferred_element_type=F32)


def send_kernel(me_ref, cam_ref, basis_ref, params_ref, req_ref, *refs, nd, cap, rows):
    outs = refs[:nd]
    idx_out, w_out, feat, w_scr = refs[nd:]
    me = me_ref[0]
    width = params_ref.shape[1]
    coefs = basis_ref.shape[-1]
    idx_out[...] = jnp.zeros_like(idx_out)
    for j in range(nd):
        dest = lax.rem(me + j, nd)
        for i in range(rows):
            size = min(LANES, cap - i * LANES)
            idx_out[j * rows + i : j * rows + i + 1, 0:size] = req_ref[
                0, dest, 0, 0:1, i * LANES : i * LANES + size
            ]
    w_scr[...] = jnp.zeros_like(w_scr)
    w_scr[0:2, 0:4] = cam_ref[0]
    w_scr[2:3, 0:coefs] = basis_ref[...]
    packed = w_scr[...]
    lane8 = lax.broadcasted_iota(jnp.int32, (8, LANES), 1)
    row8 = lax.broadcasted_iota(jnp.int32, (8, LANES), 0)
    basis_row = jnp.broadcast_to(packed[2:3, :], (8, LANES))
    camera_row = jnp.where((row8 < 2), packed, 0.0)
    at10 = pltpu.roll(basis_row, 10, 1)
    w_out[...] = camera_row + jnp.where(row8 == 0, at10, 0.0)
    weights = jnp.where(lane8 < 3, camera_row, 0.0)
    weights = weights + jnp.where(row8 == 2, at10, 0.0)
    weights = weights + jnp.where(row8 == 3, pltpu.roll(basis_row, 10 + coefs, 1), 0.0)
    weights = weights + jnp.where(row8 == 4, pltpu.roll(basis_row, 10 + 2 * coefs, 1), 0.0)
    w_scr[...] = weights
    linear = lax.dot_general(
        w_scr[:, 0 : params_ref.shape[0]],
        params_ref[...],
        (((1,), (0,)), ((), ())),
        precision=lax.Precision.HIGHEST,
        preferred_element_type=F32,
    )

    def cam(i, j):
        return cam_ref[0, i : i + 1, j : j + 1]

    def row(i):
        return params_ref[i : i + 1, :]

    lx, lyx, ly, lzx, lzy, lz = [row(i) for i in range(3, 9)]
    m = []
    for i in range(2):
        a0, a1, a2 = cam(i, 0), cam(i, 1), cam(i, 2)
        m.append((a0 * lx + a1 * lyx + a2 * lzx, a1 * ly + a2 * lzy, a2 * lz))
    upper = m[0][0] * m[0][0] + m[0][1] * m[0][1] + m[0][2] * m[0][2] + DILATION
    cross = m[0][0] * m[1][0] + m[0][1] * m[1][1] + m[0][2] * m[1][2]
    lower = m[1][0] * m[1][0] + m[1][1] * m[1][1] + m[1][2] * m[1][2] + DILATION
    inverse = 1.0 / (upper * lower - cross * cross)
    logit = row(9)
    log_opacity = jnp.minimum(logit, 0.0) * LOG2E - LOG2E * jnp.log(1.0 + jnp.exp(-jnp.abs(logit)))
    feat[0:1, :] = linear[0:1, :] + cam(0, 3)
    feat[1:2, :] = linear[1:2, :] + cam(1, 3)
    feat[2:3, :] = lower * inverse * (0.5 * LOG2E)
    feat[3:4, :] = -cross * inverse * LOG2E
    feat[4:5, :] = upper * inverse * (0.5 * LOG2E)
    feat[5:6, :] = log_opacity
    for c in range(3):
        feat[6 + c : 7 + c, :] = linear[2 + c : 3 + c, :] + 0.5

    total = nd * rows
    step = 8 if total % 8 == 0 else total
    source_rows = width // LANES
    for first in range(0, total, step):
        index = idx_out[first : first + step, :]
        low = index & (LANES - 1)
        high = index >> 7
        acc = [jnp.zeros((step, LANES), F32) for _ in range(FEATS)]
        for r in range(source_rows):
            here = high == r
            for f in range(FEATS):
                source = jnp.broadcast_to(feat[f : f + 1, r * LANES : (r + 1) * LANES], (step, LANES))
                acc[f] = jnp.where(here, lane_take(source, low), acc[f])
        for f in range(FEATS):
            for n in range(step):
                j, i = divmod(first + n, rows)
                if rows % step == 0:
                    if n == 0:
                        outs[j][f, i : i + step, :] = acc[f]
                else:
                    outs[j][f, i : i + 1, :] = acc[f][n : n + 1, :]


def vmem_spec():
    return pl.BlockSpec(memory_space=pltpu.VMEM)


def smem_spec():
    return pl.BlockSpec(memory_space=pltpu.SMEM)


def send(me, cameras, basis, params, requests, nd, cap, rows):
    return pl.pallas_call(
        partial(send_kernel, nd=nd, cap=cap, rows=rows),
        in_specs=[smem_spec()] + [vmem_spec()] * 4,
        out_specs=[vmem_spec()] * (nd + 2),
        out_shape=[jax.ShapeDtypeStruct((FEATS, rows, LANES), F32)] * nd
        + [
            jax.ShapeDtypeStruct((nd * rows, LANES), jnp.int32),
            jax.ShapeDtypeStruct((8, LANES), F32),
        ],
        scratch_shapes=[pltpu.VMEM((16, params.shape[1]), F32), pltpu.VMEM((8, LANES), F32)],
        compiler_params=pltpu.CompilerParams(vmem_limit_bytes=40 * 1024 * 1024),
        name="project_gather",
    )(me, cameras, basis, params, requests)


def scatter_products(value_rows, index_rows, spread, hot, out_rows):
    width = value_rows[0][0].shape[1]
    for n, (values, (high, low)) in enumerate(zip(value_rows, index_rows)):
        columns = slice(n * width, (n + 1) * width)
        high_iota = lax.broadcasted_iota(jnp.int32, (out_rows, width), 0)
        low_iota = lax.broadcasted_iota(jnp.int32, (LANES, width), 0)
        here = high_iota == high
        hot[:, columns] = jnp.where(low_iota == low, 1.0, 0.0).astype(BF16)
        for f in range(FEATS):
            hi, lo = split2(values[f])
            hi, lo = hi.astype(F32), lo.astype(F32)
            spread[f * out_rows : (f + 1) * out_rows, columns] = jnp.where(here, hi, 0.0).astype(BF16)
            base = (FEATS + f) * out_rows
            spread[base : base + out_rows, columns] = jnp.where(here, lo, 0.0).astype(BF16)


def render_kernel(me_ref, *refs, nd, cap, rows, tiles, entries):
    recv = refs[:nd]
    blocks_ref, orders_ref, counts_ref, ids_ref, target_ref = refs[nd : nd + 5]
    outs = refs[nd + 5 : 2 * nd + 5]
    (images_ref, coef, a_scr, t_scr, q_scr, whi_scr, wlo_scr, ghi_scr, glo_scr, g_rows, mom, spread, hot) = refs[
        2 * nd + 5 :
    ]
    me = me_ref[0]
    pixels = SIDE * SIDE
    chunk = entries // 8
    halves = entries // LANES
    table_rows = nd * rows

    place = lax.broadcasted_iota(jnp.int32, (tiles, entries), 1)
    rank = (place & 7) * chunk + (place >> 3)

    def take_wide(source, index):
        parts = []
        for c in range(halves):
            wanted = index[:, c * LANES : (c + 1) * LANES]
            low = wanted & (LANES - 1)
            high = wanted >> 7
            value = lane_take(source[:, 0:LANES], low)
            for h in range(1, halves):
                value = jnp.where(high == h, lane_take(source[:, h * LANES : (h + 1) * LANES], low), value)
            parts.append(value)
        return jnp.concatenate(parts, axis=1)

    def put(ref, at, value):
        for h in range(halves):
            ref[h, at : at + value.shape[0], :] = value[:, h * LANES : (h + 1) * LANES]

    def column(ref):
        square = jnp.broadcast_to(ref[0, 0].astype(F32), (tiles, tiles))
        diagonal = lax.broadcasted_iota(jnp.int32, (tiles, tiles), 0) == lax.broadcasted_iota(
            jnp.int32, (tiles, tiles), 1
        )
        return jnp.sum(jnp.where(diagonal, square, 0.0), axis=1, keepdims=True).astype(jnp.int32)

    order = take_wide(orders_ref[0, 0, 0], rank)
    slot = take_wide(blocks_ref[0, 0, 0], order)
    shard = jnp.zeros_like(slot)
    for i in range(1, nd):
        shard = shard + (slot >= i * cap).astype(jnp.int32)
    offset = slot - shard * cap
    hop = me - shard
    hop = jnp.where(hop < 0, hop + nd, hop)
    slot_row = hop * rows + (offset >> 7)
    slot_lane = offset & (LANES - 1)
    live = rank < column(counts_ref)
    tile_id = column(ids_ref)
    centre_x = ((tile_id % TW) * SIDE).astype(F32) + 0.5 * SIDE
    centre_y = ((tile_id // TW) * SIDE).astype(F32) + 0.5 * SIDE

    pieces = [[None] * halves for _ in range(FEATS)]
    for c in range(halves):
        low = slot_lane[:, c * LANES : (c + 1) * LANES]
        high = slot_row[:, c * LANES : (c + 1) * LANES]
        acc = [jnp.zeros((tiles, LANES), F32) for _ in range(FEATS)]
        for n in range(table_rows):
            here = high == n
            for f in range(FEATS):
                source = jnp.broadcast_to(recv[n // rows][f, n % rows : n % rows + 1, :], (tiles, LANES))
                acc[f] = jnp.where(here, lane_take(source, low), acc[f])
        for f in range(FEATS):
            pieces[f][c] = acc[f]
    mean_x, mean_y, con_a, con_b, con_c, log_op, red, green, blue = [jnp.concatenate(p, axis=1) for p in pieces]
    mean_x = mean_x - centre_x
    mean_y = mean_y - centre_y
    bx = con_a * mean_x
    by = con_c * mean_y
    constant = log_op - (bx * mean_x + con_b * mean_x * mean_y + by * mean_y)
    constant = jnp.where(live, constant, DEAD)
    poly = [constant, 2.0 * bx + con_b * mean_y, 2.0 * by + con_b * mean_x, -con_a, -con_b, -con_c]
    for i, value in enumerate(poly):
        rest = value
        for part in range(3):
            piece = rest.astype(BF16).astype(F32)
            rest = rest - piece
            at = (6 * part + i) * tiles
            put(coef, at, piece)
    for i, value in enumerate((red, green, blue)):
        first = value.astype(BF16).astype(F32)
        second = (value - first).astype(BF16).astype(F32)
        for block, piece in enumerate((first, first, second, second)):
            at = (18 + 3 * block + i) * tiles
            put(coef, at, piece)
    coef[:, 30 * tiles : 32 * tiles, :] = jnp.zeros((halves, 2 * tiles, LANES), F32)

    pixel = lax.broadcasted_iota(jnp.int32, (1, pixels), 1)
    px = (pixel & (SIDE - 1)).astype(F32) + (0.5 - 0.5 * SIDE)
    py = (pixel >> 4).astype(F32) + (0.5 - 0.5 * SIDE)
    one = jnp.ones((1, pixels), F32)
    monomials = [one, px, py, px * px, px * py, py * py]
    zero = jnp.zeros((1, pixels), F32)
    basis_scr = g_rows
    for part in range(3):
        for i in range(6):
            basis_scr[6 * part + i : 6 * part + i + 1, :] = monomials[i]
    basis_scr[18:32, :] = jnp.zeros((14, pixels), F32)
    basis = basis_scr[...].astype(BF16)
    moment_basis = jnp.concatenate(monomials + [zero, zero], axis=0).astype(BF16)
    g_rows[0:18, :] = jnp.zeros((18, pixels), F32)

    sub_e = lax.broadcasted_iota(jnp.int32, (8, entries), 0)
    own_chunk = jnp.where(sub_e == (lax.broadcasted_iota(jnp.int32, (8, entries), 1) & 7), 1.0, 0.0)
    sub_p = lax.broadcasted_iota(jnp.int32, (8, pixels), 0)

    def down(x, by, fill):
        return jnp.where(sub_p >= by, pltpu.roll(x, by, 0), fill)

    def up(x, by, fill):
        return jnp.where(sub_p < 8 - by, pltpu.roll(x, 8 - by, 0), fill)

    def tile(t, carry):
        table = [coef[h, pl.ds(t, 32, stride=tiles), :] for h in range(halves)]
        table = jnp.concatenate(table, axis=1)
        lhs = table.T.astype(BF16)
        a_scr[...] = jnp.exp2(jnp.minimum(dot(lhs, basis, 1, 0), 0.0))
        trans = jnp.ones((8, pixels), F32)
        for jj in range(entries // 16):
            w = []
            for h in range(2):
                at = slice(16 * jj + 8 * h, 16 * jj + 8 * h + 8)
                t_scr[at, :] = trans
                value = trans * a_scr[at, :]
                trans = trans - value
                w.append(value)
            at = slice(16 * jj, 16 * jj + 16)
            whi_scr[at, :], wlo_scr[at, :] = split2(jnp.concatenate(w, axis=0))
        colour = [own_chunk * table[18 + i : 19 + i, :] for i in range(3)]
        colour = colour + [own_chunk * table[24 + i : 25 + i, :] for i in range(3)]
        colour = jnp.concatenate(colour, axis=0).astype(BF16)
        local = dot(colour, whi_scr[...], 1, 0) + dot(colour, wlo_scr[...], 1, 0)
        local = [local[8 * i : 8 * i + 8, :] + local[24 + 8 * i : 32 + 8 * i, :] for i in range(3)]
        before = down(trans, 1, 1.0)
        for by in (1, 2, 4):
            before = before * down(before, by, 1.0)
        tinted = []
        inner = jnp.zeros((8, pixels), F32)
        for i in range(3):
            image = jnp.sum(before * local[i], axis=0, keepdims=True)
            images_ref[0, 0, 0, t, i : i + 1, :] = image
            residual = image - target_ref[0, 0, 0, t, i : i + 1, :]
            first = residual.astype(BF16).astype(F32)
            second = (residual - first).astype(BF16).astype(F32)
            g_rows[18 + i : 19 + i, :] = first
            g_rows[21 + i : 22 + i, :] = second
            g_rows[24 + i : 25 + i, :] = first
            g_rows[27 + i : 28 + i, :] = second
            tinted.append(before * residual)
            inner = inner + residual * local[i]
        q_scr[...] = dot(lhs, g_rows[...].astype(BF16), 1, 0)
        tinted_hi, tinted_lo = split2(jnp.concatenate(tinted, axis=0))
        tinted = jnp.concatenate([tinted_hi.astype(F32), tinted_lo.astype(F32)], axis=0).astype(BF16)
        colour_grad = dot(tinted, whi_scr[...], 1, 1) + dot(tinted, wlo_scr[...], 1, 1)
        rows_out = []
        for i in range(3):
            both = colour_grad[8 * i : 8 * i + 8, :] + colour_grad[24 + 8 * i : 32 + 8 * i, :]
            rows_out.append(jnp.sum(own_chunk * both, axis=0, keepdims=True))
        add = up(inner, 1, 0.0)
        scale = up(trans, 1, 0.0)
        for by in (1, 2, 4):
            add = add + scale * up(add, by, 0.0)
            scale = scale * up(scale, by, 0.0)
        behind = add
        for jj in reversed(range(entries // 16)):
            g = [None, None]
            for h in (1, 0):
                at = slice(16 * jj + 8 * h, 16 * jj + 8 * h + 8)
                moved = a_scr[at, :] * (q_scr[at, :] - behind)
                behind = behind + moved
                g[h] = (t_scr[at, :] * before) * moved
            at = slice(16 * jj, 16 * jj + 16)
            ghi_scr[at, :], glo_scr[at, :] = split2(jnp.concatenate(g, axis=0))
        moments = dot(moment_basis, ghi_scr[...], 1, 1) + dot(moment_basis, glo_scr[...], 1, 1)
        for h in range(halves):
            columns = slice(h * LANES, (h + 1) * LANES)
            mom[h, pl.ds(t, 8, stride=tiles), :] = moments[:, columns]
            for i in range(3):
                mom[h, pl.ds((8 + i) * tiles + t, 1), :] = rows_out[i][:, columns]
        return carry

    lax.fori_loop(0, tiles, tile, 0)

    def got(i):
        return jnp.concatenate([mom[h, i * tiles : (i + 1) * tiles, :] for h in range(halves)], axis=1)

    m0, m1, m2, m3, m4, m5 = [got(i) for i in range(6)]
    su = m1 - mean_x * m0
    sv = m2 - mean_y * m0
    suu = m3 - mean_x * (m1 + su)
    suv = m4 - mean_x * m2 - mean_y * su
    svv = m5 - mean_y * (m2 + sv)
    grads = [
        LN2 * (2.0 * con_a * su + con_b * sv),
        LN2 * (con_b * su + 2.0 * con_c * sv),
        -0.5 * suu,
        -suv,
        -0.5 * svv,
        m0,
    ] + [got(8 + i) for i in range(3)]
    value_rows = [[g[t : t + 1, :] for g in grads] for t in range(tiles)]
    index_rows = [(slot_row[t : t + 1, :], slot_lane[t : t + 1, :]) for t in range(tiles)]
    scatter_products(value_rows, index_rows, spread, hot, table_rows)
    summed = dot(spread[...], hot[...], 1, 1)
    for f in range(FEATS):
        both = (
            summed[f * table_rows : (f + 1) * table_rows, :]
            + summed[(FEATS + f) * table_rows : (FEATS + f + 1) * table_rows, :]
        )
        for j in range(nd):
            outs[j][f] = both[j * rows : (j + 1) * rows, :]


def render(me, received, blocks, orders, counts, ids, target, nd, cap, rows):
    tiles, entries = blocks.shape[3:]
    pixels = SIDE * SIDE
    return pl.pallas_call(
        partial(render_kernel, nd=nd, cap=cap, rows=rows, tiles=tiles, entries=entries),
        in_specs=[smem_spec()] + [vmem_spec()] * (nd + 5),
        out_specs=[vmem_spec()] * (nd + 1),
        out_shape=[jax.ShapeDtypeStruct((FEATS, rows, LANES), F32)] * nd
        + [jax.ShapeDtypeStruct(target.shape, F32)],
        scratch_shapes=[
            pltpu.VMEM((entries // LANES, 32 * tiles, LANES), F32),
            pltpu.VMEM((entries, pixels), F32),
            pltpu.VMEM((entries, pixels), F32),
            pltpu.VMEM((entries, pixels), F32),
            pltpu.VMEM((entries, pixels), BF16),
            pltpu.VMEM((entries, pixels), BF16),
            pltpu.VMEM((entries, pixels), BF16),
            pltpu.VMEM((entries, pixels), BF16),
            pltpu.VMEM((32, pixels), F32),
            pltpu.VMEM((entries // LANES, 11 * tiles, LANES), F32),
            pltpu.VMEM((2 * FEATS * nd * rows, tiles * entries), BF16),
            pltpu.VMEM((LANES, tiles * entries), BF16),
        ],
        compiler_params=pltpu.CompilerParams(vmem_limit_bytes=48 * 1024 * 1024),
        name="render_tiles",
    )(me, *received, blocks, orders, counts, ids, target)


def owner_kernel(me_ref, *refs, nd, rows, parts, nv, nc, out_rows):
    recv = refs[:nd]
    idx_ref, w_ref = refs[nd : nd + 2]
    outs = refs[nd + 2 : nd + 2 + parts]
    spread, hot, summed = refs[nd + 2 + parts :]
    my_view = me_ref[1]
    my_chip = me_ref[2]
    value_rows = []
    index_rows = []
    for n in range(nd * rows):
        value_rows.append([recv[n // rows][f, n % rows : n % rows + 1, :] for f in range(FEATS)])
        index = idx_ref[n : n + 1, :]
        index_rows.append((index >> 7, index & (LANES - 1)))
    scatter_products(value_rows, index_rows, spread, hot, out_rows)
    result = dot(spread[...], hot[...], 1, 1)
    share = out_rows // parts
    for f in range(FEATS):
        both = (
            result[f * out_rows : (f + 1) * out_rows, :]
            + result[(FEATS + f) * out_rows : (FEATS + f + 1) * out_rows, :]
        )
        for p in range(parts):
            summed[p, f] = both[p * share : (p + 1) * share, :]
    for p in range(parts):
        summed[p, FEATS] = w_ref[0:share, :]
    for dv in range(nv):
        for dc in range(nc):
            where = lax.rem(my_view + dv, nv) * nc + lax.rem(my_chip + dc, nc)
            outs[dv * nc + dc][...] = summed[where]


def owner_sums(me, received, index, weights, nd, rows, nv, nc, width):
    parts = nv * nc
    out_rows = width // LANES
    share = out_rows // parts
    return pl.pallas_call(
        partial(owner_kernel, nd=nd, rows=rows, parts=parts, nv=nv, nc=nc, out_rows=out_rows),
        in_specs=[smem_spec()] + [vmem_spec()] * (nd + 2),
        out_specs=[vmem_spec()] * parts,
        out_shape=[jax.ShapeDtypeStruct((FEATS + 1, share, LANES), F32)] * parts,
        scratch_shapes=[
            pltpu.VMEM((2 * FEATS * out_rows, nd * rows * LANES), BF16),
            pltpu.VMEM((LANES, nd * rows * LANES), BF16),
            pltpu.VMEM((parts, FEATS + 1, share, LANES), F32),
        ],
        compiler_params=pltpu.CompilerParams(vmem_limit_bytes=48 * 1024 * 1024),
        name="owner_sums",
    )(me, *received, index, weights)


def pullback_kernel(at_ref, params_ref, *refs, nv, nc, coefs):
    recv = refs[: nv * nc]
    out_ref, flat = refs[nv * nc :]
    share = recv[0].shape[1]
    columns = share * LANES

    def row(i):
        return params_ref[i : i + 1, :]

    lx, lyx, ly, lzx, lzy, lz = [row(i) for i in range(3, 9)]
    total = [jnp.zeros((1, columns), F32) for _ in range(10)]
    harmonics = [jnp.zeros((coefs, columns), F32) for _ in range(3)]
    square = lax.broadcasted_iota(jnp.int32, (coefs, LANES), 1) == lax.broadcasted_iota(
        jnp.int32, (coefs, LANES), 0
    ) + 10
    for v in range(nv):
        packed = recv[v * nc][FEATS]
        for i in range(share):
            block = recv[v * nc][0:FEATS, i, :]
            for c in range(1, nc):
                block = block + recv[v * nc + c][0:FEATS, i, :]
            flat[0:FEATS, i * LANES : (i + 1) * LANES] = block
        gx, gy, g0, g1, g2, gh, gr, gg, gb = [flat[f : f + 1, :] for f in range(FEATS)]
        cam = [[packed[i : i + 1, j : j + 1] for j in range(3)] for i in range(2)]
        for j in range(3):
            total[j] = total[j] + cam[0][j] * gx + cam[1][j] * gy
        m = []
        for i in range(2):
            a0, a1, a2 = cam[i]
            m.append((a0 * lx + a1 * lyx + a2 * lzx, a1 * ly + a2 * lzy, a2 * lz))
        upper = m[0][0] * m[0][0] + m[0][1] * m[0][1] + m[0][2] * m[0][2] + DILATION
        cross = m[0][0] * m[1][0] + m[0][1] * m[1][1] + m[0][2] * m[1][2]
        lower = m[1][0] * m[1][0] + m[1][1] * m[1][1] + m[1][2] * m[1][2] + DILATION
        inverse = 1.0 / (upper * lower - cross * cross)
        c0, c1, c2 = lower * inverse, -cross * inverse, upper * inverse
        h1 = 0.5 * g1
        k00, k01 = g0 * c0 + h1 * c1, g0 * c1 + h1 * c2
        k10, k11 = h1 * c0 + g2 * c1, h1 * c1 + g2 * c2
        s00 = -(c0 * k00 + c1 * k10)
        s01 = -(c0 * k01 + c1 * k11)
        s11 = -(c1 * k01 + c2 * k11)
        gm = [[2.0 * (s00 * m[0][k] + s01 * m[1][k]) for k in range(3)]]
        gm.append([2.0 * (s01 * m[0][k] + s11 * m[1][k]) for k in range(3)])
        at = 3
        for i in range(3):
            for k in range(i + 1):
                total[at] = total[at] + cam[0][i] * gm[0][k] + cam[1][i] * gm[1][k]
                at += 1
        total[9] = total[9] + gh
        basis = jnp.sum(jnp.where(square, packed[0:1, :], 0.0), axis=1, keepdims=True)
        for c, g in enumerate((gr, gg, gb)):
            harmonics[c] = harmonics[c] + basis * g
    logit = row(9)
    total[9] = total[9] / (1.0 + jnp.exp(logit))
    for i in range(10):
        out_ref[i : i + 1, :] = total[i]
    for c in range(3):
        out_ref[10 + c * coefs : 10 + (c + 1) * coefs, :] = harmonics[c]


def pull_back(at, params, received, nv, nc, coefs):
    parts = nv * nc
    columns = params.shape[1] // parts
    block = received[0].shape
    return pl.pallas_call(
        partial(pullback_kernel, nv=nv, nc=nc, coefs=coefs),
        grid_spec=pltpu.PrefetchScalarGridSpec(
            num_scalar_prefetch=1,
            grid=(1,),
            in_specs=[pl.BlockSpec((params.shape[0], columns), lambda i, at_ref: (0, at_ref[0]))]
            + [pl.BlockSpec(block, lambda i, at_ref: (0, 0, 0))] * parts,
            out_specs=pl.BlockSpec((params.shape[0], columns), lambda i, at_ref: (0, 0)),
            scratch_shapes=[pltpu.VMEM((16, columns), F32)],
        ),
        out_shape=jax.ShapeDtypeStruct((params.shape[0], columns), F32),
        compiler_params=pltpu.CompilerParams(vmem_limit_bytes=40 * 1024 * 1024),
        name="pull_back",
    )(at, params, *received)


def local(
    params,
    cameras,
    view_basis,
    tile_lists,
    margin_blocks,
    depth_orders,
    tile_counts,
    requests,
    target,
    *,
    nd,
    nv,
    nc,
):
    cap = requests.shape[4]
    rows = -(-cap // LANES)
    my_view = lax.axis_index("view")
    my_chip = lax.axis_index("chip")
    me = jnp.stack([lax.axis_index("dev"), my_view, my_chip]).astype(jnp.int32)
    at = (my_view * nc + my_chip).astype(jnp.int32).reshape(1)

    *packets, index, weights = send(me, cameras, view_basis, params, requests, nd, cap, rows)
    received = [packets[0]]
    for j in range(1, nd):
        received.append(lax.ppermute(packets[j], "dev", [(i, (i + j) % nd) for i in range(nd)]))
    *returns, images = render(
        me, received, margin_blocks, depth_orders, tile_counts, tile_lists, target, nd, cap, rows
    )
    back = [returns[0]]
    for j in range(1, nd):
        back.append(lax.ppermute(returns[j], "dev", [((i + j) % nd, i) for i in range(nd)]))
    shares = owner_sums(me, back, index, weights, nd, rows, nv, nc, params.shape[1])
    arrived = []
    for dv in range(nv):
        for dc in range(nc):
            pairs = [
                (v * nc + c, (v + dv) % nv * nc + (c + dc) % nc) for v in range(nv) for c in range(nc)
            ]
            piece = shares[dv * nc + dc]
            arrived.append(piece if dv + dc == 0 else lax.ppermute(piece, ("view", "chip"), pairs))
    grads = pull_back(at, params, arrived, nv, nc, view_basis.shape[1])
    return (grads, images)


def solution(mesh):
    return jax.shard_map(
        partial(local, nd=mesh.shape["dev"], nv=mesh.shape["view"], nc=mesh.shape["chip"]),
        mesh=mesh,
        in_specs=(
            P(None, ("groups", "dev")),
            P(("groups", "view"), None, None),
            P(("groups", "view"), None),
            P("view", ("groups", "dev"), "chip", None),
            P("view", ("groups", "dev"), "chip", None, None),
            P("view", ("groups", "dev"), "chip", None, None),
            P("view", ("groups", "dev"), "chip", None),
            P("view", None, "chip", ("groups", "dev"), None),
            P("view", ("groups", "dev"), "chip", None, None, None),
        ),
        out_specs=(
            P(None, ("groups", "dev", "view", "chip")),
            P("view", ("groups", "dev"), "chip", None, None, None),
        ),
        check_vma=False,
    )
```

```python
from functools import partial

import jax
import jax.numpy as jnp
from jax import lax
from jax.experimental import pallas as pl
from jax.experimental.pallas import tpu as pltpu
from jax.sharding import PartitionSpec as P

SIDE = 16
TW = 16
LANES = 128
LOG2E = 1.4426950408889634
LN2 = 0.6931471805599453
DILATION = 0.3
DEAD = -1e30
F32 = jnp.float32
BF16 = jnp.bfloat16
FEATS = 9
GROUP = 16


def lane_take(row, index):
    return jnp.take_along_axis(row, index, axis=1, mode="promise_in_bounds")


def split2(x):
    hi = x.astype(BF16)
    return hi, (x - hi.astype(F32)).astype(BF16)


def dot(a, b, ca, cb):
    return lax.dot_general(a, b, (((ca,), (cb,)), ((), ())), preferred_element_type=F32)


def send_kernel(me_ref, cam_ref, basis_ref, params_ref, req_ref, *refs, nd, cap, rows):
    outs = refs[:nd]
    idx_out, w_out, feat, w_scr = refs[nd:]
    me = me_ref[0]
    width = params_ref.shape[1]
    coefs = basis_ref.shape[-1]
    idx_out[...] = jnp.zeros_like(idx_out)
    for j in range(nd):
        dest = lax.rem(me + j, nd)
        for i in range(rows):
            size = min(LANES, cap - i * LANES)
            idx_out[j * rows + i : j * rows + i + 1, 0:size] = req_ref[
                0, dest, 0, 0:1, i * LANES : i * LANES + size
            ]
    w_scr[...] = jnp.zeros_like(w_scr)
    w_scr[0:2, 0:4] = cam_ref[0]
    w_scr[2:3, 0:coefs] = basis_ref[...]
    packed = w_scr[...]
    lane8 = lax.broadcasted_iota(jnp.int32, (8, LANES), 1)
    row8 = lax.broadcasted_iota(jnp.int32, (8, LANES), 0)
    basis_row = jnp.broadcast_to(packed[2:3, :], (8, LANES))
    camera_row = jnp.where((row8 < 2), packed, 0.0)
    at10 = pltpu.roll(basis_row, 10, 1)
    w_out[...] = camera_row + jnp.where(row8 == 0, at10, 0.0)
    weights = jnp.where(lane8 < 3, camera_row, 0.0)
    weights = weights + jnp.where(row8 == 2, at10, 0.0)
    weights = weights + jnp.where(row8 == 3, pltpu.roll(basis_row, 10 + coefs, 1), 0.0)
    weights = weights + jnp.where(row8 == 4, pltpu.roll(basis_row, 10 + 2 * coefs, 1), 0.0)
    w_scr[...] = weights
    linear = lax.dot_general(
        w_scr[:, 0 : params_ref.shape[0]],
        params_ref[...],
        (((1,), (0,)), ((), ())),
        precision=lax.Precision.HIGHEST,
        preferred_element_type=F32,
    )

    def cam(i, j):
        return cam_ref[0, i : i + 1, j : j + 1]

    def row(i):
        return params_ref[i : i + 1, :]

    lx, lyx, ly, lzx, lzy, lz = [row(i) for i in range(3, 9)]
    m = []
    for i in range(2):
        a0, a1, a2 = cam(i, 0), cam(i, 1), cam(i, 2)
        m.append((a0 * lx + a1 * lyx + a2 * lzx, a1 * ly + a2 * lzy, a2 * lz))
    upper = m[0][0] * m[0][0] + m[0][1] * m[0][1] + m[0][2] * m[0][2] + DILATION
    cross = m[0][0] * m[1][0] + m[0][1] * m[1][1] + m[0][2] * m[1][2]
    lower = m[1][0] * m[1][0] + m[1][1] * m[1][1] + m[1][2] * m[1][2] + DILATION
    inverse = 1.0 / (upper * lower - cross * cross)
    logit = row(9)
    log_opacity = jnp.minimum(logit, 0.0) * LOG2E - LOG2E * jnp.log(1.0 + jnp.exp(-jnp.abs(logit)))
    feat[0:1, :] = linear[0:1, :] + cam(0, 3)
    feat[1:2, :] = linear[1:2, :] + cam(1, 3)
    feat[2:3, :] = lower * inverse * (0.5 * LOG2E)
    feat[3:4, :] = -cross * inverse * LOG2E
    feat[4:5, :] = upper * inverse * (0.5 * LOG2E)
    feat[5:6, :] = log_opacity
    for c in range(3):
        feat[6 + c : 7 + c, :] = linear[2 + c : 3 + c, :] + 0.5

    total = nd * rows
    step = 8 if total % 8 == 0 else total
    source_rows = width // LANES
    for first in range(0, total, step):
        index = idx_out[first : first + step, :]
        low = index & (LANES - 1)
        high = index >> 7
        acc = [jnp.zeros((step, LANES), F32) for _ in range(FEATS)]
        for r in range(source_rows):
            here = high == r
            for f in range(FEATS):
                source = jnp.broadcast_to(feat[f : f + 1, r * LANES : (r + 1) * LANES], (step, LANES))
                acc[f] = jnp.where(here, lane_take(source, low), acc[f])
        for f in range(FEATS):
            for n in range(step):
                j, i = divmod(first + n, rows)
                if rows % step == 0:
                    if n == 0:
                        outs[j][f, i : i + step, :] = acc[f]
                else:
                    outs[j][f, i : i + 1, :] = acc[f][n : n + 1, :]


def vmem_spec():
    return pl.BlockSpec(memory_space=pltpu.VMEM)


def smem_spec():
    return pl.BlockSpec(memory_space=pltpu.SMEM)


def send(me, cameras, basis, params, requests, nd, cap, rows):
    return pl.pallas_call(
        partial(send_kernel, nd=nd, cap=cap, rows=rows),
        in_specs=[smem_spec()] + [vmem_spec()] * 4,
        out_specs=[vmem_spec()] * (nd + 2),
        out_shape=[jax.ShapeDtypeStruct((FEATS, rows, LANES), F32)] * nd
        + [
            jax.ShapeDtypeStruct((nd * rows, LANES), jnp.int32),
            jax.ShapeDtypeStruct((8, LANES), F32),
        ],
        scratch_shapes=[pltpu.VMEM((16, params.shape[1]), F32), pltpu.VMEM((8, LANES), F32)],
        compiler_params=pltpu.CompilerParams(vmem_limit_bytes=40 * 1024 * 1024),
        name="project_gather",
    )(me, cameras, basis, params, requests)


def scatter_products(value_rows, index_rows, spread, hot, out_rows):
    width = value_rows[0][0].shape[1]
    for n, (values, (high, low)) in enumerate(zip(value_rows, index_rows)):
        columns = slice(n * width, (n + 1) * width)
        high_iota = lax.broadcasted_iota(jnp.int32, (out_rows, width), 0)
        low_iota = lax.broadcasted_iota(jnp.int32, (LANES, width), 0)
        here = high_iota == high
        hot[:, columns] = jnp.where(low_iota == low, 1.0, 0.0).astype(BF16)
        for f in range(FEATS):
            hi, lo = split2(values[f])
            hi, lo = hi.astype(F32), lo.astype(F32)
            spread[f * out_rows : (f + 1) * out_rows, columns] = jnp.where(here, hi, 0.0).astype(BF16)
            base = (FEATS + f) * out_rows
            spread[base : base + out_rows, columns] = jnp.where(here, lo, 0.0).astype(BF16)


def render_kernel(me_ref, *refs, nd, cap, rows, tiles, entries):
    recv = refs[:nd]
    blocks_ref, orders_ref, counts_ref, ids_ref, target_ref = refs[nd : nd + 5]
    outs = refs[nd + 5 : 2 * nd + 5]
    (images_ref, coef, a_scr, t_scr, q_scr, whi_scr, wlo_scr, ghi_scr, glo_scr, g_rows, mom, spread, hot) = refs[
        2 * nd + 5 :
    ]
    me = me_ref[0]
    pixels = SIDE * SIDE
    chunk = entries // 8
    halves = entries // LANES
    table_rows = nd * rows

    place = lax.broadcasted_iota(jnp.int32, (tiles, entries), 1)
    rank = (place & 7) * chunk + (place >> 3)

    def take_wide(source, index):
        parts = []
        for c in range(halves):
            wanted = index[:, c * LANES : (c + 1) * LANES]
            low = wanted & (LANES - 1)
            high = wanted >> 7
            value = lane_take(source[:, 0:LANES], low)
            for h in range(1, halves):
                value = jnp.where(high == h, lane_take(source[:, h * LANES : (h + 1) * LANES], low), value)
            parts.append(value)
        return jnp.concatenate(parts, axis=1)

    def put(ref, at, value):
        for h in range(halves):
            ref[h, at : at + value.shape[0], :] = value[:, h * LANES : (h + 1) * LANES]

    def column(ref):
        square = jnp.broadcast_to(ref[0, 0].astype(F32), (tiles, tiles))
        diagonal = lax.broadcasted_iota(jnp.int32, (tiles, tiles), 0) == lax.broadcasted_iota(
            jnp.int32, (tiles, tiles), 1
        )
        return jnp.sum(jnp.where(diagonal, square, 0.0), axis=1, keepdims=True).astype(jnp.int32)

    order = take_wide(orders_ref[0, 0, 0], rank)
    slot = take_wide(blocks_ref[0, 0, 0], order)
    shard = jnp.zeros_like(slot)
    for i in range(1, nd):
        shard = shard + (slot >= i * cap).astype(jnp.int32)
    offset = slot - shard * cap
    hop = me - shard
    hop = jnp.where(hop < 0, hop + nd, hop)
    slot_row = hop * rows + (offset >> 7)
    slot_lane = offset & (LANES - 1)
    live = rank < column(counts_ref)
    tile_id = column(ids_ref)
    centre_x = ((tile_id % TW) * SIDE).astype(F32) + 0.5 * SIDE
    centre_y = ((tile_id // TW) * SIDE).astype(F32) + 0.5 * SIDE

    pieces = [[None] * halves for _ in range(FEATS)]
    for c in range(halves):
        low = slot_lane[:, c * LANES : (c + 1) * LANES]
        high = slot_row[:, c * LANES : (c + 1) * LANES]
        acc = [jnp.zeros((tiles, LANES), F32) for _ in range(FEATS)]
        for n in range(table_rows):
            here = high == n
            for f in range(FEATS):
                source = jnp.broadcast_to(recv[n // rows][f, n % rows : n % rows + 1, :], (tiles, LANES))
                acc[f] = jnp.where(here, lane_take(source, low), acc[f])
        for f in range(FEATS):
            pieces[f][c] = acc[f]
    mean_x, mean_y, con_a, con_b, con_c, log_op, red, green, blue = [jnp.concatenate(p, axis=1) for p in pieces]
    mean_x = mean_x - centre_x
    mean_y = mean_y - centre_y
    bx = con_a * mean_x
    by = con_c * mean_y
    constant = log_op - (bx * mean_x + con_b * mean_x * mean_y + by * mean_y)
    constant = jnp.where(live, constant, DEAD)
    poly = [constant, 2.0 * bx + con_b * mean_y, 2.0 * by + con_b * mean_x, -con_a, -con_b, -con_c]
    for i, value in enumerate(poly):
        rest = value
        for part in range(3):
            piece = rest.astype(BF16).astype(F32)
            rest = rest - piece
            at = (6 * part + i) * tiles
            put(coef, at, piece)
    for i, value in enumerate((red, green, blue)):
        first = value.astype(BF16).astype(F32)
        second = (value - first).astype(BF16).astype(F32)
        for block, piece in enumerate((first, first, second, second)):
            at = (18 + 3 * block + i) * tiles
            put(coef, at, piece)
    coef[:, 30 * tiles : 32 * tiles, :] = jnp.zeros((halves, 2 * tiles, LANES), F32)

    pixel = lax.broadcasted_iota(jnp.int32, (1, pixels), 1)
    px = (pixel & (SIDE - 1)).astype(F32) + (0.5 - 0.5 * SIDE)
    py = (pixel >> 4).astype(F32) + (0.5 - 0.5 * SIDE)
    one = jnp.ones((1, pixels), F32)
    monomials = [one, px, py, px * px, px * py, py * py]
    zero = jnp.zeros((1, pixels), F32)
    basis_scr = g_rows.at[0]
    for part in range(3):
        for i in range(6):
            basis_scr[6 * part + i : 6 * part + i + 1, :] = monomials[i]
    basis_scr[18:32, :] = jnp.zeros((14, pixels), F32)
    basis = basis_scr[...].astype(BF16)
    moment_basis = jnp.concatenate(monomials + [zero, zero], axis=0).astype(BF16)
    g_rows[...] = jnp.zeros_like(g_rows)

    sub_e = lax.broadcasted_iota(jnp.int32, (8, entries), 0)
    own_chunk = jnp.where(sub_e == (lax.broadcasted_iota(jnp.int32, (8, entries), 1) & 7), 1.0, 0.0)
    sub_p = lax.broadcasted_iota(jnp.int32, (8, pixels), 0)

    def down(x, by, fill):
        return jnp.where(sub_p >= by, pltpu.roll(x, by, 0), fill)

    def up(x, by, fill):
        return jnp.where(sub_p < 8 - by, pltpu.roll(x, 8 - by, 0), fill)

    def group(step, carry):
        lanes = range(GROUP)
        ts = [step * GROUP + u for u in lanes]
        tables, lhs = [], []
        for u in lanes:
            table = [coef[h, pl.ds(ts[u], 32, stride=tiles), :] for h in range(halves)]
            tables.append(jnp.concatenate(table, axis=1))
            lhs.append(tables[u].T.astype(BF16))
            a_scr[u] = jnp.exp2(jnp.minimum(dot(lhs[u], basis, 1, 0), 0.0))
        trans = [jnp.ones((8, pixels), F32) for _ in lanes]
        for jj in range(entries // 16):
            for u in lanes:
                w = []
                for h in range(2):
                    at = slice(16 * jj + 8 * h, 16 * jj + 8 * h + 8)
                    t_scr[u, at, :] = trans[u]
                    value = trans[u] * a_scr[u, at, :]
                    trans[u] = trans[u] - value
                    w.append(value)
                at = slice(16 * jj, 16 * jj + 16)
                whi_scr[u, at, :], wlo_scr[u, at, :] = split2(jnp.concatenate(w, axis=0))
        befores, tints, behinds = [], [], []
        for u in lanes:
            table, t = tables[u], ts[u]
            colour = [own_chunk * table[18 + i : 19 + i, :] for i in range(3)]
            colour = colour + [own_chunk * table[24 + i : 25 + i, :] for i in range(3)]
            colour = jnp.concatenate(colour, axis=0).astype(BF16)
            local = dot(colour, whi_scr[u], 1, 0) + dot(colour, wlo_scr[u], 1, 0)
            local = [local[8 * i : 8 * i + 8, :] + local[24 + 8 * i : 32 + 8 * i, :] for i in range(3)]
            before = down(trans[u], 1, 1.0)
            for by in (1, 2, 4):
                before = before * down(before, by, 1.0)
            tinted = []
            inner = jnp.zeros((8, pixels), F32)
            for i in range(3):
                image = jnp.sum(before * local[i], axis=0, keepdims=True)
                images_ref[0, 0, 0, t, i : i + 1, :] = image
                residual = image - target_ref[0, 0, 0, t, i : i + 1, :]
                first = residual.astype(BF16).astype(F32)
                second = (residual - first).astype(BF16).astype(F32)
                g_rows[u, 18 + i : 19 + i, :] = first
                g_rows[u, 21 + i : 22 + i, :] = second
                g_rows[u, 24 + i : 25 + i, :] = first
                g_rows[u, 27 + i : 28 + i, :] = second
                tinted.append(before * residual)
                inner = inner + residual * local[i]
            q_scr[u] = dot(lhs[u], g_rows[u].astype(BF16), 1, 0)
            tinted_hi, tinted_lo = split2(jnp.concatenate(tinted, axis=0))
            tints.append(jnp.concatenate([tinted_hi.astype(F32), tinted_lo.astype(F32)], axis=0).astype(BF16))
            add = up(inner, 1, 0.0)
            scale = up(trans[u], 1, 0.0)
            for by in (1, 2, 4):
                add = add + scale * up(add, by, 0.0)
                scale = scale * up(scale, by, 0.0)
            behinds.append(add)
            befores.append(before)
        rows_out = []
        for u in lanes:
            colour_grad = dot(tints[u], whi_scr[u], 1, 1) + dot(tints[u], wlo_scr[u], 1, 1)
            for i in range(3):
                both = colour_grad[8 * i : 8 * i + 8, :] + colour_grad[24 + 8 * i : 32 + 8 * i, :]
                rows_out.append(jnp.sum(own_chunk * both, axis=0, keepdims=True))
        for jj in reversed(range(entries // 16)):
            for u in lanes:
                g = [None, None]
                for h in (1, 0):
                    at = slice(16 * jj + 8 * h, 16 * jj + 8 * h + 8)
                    moved = a_scr[u, at, :] * (q_scr[u, at, :] - behinds[u])
                    behinds[u] = behinds[u] + moved
                    g[h] = (t_scr[u, at, :] * befores[u]) * moved
                at = slice(16 * jj, 16 * jj + 16)
                ghi_scr[u, at, :], glo_scr[u, at, :] = split2(jnp.concatenate(g, axis=0))
        for u in lanes:
            moments = dot(moment_basis, ghi_scr[u], 1, 1) + dot(moment_basis, glo_scr[u], 1, 1)
            for h in range(halves):
                columns = slice(h * LANES, (h + 1) * LANES)
                mom[h, pl.ds(ts[u], 8, stride=tiles), :] = moments[:, columns]
                for i in range(3):
                    mom[h, pl.ds((8 + i) * tiles + ts[u], 1), :] = rows_out[3 * u + i][:, columns]
        return carry

    lax.fori_loop(0, tiles // GROUP, group, 0)

    def got(i):
        return jnp.concatenate([mom[h, i * tiles : (i + 1) * tiles, :] for h in range(halves)], axis=1)

    m0, m1, m2, m3, m4, m5 = [got(i) for i in range(6)]
    su = m1 - mean_x * m0
    sv = m2 - mean_y * m0
    suu = m3 - mean_x * (m1 + su)
    suv = m4 - mean_x * m2 - mean_y * su
    svv = m5 - mean_y * (m2 + sv)
    grads = [
        LN2 * (2.0 * con_a * su + con_b * sv),
        LN2 * (con_b * su + 2.0 * con_c * sv),
        -0.5 * suu,
        -suv,
        -0.5 * svv,
        m0,
    ] + [got(8 + i) for i in range(3)]
    value_rows = [[g[t : t + 1, :] for g in grads] for t in range(tiles)]
    index_rows = [(slot_row[t : t + 1, :], slot_lane[t : t + 1, :]) for t in range(tiles)]
    scatter_products(value_rows, index_rows, spread, hot, table_rows)
    summed = dot(spread[...], hot[...], 1, 1)
    for f in range(FEATS):
        both = (
            summed[f * table_rows : (f + 1) * table_rows, :]
            + summed[(FEATS + f) * table_rows : (FEATS + f + 1) * table_rows, :]
        )
        for j in range(nd):
            outs[j][f] = both[j * rows : (j + 1) * rows, :]


def render(me, received, blocks, orders, counts, ids, target, nd, cap, rows):
    tiles, entries = blocks.shape[3:]
    pixels = SIDE * SIDE
    return pl.pallas_call(
        partial(render_kernel, nd=nd, cap=cap, rows=rows, tiles=tiles, entries=entries),
        in_specs=[smem_spec()] + [vmem_spec()] * (nd + 5),
        out_specs=[vmem_spec()] * (nd + 1),
        out_shape=[jax.ShapeDtypeStruct((FEATS, rows, LANES), F32)] * nd
        + [jax.ShapeDtypeStruct(target.shape, F32)],
        scratch_shapes=[
            pltpu.VMEM((entries // LANES, 32 * tiles, LANES), F32),
            pltpu.VMEM((GROUP, entries, pixels), F32),
            pltpu.VMEM((GROUP, entries, pixels), F32),
            pltpu.VMEM((GROUP, entries, pixels), F32),
            pltpu.VMEM((GROUP, entries, pixels), BF16),
            pltpu.VMEM((GROUP, entries, pixels), BF16),
            pltpu.VMEM((GROUP, entries, pixels), BF16),
            pltpu.VMEM((GROUP, entries, pixels), BF16),
            pltpu.VMEM((GROUP, 32, pixels), F32),
            pltpu.VMEM((entries // LANES, 11 * tiles, LANES), F32),
            pltpu.VMEM((2 * FEATS * nd * rows, tiles * entries), BF16),
            pltpu.VMEM((LANES, tiles * entries), BF16),
        ],
        compiler_params=pltpu.CompilerParams(vmem_limit_bytes=48 * 1024 * 1024),
        name="render_tiles",
    )(me, *received, blocks, orders, counts, ids, target)


def owner_kernel(me_ref, *refs, nd, rows, parts, nv, nc, out_rows):
    recv = refs[:nd]
    idx_ref, w_ref = refs[nd : nd + 2]
    outs = refs[nd + 2 : nd + 2 + parts]
    spread, hot, summed = refs[nd + 2 + parts :]
    my_view = me_ref[1]
    my_chip = me_ref[2]
    value_rows = []
    index_rows = []
    for n in range(nd * rows):
        value_rows.append([recv[n // rows][f, n % rows : n % rows + 1, :] for f in range(FEATS)])
        index = idx_ref[n : n + 1, :]
        index_rows.append((index >> 7, index & (LANES - 1)))
    scatter_products(value_rows, index_rows, spread, hot, out_rows)
    result = dot(spread[...], hot[...], 1, 1)
    share = out_rows // parts
    for f in range(FEATS):
        both = (
            result[f * out_rows : (f + 1) * out_rows, :]
            + result[(FEATS + f) * out_rows : (FEATS + f + 1) * out_rows, :]
        )
        for p in range(parts):
            summed[p, f] = both[p * share : (p + 1) * share, :]
    for p in range(parts):
        summed[p, FEATS] = w_ref[0:share, :]
    for dv in range(nv):
        for dc in range(nc):
            where = lax.rem(my_view + dv, nv) * nc + lax.rem(my_chip + dc, nc)
            outs[dv * nc + dc][...] = summed[where]


def owner_sums(me, received, index, weights, nd, rows, nv, nc, width):
    parts = nv * nc
    out_rows = width // LANES
    share = out_rows // parts
    return pl.pallas_call(
        partial(owner_kernel, nd=nd, rows=rows, parts=parts, nv=nv, nc=nc, out_rows=out_rows),
        in_specs=[smem_spec()] + [vmem_spec()] * (nd + 2),
        out_specs=[vmem_spec()] * parts,
        out_shape=[jax.ShapeDtypeStruct((FEATS + 1, share, LANES), F32)] * parts,
        scratch_shapes=[
            pltpu.VMEM((2 * FEATS * out_rows, nd * rows * LANES), BF16),
            pltpu.VMEM((LANES, nd * rows * LANES), BF16),
            pltpu.VMEM((parts, FEATS + 1, share, LANES), F32),
        ],
        compiler_params=pltpu.CompilerParams(vmem_limit_bytes=48 * 1024 * 1024),
        name="owner_sums",
    )(me, *received, index, weights)


def pullback_kernel(at_ref, params_ref, *refs, nv, nc, coefs):
    recv = refs[: nv * nc]
    out_ref, flat = refs[nv * nc :]
    share = recv[0].shape[1]
    columns = share * LANES

    def row(i):
        return params_ref[i : i + 1, :]

    lx, lyx, ly, lzx, lzy, lz = [row(i) for i in range(3, 9)]
    total = [jnp.zeros((1, columns), F32) for _ in range(10)]
    harmonics = [jnp.zeros((coefs, columns), F32) for _ in range(3)]
    square = lax.broadcasted_iota(jnp.int32, (coefs, LANES), 1) == lax.broadcasted_iota(
        jnp.int32, (coefs, LANES), 0
    ) + 10
    for v in range(nv):
        packed = recv[v * nc][FEATS]
        for i in range(share):
            block = recv[v * nc][0:FEATS, i, :]
            for c in range(1, nc):
                block = block + recv[v * nc + c][0:FEATS, i, :]
            flat[0:FEATS, i * LANES : (i + 1) * LANES] = block
        gx, gy, g0, g1, g2, gh, gr, gg, gb = [flat[f : f + 1, :] for f in range(FEATS)]
        cam = [[packed[i : i + 1, j : j + 1] for j in range(3)] for i in range(2)]
        for j in range(3):
            total[j] = total[j] + cam[0][j] * gx + cam[1][j] * gy
        m = []
        for i in range(2):
            a0, a1, a2 = cam[i]
            m.append((a0 * lx + a1 * lyx + a2 * lzx, a1 * ly + a2 * lzy, a2 * lz))
        upper = m[0][0] * m[0][0] + m[0][1] * m[0][1] + m[0][2] * m[0][2] + DILATION
        cross = m[0][0] * m[1][0] + m[0][1] * m[1][1] + m[0][2] * m[1][2]
        lower = m[1][0] * m[1][0] + m[1][1] * m[1][1] + m[1][2] * m[1][2] + DILATION
        inverse = 1.0 / (upper * lower - cross * cross)
        c0, c1, c2 = lower * inverse, -cross * inverse, upper * inverse
        h1 = 0.5 * g1
        k00, k01 = g0 * c0 + h1 * c1, g0 * c1 + h1 * c2
        k10, k11 = h1 * c0 + g2 * c1, h1 * c1 + g2 * c2
        s00 = -(c0 * k00 + c1 * k10)
        s01 = -(c0 * k01 + c1 * k11)
        s11 = -(c1 * k01 + c2 * k11)
        gm = [[2.0 * (s00 * m[0][k] + s01 * m[1][k]) for k in range(3)]]
        gm.append([2.0 * (s01 * m[0][k] + s11 * m[1][k]) for k in range(3)])
        at = 3
        for i in range(3):
            for k in range(i + 1):
                total[at] = total[at] + cam[0][i] * gm[0][k] + cam[1][i] * gm[1][k]
                at += 1
        total[9] = total[9] + gh
        basis = jnp.sum(jnp.where(square, packed[0:1, :], 0.0), axis=1, keepdims=True)
        for c, g in enumerate((gr, gg, gb)):
            harmonics[c] = harmonics[c] + basis * g
    logit = row(9)
    total[9] = total[9] / (1.0 + jnp.exp(logit))
    for i in range(10):
        out_ref[i : i + 1, :] = total[i]
    for c in range(3):
        out_ref[10 + c * coefs : 10 + (c + 1) * coefs, :] = harmonics[c]


def pull_back(at, params, received, nv, nc, coefs):
    parts = nv * nc
    columns = params.shape[1] // parts
    block = received[0].shape
    return pl.pallas_call(
        partial(pullback_kernel, nv=nv, nc=nc, coefs=coefs),
        grid_spec=pltpu.PrefetchScalarGridSpec(
            num_scalar_prefetch=1,
            grid=(1,),
            in_specs=[pl.BlockSpec((params.shape[0], columns), lambda i, at_ref: (0, at_ref[0]))]
            + [pl.BlockSpec(block, lambda i, at_ref: (0, 0, 0))] * parts,
            out_specs=pl.BlockSpec((params.shape[0], columns), lambda i, at_ref: (0, 0)),
            scratch_shapes=[pltpu.VMEM((16, columns), F32)],
        ),
        out_shape=jax.ShapeDtypeStruct((params.shape[0], columns), F32),
        compiler_params=pltpu.CompilerParams(vmem_limit_bytes=40 * 1024 * 1024),
        name="pull_back",
    )(at, params, *received)


def local(
    params,
    cameras,
    view_basis,
    tile_lists,
    margin_blocks,
    depth_orders,
    tile_counts,
    requests,
    target,
    *,
    nd,
    nv,
    nc,
):
    cap = requests.shape[4]
    rows = -(-cap // LANES)
    my_view = lax.axis_index("view")
    my_chip = lax.axis_index("chip")
    me = jnp.stack([lax.axis_index("dev"), my_view, my_chip]).astype(jnp.int32)
    at = (my_view * nc + my_chip).astype(jnp.int32).reshape(1)

    *packets, index, weights = send(me, cameras, view_basis, params, requests, nd, cap, rows)
    received = [packets[0]]
    for j in range(1, nd):
        received.append(lax.ppermute(packets[j], "dev", [(i, (i + j) % nd) for i in range(nd)]))
    *returns, images = render(
        me, received, margin_blocks, depth_orders, tile_counts, tile_lists, target, nd, cap, rows
    )
    back = [returns[0]]
    for j in range(1, nd):
        back.append(lax.ppermute(returns[j], "dev", [((i + j) % nd, i) for i in range(nd)]))
    shares = owner_sums(me, back, index, weights, nd, rows, nv, nc, params.shape[1])
    arrived = []
    for dv in range(nv):
        for dc in range(nc):
            pairs = [
                (v * nc + c, (v + dv) % nv * nc + (c + dc) % nc) for v in range(nv) for c in range(nc)
            ]
            piece = shares[dv * nc + dc]
            arrived.append(piece if dv + dc == 0 else lax.ppermute(piece, ("view", "chip"), pairs))
    grads = pull_back(at, params, arrived, nv, nc, view_basis.shape[1])
    return (grads, images)


def solution(mesh):
    return jax.shard_map(
        partial(local, nd=mesh.shape["dev"], nv=mesh.shape["view"], nc=mesh.shape["chip"]),
        mesh=mesh,
        in_specs=(
            P(None, ("groups", "dev")),
            P(("groups", "view"), None, None),
            P(("groups", "view"), None),
            P("view", ("groups", "dev"), "chip", None),
            P("view", ("groups", "dev"), "chip", None, None),
            P("view", ("groups", "dev"), "chip", None, None),
            P("view", ("groups", "dev"), "chip", None),
            P("view", None, "chip", ("groups", "dev"), None),
            P("view", ("groups", "dev"), "chip", None, None, None),
        ),
        out_specs=(
            P(None, ("groups", "dev", "view", "chip")),
            P("view", ("groups", "dev"), "chip", None, None, None),
        ),
        check_vma=False,
    )
```

```python
from functools import partial

import jax
import jax.numpy as jnp
from jax import lax
from jax.experimental import pallas as pl
from jax.experimental.pallas import tpu as pltpu
from jax.sharding import PartitionSpec as P

SIDE = 16
TW = 16
LANES = 128
LOG2E = 1.4426950408889634
LN2 = 0.6931471805599453
DILATION = 0.3
DEAD = -1e30
F32 = jnp.float32
BF16 = jnp.bfloat16
FEATS = 9
FORTH = (1, 2, 3)
BACK = (1, 2, 3)
GROUP = 16


def lane_take(row, index):
    return jnp.take_along_axis(row, index, axis=1, mode="promise_in_bounds")


def split2(x):
    hi = x.astype(BF16)
    return hi, (x - hi.astype(F32)).astype(BF16)


def dot(a, b, ca, cb):
    return lax.dot_general(a, b, (((ca,), (cb,)), ((), ())), preferred_element_type=F32)


def send_kernel(cam_hbm, basis_hbm, params_hbm, req_hbm, *refs, later, nd, nc, cap, rows):
    later_hbm = refs[:later]
    outs = refs[later : later + nd]
    idx_out, w_out, own_out = refs[later + nd : later + nd + 3]
    later_out = refs[later + nd + 3 : 2 * later + nd + 3]
    feat, w_scr, cam_ref, basis_ref, params_ref, req_ref, sems = refs[2 * later + nd + 3 :]
    me = lax.axis_index("dev")
    share = own_out.shape[1]
    owned = pl.multiple_of((lax.axis_index("view") * nc + lax.axis_index("chip")) * share, LANES)
    copies = [
        (params_hbm, params_ref),
        (cam_hbm, cam_ref),
        (basis_hbm, basis_ref),
        (req_hbm, req_ref),
        (params_hbm.at[:, pl.ds(owned, share)], own_out),
    ] + list(zip(later_hbm, later_out))
    copies = [pltpu.make_async_copy(source, target, sems.at[i]) for i, (source, target) in enumerate(copies)]
    for copy in copies:
        copy.start()
    for copy in copies[1:4]:
        copy.wait()
    width = params_ref.shape[1]
    coefs = basis_ref.shape[-1]
    idx_out[...] = jnp.zeros_like(idx_out)
    for j in range(nd):
        dest = me ^ j
        for i in range(rows):
            size = min(LANES, cap - i * LANES)
            idx_out[j * rows + i : j * rows + i + 1, 0:size] = req_ref[
                0, dest, 0, 0:1, i * LANES : i * LANES + size
            ]
    w_scr[...] = jnp.zeros_like(w_scr)
    w_scr[0:2, 0:4] = cam_ref[0]
    w_scr[2:3, 0:coefs] = basis_ref[...]
    packed = w_scr[...]
    lane8 = lax.broadcasted_iota(jnp.int32, (8, LANES), 1)
    row8 = lax.broadcasted_iota(jnp.int32, (8, LANES), 0)
    basis_row = jnp.broadcast_to(packed[2:3, :], (8, LANES))
    camera_row = jnp.where((row8 < 2), packed, 0.0)
    at10 = pltpu.roll(basis_row, 10, 1)
    w_out[...] = camera_row + jnp.where(row8 == 0, at10, 0.0)
    weights = jnp.where(lane8 < 3, camera_row, 0.0)
    weights = weights + jnp.where(row8 == 2, at10, 0.0)
    weights = weights + jnp.where(row8 == 3, pltpu.roll(basis_row, 10 + coefs, 1), 0.0)
    weights = weights + jnp.where(row8 == 4, pltpu.roll(basis_row, 10 + 2 * coefs, 1), 0.0)
    w_scr[...] = weights
    copies[0].wait()
    linear = lax.dot_general(
        w_scr[:, 0 : params_ref.shape[0]],
        params_ref[...],
        (((1,), (0,)), ((), ())),
        precision=lax.Precision.HIGHEST,
        preferred_element_type=F32,
    )

    def cam(i, j):
        return cam_ref[0, i : i + 1, j : j + 1]

    def row(i):
        return params_ref[i : i + 1, :]

    lx, lyx, ly, lzx, lzy, lz = [row(i) for i in range(3, 9)]
    m = []
    for i in range(2):
        a0, a1, a2 = cam(i, 0), cam(i, 1), cam(i, 2)
        m.append((a0 * lx + a1 * lyx + a2 * lzx, a1 * ly + a2 * lzy, a2 * lz))
    upper = m[0][0] * m[0][0] + m[0][1] * m[0][1] + m[0][2] * m[0][2] + DILATION
    cross = m[0][0] * m[1][0] + m[0][1] * m[1][1] + m[0][2] * m[1][2]
    lower = m[1][0] * m[1][0] + m[1][1] * m[1][1] + m[1][2] * m[1][2] + DILATION
    inverse = 1.0 / (upper * lower - cross * cross)
    logit = row(9)
    log_opacity = jnp.minimum(logit, 0.0) * LOG2E - LOG2E * jnp.log(1.0 + jnp.exp(-jnp.abs(logit)))
    feat[0:1, :] = linear[0:1, :] + cam(0, 3)
    feat[1:2, :] = linear[1:2, :] + cam(1, 3)
    feat[2:3, :] = lower * inverse * (0.5 * LOG2E)
    feat[3:4, :] = -cross * inverse * LOG2E
    feat[4:5, :] = upper * inverse * (0.5 * LOG2E)
    feat[5:6, :] = log_opacity
    for c in range(3):
        feat[6 + c : 7 + c, :] = linear[2 + c : 3 + c, :] + 0.5

    total = nd * rows
    step = 8 if total % 8 == 0 else total
    source_rows = width // LANES
    for first in range(0, total, step):
        index = idx_out[first : first + step, :]
        low = index & (LANES - 1)
        high = index >> 7
        acc = [jnp.zeros((step, LANES), F32) for _ in range(FEATS)]
        for r in range(source_rows):
            here = high == r
            for f in range(FEATS):
                source = jnp.broadcast_to(feat[f : f + 1, r * LANES : (r + 1) * LANES], (step, LANES))
                acc[f] = jnp.where(here, lane_take(source, low), acc[f])
        for f in range(FEATS):
            for n in range(step):
                j, i = divmod(first + n, rows)
                if rows % step == 0:
                    if n == 0:
                        outs[j][f, i : i + step, :] = acc[f]
                else:
                    outs[j][f, i : i + 1, :] = acc[f][n : n + 1, :]
    for copy in copies[4:]:
        copy.wait()


def vmem_spec():
    return pl.BlockSpec(memory_space=pltpu.VMEM)


def smem_spec():
    return pl.BlockSpec(memory_space=pltpu.SMEM)


def send(cameras, basis, params, requests, later, nd, nv, nc, cap, rows):
    count, width = params.shape
    first = (cameras, basis, params, requests)
    out_shape = [jax.ShapeDtypeStruct((FEATS, rows, LANES), F32)] * nd
    out_shape += [
        jax.ShapeDtypeStruct((nd * rows, LANES), jnp.int32),
        jax.ShapeDtypeStruct((8, LANES), F32),
        jax.ShapeDtypeStruct((count, width // (nv * nc)), F32),
    ]
    out_shape += [jax.ShapeDtypeStruct(x.shape, x.dtype) for x in later]
    return pl.pallas_call(
        partial(send_kernel, later=len(later), nd=nd, nc=nc, cap=cap, rows=rows),
        in_specs=[pl.BlockSpec(memory_space=pl.ANY)] * (4 + len(later)),
        out_specs=[vmem_spec()] * len(out_shape),
        out_shape=out_shape,
        scratch_shapes=[pltpu.VMEM((16, width), F32), pltpu.VMEM((8, LANES), F32)]
        + [pltpu.VMEM(x.shape, x.dtype) for x in first]
        + [pltpu.SemaphoreType.DMA((5 + len(later),))],
        compiler_params=pltpu.CompilerParams(vmem_limit_bytes=60 * 1024 * 1024),
        name="project_gather",
    )(*first, *later)


def fold_of(block):
    return 2 if block % 2 == 0 else 1


def fold(row, lane, block):
    wide = fold_of(block)
    height = block // wide
    inside = lax.rem(row, block)
    return lax.div(row, block) * height + lax.rem(inside, height), lax.div(inside, height) * LANES + lane


def place_hot(hot, at, column, wide):
    size = column.shape[0]
    lane = lax.broadcasted_iota(jnp.int32, (size, wide * LANES), 1)
    hot[at : at + size, :] = jnp.where(lane == column, 1.0, 0.0).astype(BF16)


def place_mask(mask, at, row):
    size = row.shape[1]
    high = lax.broadcasted_iota(jnp.int32, (mask.shape[0], size), 0)
    mask[:, at : at + size] = jnp.where(high == row, 1.0, 0.0).astype(BF16)


def place_values(spread, at, mask, values):
    height, size = mask.shape
    for f, pair in enumerate(values):
        for part, row in enumerate(pair):
            base = (part * FEATS + f) * height
            wide_row = jnp.broadcast_to(row, (height, size)).astype(BF16)
            spread[base : base + height, at : at + size] = mask * wide_row


def exact_parts(x):
    hi = x.astype(BF16).astype(F32)
    return hi, (x - hi).astype(BF16).astype(F32)


def take_rows(source, high, low, first_row, count, start):
    acc = list(start)
    for n in range(first_row, first_row + count):
        here = high == n
        for f in range(FEATS):
            value = jnp.broadcast_to(source(f, n), low.shape)
            acc[f] = jnp.where(here, lane_take(value, low), acc[f])
    return acc


def index_kernel(
    own_ref, blocks_ref, orders_ref, counts_ref, high_out, low_out, live_out, part_out, mask_out, hot_out, *, nd, cap
):
    me = lax.axis_index("dev")
    rows = own_ref.shape[1]
    tiles, entries = blocks_ref.shape[3:]
    chunk = entries // 8
    halves = entries // LANES

    place = lax.broadcasted_iota(jnp.int32, (tiles, entries), 1)
    rank = (place & 7) * chunk + (place >> 3)

    def take_wide(source, index):
        parts = []
        for c in range(halves):
            wanted = index[:, c * LANES : (c + 1) * LANES]
            low = wanted & (LANES - 1)
            high = wanted >> 7
            value = lane_take(source[:, 0:LANES], low)
            for h in range(1, halves):
                value = jnp.where(high == h, lane_take(source[:, h * LANES : (h + 1) * LANES], low), value)
            parts.append(value)
        return jnp.concatenate(parts, axis=1)

    order = take_wide(orders_ref[0, 0, 0], rank)
    slot = take_wide(blocks_ref[0, 0, 0], order)
    shard = jnp.zeros_like(slot)
    for i in range(1, nd):
        shard = shard + (slot >= i * cap).astype(jnp.int32)
    offset = slot - shard * cap
    slot_row = (shard ^ me) * rows + (offset >> 7)
    slot_lane = offset & (LANES - 1)
    high_out[...] = slot_row
    low_out[...] = slot_lane
    live_out[...] = jnp.where(rank < column_of(counts_ref, tiles), 1.0, 0.0)
    for c in range(halves):
        columns = slice(c * LANES, (c + 1) * LANES)
        for first in range(0, tiles, 8):
            low = slot_lane[first : first + 8, columns]
            high = slot_row[first : first + 8, columns]
            start = [jnp.zeros((8, LANES), F32)] * FEATS
            acc = take_rows(lambda f, n: own_ref[f, n : n + 1, :], high, low, 0, rows, start)
            for f in range(FEATS):
                part_out[f, first : first + 8, columns] = acc[f]
    wide = fold_of(rows)
    key_high, key_low = fold(slot_row, slot_lane, rows)
    key_columns = key_low.astype(F32).T.astype(jnp.int32)
    for t in range(tiles):
        place_mask(mask_out, t * entries, key_high[t : t + 1, :])
        place_hot(hot_out, t * entries, key_columns[:, t : t + 1], wide)


def tile_indices(own, blocks, orders, counts, nd, cap):
    rows = own.shape[1]
    tiles, entries = blocks.shape[3:]
    wide = fold_of(rows)
    return pl.pallas_call(
        partial(index_kernel, nd=nd, cap=cap),
        in_specs=[vmem_spec()] * 4,
        out_specs=[vmem_spec()] * 6,
        out_shape=[
            jax.ShapeDtypeStruct((tiles, entries), jnp.int32),
            jax.ShapeDtypeStruct((tiles, entries), jnp.int32),
            jax.ShapeDtypeStruct((tiles, entries), F32),
            jax.ShapeDtypeStruct((FEATS, tiles, entries), F32),
            jax.ShapeDtypeStruct((nd * rows // wide, tiles * entries), BF16),
            jax.ShapeDtypeStruct((tiles * entries, wide * LANES), BF16),
        ],
        compiler_params=pltpu.CompilerParams(vmem_limit_bytes=40 * 1024 * 1024),
        name="prep_tiles",
    )(own, blocks, orders, counts)


def column_of(ref, tiles):
    square = jnp.broadcast_to(ref[0, 0].astype(F32), (tiles, tiles))
    diagonal = lax.broadcasted_iota(jnp.int32, (tiles, tiles), 0) == lax.broadcasted_iota(jnp.int32, (tiles, tiles), 1)
    return jnp.sum(jnp.where(diagonal, square, 0.0), axis=1, keepdims=True).astype(jnp.int32)


def render_kernel(*refs, nd, rows, tiles, entries):
    recv = refs[: nd - 1]
    high_ref, low_ref, live_ref, part_ref, mask_ref, hot_ref, ids_ref, target_ref = refs[nd - 1 : nd + 7]
    outs = refs[nd + 7 : 2 * nd + 7]
    (images_ref, coef, a_scr, t_scr, q_scr, whi_scr, wlo_scr, ghi_scr, glo_scr, g_rows, mom, spread) = refs[2 * nd + 7 :]
    pixels = SIDE * SIDE
    halves = entries // LANES
    table_rows = nd * rows

    def put(ref, at, value):
        for h in range(halves):
            ref[h, at : at + value.shape[0], :] = value[:, h * LANES : (h + 1) * LANES]

    tile_id = column_of(ids_ref, tiles)
    centre_x = ((tile_id % TW) * SIDE).astype(F32) + 0.5 * SIDE
    centre_y = ((tile_id // TW) * SIDE).astype(F32) + 0.5 * SIDE
    live = live_ref[...] > 0.5

    pieces = [[[] for _ in range(halves)] for _ in range(FEATS)]
    for c in range(halves):
        columns = slice(c * LANES, (c + 1) * LANES)
        for first in range(0, tiles, 8):
            low = low_ref[first : first + 8, columns]
            high = high_ref[first : first + 8, columns]
            start = [part_ref[f, first : first + 8, columns] for f in range(FEATS)]
            acc = take_rows(
                lambda f, n: recv[n // rows - 1][f, n % rows : n % rows + 1, :], high, low, rows, table_rows - rows, start
            )
            for f in range(FEATS):
                pieces[f][c].append(acc[f])
    pieces = [[jnp.concatenate(p, axis=0) for p in both] for both in pieces]
    mean_x, mean_y, con_a, con_b, con_c, log_op, red, green, blue = [jnp.concatenate(p, axis=1) for p in pieces]
    mean_x = mean_x - centre_x
    mean_y = mean_y - centre_y
    bx = con_a * mean_x
    by = con_c * mean_y
    constant = log_op - (bx * mean_x + con_b * mean_x * mean_y + by * mean_y)
    constant = jnp.where(live, constant, DEAD)
    poly = [constant, 2.0 * bx + con_b * mean_y, 2.0 * by + con_b * mean_x, -con_a, -con_b, -con_c]
    for i, value in enumerate(poly):
        rest = value
        for part in range(3):
            piece = rest.astype(BF16).astype(F32)
            rest = rest - piece
            at = (6 * part + i) * tiles
            put(coef, at, piece)
    for i, value in enumerate((red, green, blue)):
        first = value.astype(BF16).astype(F32)
        second = (value - first).astype(BF16).astype(F32)
        for block, piece in enumerate((first, first, second, second)):
            at = (18 + 3 * block + i) * tiles
            put(coef, at, piece)
    coef[:, 30 * tiles : 32 * tiles, :] = jnp.zeros((halves, 2 * tiles, LANES), F32)

    pixel = lax.broadcasted_iota(jnp.int32, (1, pixels), 1)
    px = (pixel & (SIDE - 1)).astype(F32) + (0.5 - 0.5 * SIDE)
    py = (pixel >> 4).astype(F32) + (0.5 - 0.5 * SIDE)
    one = jnp.ones((1, pixels), F32)
    monomials = [one, px, py, px * px, px * py, py * py]
    zero = jnp.zeros((1, pixels), F32)
    basis_scr = g_rows.at[0]
    for part in range(3):
        for i in range(6):
            basis_scr[6 * part + i : 6 * part + i + 1, :] = monomials[i]
    basis_scr[18:32, :] = jnp.zeros((14, pixels), F32)
    basis = basis_scr[...].astype(BF16)
    moment_basis = jnp.concatenate(monomials + [zero, zero], axis=0).astype(BF16)
    g_rows[...] = jnp.zeros_like(g_rows)

    sub_e = lax.broadcasted_iota(jnp.int32, (8, entries), 0)
    own_chunk = jnp.where(sub_e == (lax.broadcasted_iota(jnp.int32, (8, entries), 1) & 7), 1.0, 0.0)
    sub_p = lax.broadcasted_iota(jnp.int32, (8, pixels), 0)

    def down(x, by, fill):
        return jnp.where(sub_p >= by, pltpu.roll(x, by, 0), fill)

    def up(x, by, fill):
        return jnp.where(sub_p < 8 - by, pltpu.roll(x, 8 - by, 0), fill)

    def group(step, carry):
        lanes = range(GROUP)
        ts = [step * GROUP + u for u in lanes]
        tables, lhs = [], []
        for u in lanes:
            table = [coef[h, pl.ds(ts[u], 32, stride=tiles), :] for h in range(halves)]
            tables.append(jnp.concatenate(table, axis=1))
            lhs.append(tables[u].T.astype(BF16))
            a_scr[u] = jnp.exp2(jnp.minimum(dot(lhs[u], basis, 1, 0), 0.0))
        trans = [jnp.ones((8, pixels), F32) for _ in lanes]
        for jj in range(entries // 16):
            for u in lanes:
                w = []
                for h in range(2):
                    at = slice(16 * jj + 8 * h, 16 * jj + 8 * h + 8)
                    t_scr[u, at, :] = trans[u]
                    value = trans[u] * a_scr[u, at, :]
                    trans[u] = trans[u] - value
                    w.append(value)
                at = slice(16 * jj, 16 * jj + 16)
                whi_scr[u, at, :], wlo_scr[u, at, :] = split2(jnp.concatenate(w, axis=0))
        befores, tints, behinds = [], [], []
        for u in lanes:
            table, t = tables[u], ts[u]
            colour = [own_chunk * table[18 + i : 19 + i, :] for i in range(3)]
            colour = colour + [own_chunk * table[24 + i : 25 + i, :] for i in range(3)]
            colour = jnp.concatenate(colour, axis=0).astype(BF16)
            local = dot(colour, whi_scr[u], 1, 0) + dot(colour, wlo_scr[u], 1, 0)
            local = [local[8 * i : 8 * i + 8, :] + local[24 + 8 * i : 32 + 8 * i, :] for i in range(3)]
            before = down(trans[u], 1, 1.0)
            for by in (1, 2, 4):
                before = before * down(before, by, 1.0)
            tinted = []
            inner = jnp.zeros((8, pixels), F32)
            for i in range(3):
                image = jnp.sum(before * local[i], axis=0, keepdims=True)
                images_ref[0, 0, 0, i, pl.ds(t, 1), :] = image
                residual = image - target_ref[0, 0, 0, i, pl.ds(t, 1), :]
                first = residual.astype(BF16).astype(F32)
                second = (residual - first).astype(BF16).astype(F32)
                g_rows[u, 18 + i : 19 + i, :] = first
                g_rows[u, 21 + i : 22 + i, :] = second
                g_rows[u, 24 + i : 25 + i, :] = first
                g_rows[u, 27 + i : 28 + i, :] = second
                tinted.append(before * residual)
                inner = inner + residual * local[i]
            q_scr[u] = dot(lhs[u], g_rows[u].astype(BF16), 1, 0)
            tinted_hi, tinted_lo = split2(jnp.concatenate(tinted, axis=0))
            tints.append(jnp.concatenate([tinted_hi.astype(F32), tinted_lo.astype(F32)], axis=0).astype(BF16))
            add = up(inner, 1, 0.0)
            scale = up(trans[u], 1, 0.0)
            for by in (1, 2, 4):
                add = add + scale * up(add, by, 0.0)
                scale = scale * up(scale, by, 0.0)
            behinds.append(add)
            befores.append(before)
        rows_out = []
        for u in lanes:
            colour_grad = dot(tints[u], whi_scr[u], 1, 1) + dot(tints[u], wlo_scr[u], 1, 1)
            for i in range(3):
                both = colour_grad[8 * i : 8 * i + 8, :] + colour_grad[24 + 8 * i : 32 + 8 * i, :]
                rows_out.append(jnp.sum(own_chunk * both, axis=0, keepdims=True))
        for jj in reversed(range(entries // 16)):
            for u in lanes:
                g = [None, None]
                for h in (1, 0):
                    at = slice(16 * jj + 8 * h, 16 * jj + 8 * h + 8)
                    moved = a_scr[u, at, :] * (q_scr[u, at, :] - behinds[u])
                    behinds[u] = behinds[u] + moved
                    g[h] = (t_scr[u, at, :] * befores[u]) * moved
                at = slice(16 * jj, 16 * jj + 16)
                ghi_scr[u, at, :], glo_scr[u, at, :] = split2(jnp.concatenate(g, axis=0))
        for u in lanes:
            moments = dot(moment_basis, ghi_scr[u], 1, 1) + dot(moment_basis, glo_scr[u], 1, 1)
            for h in range(halves):
                columns = slice(h * LANES, (h + 1) * LANES)
                mom[h, pl.ds(ts[u], 8, stride=tiles), :] = moments[:, columns]
                for i in range(3):
                    mom[h, pl.ds((8 + i) * tiles + ts[u], 1), :] = rows_out[3 * u + i][:, columns]
        return carry

    if tiles == GROUP:
        group(0, 0)
    else:
        lax.fori_loop(0, tiles // GROUP, group, 0)

    def got(i):
        return jnp.concatenate([mom[h, i * tiles : (i + 1) * tiles, :] for h in range(halves)], axis=1)

    m0, m1, m2, m3, m4, m5 = [got(i) for i in range(6)]
    su = m1 - mean_x * m0
    sv = m2 - mean_y * m0
    suu = m3 - mean_x * (m1 + su)
    suv = m4 - mean_x * m2 - mean_y * su
    svv = m5 - mean_y * (m2 + sv)
    grads = [
        LN2 * (2.0 * con_a * su + con_b * sv),
        LN2 * (con_b * su + 2.0 * con_c * sv),
        -0.5 * suu,
        -suv,
        -0.5 * svv,
        m0,
    ] + [got(8 + i) for i in range(3)]
    parts = [exact_parts(g) for g in grads]
    for t in range(tiles):
        at = t * entries
        values = [[x[t : t + 1, :] for x in pair] for pair in parts]
        place_values(spread, at, mask_ref[:, at : at + entries], values)
    summed = dot(spread[...], hot_ref[...], 1, 0)
    wide = fold_of(rows)
    height = rows // wide
    total = table_rows // wide
    for f in range(FEATS):
        both = summed[f * total : (f + 1) * total, :] + summed[(FEATS + f) * total : (FEATS + f + 1) * total, :]
        for j in range(nd):
            for h in range(wide):
                outs[j][f, h * height : (h + 1) * height, :] = both[
                    j * height : (j + 1) * height, h * LANES : (h + 1) * LANES
                ]


def render(received, prepared, ids, target, nd, rows, tiles, entries):
    pixels = SIDE * SIDE
    return pl.pallas_call(
        partial(render_kernel, nd=nd, rows=rows, tiles=tiles, entries=entries),
        in_specs=[vmem_spec()] * (nd + 7),
        out_specs=[vmem_spec()] * (nd + 1),
        out_shape=[jax.ShapeDtypeStruct((FEATS, rows, LANES), F32)] * nd
        + [jax.ShapeDtypeStruct(target.shape, F32)],
        scratch_shapes=[
            pltpu.VMEM((entries // LANES, 32 * tiles, LANES), F32),
            pltpu.VMEM((GROUP, entries, pixels), F32),
            pltpu.VMEM((GROUP, entries, pixels), F32),
            pltpu.VMEM((GROUP, entries, pixels), F32),
            pltpu.VMEM((GROUP, entries, pixels), BF16),
            pltpu.VMEM((GROUP, entries, pixels), BF16),
            pltpu.VMEM((GROUP, entries, pixels), BF16),
            pltpu.VMEM((GROUP, entries, pixels), BF16),
            pltpu.VMEM((GROUP, 32, pixels), F32),
            pltpu.VMEM((entries // LANES, 11 * tiles, LANES), F32),
            pltpu.VMEM((2 * FEATS * nd * rows // fold_of(rows), tiles * entries), BF16),
        ],
        compiler_params=pltpu.CompilerParams(vmem_limit_bytes=48 * 1024 * 1024),
        name="render_tiles",
    )(*received, *prepared, ids, target)


def owner_index_kernel(own_ref, idx_ref, mask_out, hot_out, sum_out, spread, *, share):
    rows = own_ref.shape[1]
    index = idx_ref[...]
    key_high, key_low = fold(index >> 7, index & (LANES - 1), share)
    key_columns = key_low.astype(F32).T.astype(jnp.int32)
    wide = fold_of(share)
    for n in range(idx_ref.shape[0]):
        place_mask(mask_out, n * LANES, key_high[n : n + 1, :])
        place_hot(hot_out, n * LANES, key_columns[:, n : n + 1], wide)
    parts = [exact_parts(own_ref[f]) for f in range(FEATS)]
    for n in range(rows):
        values = [[x[n : n + 1, :] for x in pair] for pair in parts]
        place_values(spread, n * LANES, mask_out[:, n * LANES : (n + 1) * LANES], values)
    sum_out[...] = dot(spread[...], hot_out[0 : rows * LANES, :], 1, 0)


def owner_indices(own, index, share, width):
    rows = own.shape[1]
    wide = fold_of(share)
    height = width // LANES // wide
    slots = index.shape[0] * LANES
    return pl.pallas_call(
        partial(owner_index_kernel, share=share),
        in_specs=[vmem_spec()] * 2,
        out_specs=[vmem_spec()] * 3,
        out_shape=[
            jax.ShapeDtypeStruct((height, slots), BF16),
            jax.ShapeDtypeStruct((slots, wide * LANES), BF16),
            jax.ShapeDtypeStruct((2 * FEATS * height, wide * LANES), F32),
        ],
        scratch_shapes=[pltpu.VMEM((2 * FEATS * height, rows * LANES), BF16)],
        compiler_params=pltpu.CompilerParams(vmem_limit_bytes=40 * 1024 * 1024),
        name="prep_owner",
    )(own, index)


def owner_kernel(*refs, nd, rows, parts, nv, nc, share):
    recv = refs[: nd - 1]
    mask_ref, hot_ref, sum_ref, w_ref = refs[nd - 1 : nd + 3]
    outs = refs[nd + 3 : nd + 3 + parts]
    spread, summed = refs[nd + 3 + parts :]
    my_view = lax.axis_index("view")
    my_chip = lax.axis_index("chip")
    skip = rows * LANES
    for j in range(nd - 1):
        pairs = [exact_parts(recv[j][f]) for f in range(FEATS)]
        for i in range(rows):
            at = (j * rows + i) * LANES
            values = [[x[i : i + 1, :] for x in pair] for pair in pairs]
            place_values(spread, at, mask_ref[:, skip + at : skip + at + LANES], values)
    result = sum_ref[...] + dot(spread[...], hot_ref[skip:, :], 1, 0)
    wide = fold_of(share)
    height = share // wide
    total = parts * height
    for f in range(FEATS):
        both = result[f * total : (f + 1) * total, :] + result[(FEATS + f) * total : (FEATS + f + 1) * total, :]
        for p in range(parts):
            for h in range(wide):
                summed[p, f, h * height : (h + 1) * height, :] = both[
                    p * height : (p + 1) * height, h * LANES : (h + 1) * LANES
                ]
    for p in range(parts):
        summed[p, FEATS] = w_ref[0:share, :]
    for dv in range(nv):
        for dc in range(nc):
            where = lax.rem(my_view + dv, nv) * nc + lax.rem(my_chip + dc, nc)
            outs[dv * nc + dc][...] = summed[where]


def owner_sums(received, prepared, weights, nd, rows, nv, nc, share):
    parts = nv * nc
    height, slots = prepared[0].shape
    return pl.pallas_call(
        partial(owner_kernel, nd=nd, rows=rows, parts=parts, nv=nv, nc=nc, share=share),
        in_specs=[vmem_spec()] * (nd + 3),
        out_specs=[vmem_spec()] * parts,
        out_shape=[jax.ShapeDtypeStruct((FEATS + 1, share, LANES), F32)] * parts,
        scratch_shapes=[
            pltpu.VMEM((2 * FEATS * height, slots - rows * LANES), BF16),
            pltpu.VMEM((parts, FEATS + 1, share, LANES), F32),
        ],
        compiler_params=pltpu.CompilerParams(vmem_limit_bytes=40 * 1024 * 1024),
        name="owner_sums",
    )(*received, *prepared, weights)


def pullback_kernel(params_ref, *refs, nv, nc, coefs):
    recv = refs[: nv * nc]
    out_ref, flat = refs[nv * nc :]
    share = recv[0].shape[1]
    columns = share * LANES

    def row(i):
        return params_ref[i : i + 1, :]

    lx, lyx, ly, lzx, lzy, lz = [row(i) for i in range(3, 9)]
    total = [jnp.zeros((1, columns), F32) for _ in range(10)]
    harmonics = [jnp.zeros((coefs, columns), F32) for _ in range(3)]
    square = lax.broadcasted_iota(jnp.int32, (coefs, LANES), 1) == lax.broadcasted_iota(
        jnp.int32, (coefs, LANES), 0
    ) + 10
    for v in range(nv):
        packed = recv[v * nc][FEATS]
        for i in range(share):
            block = recv[v * nc][0:FEATS, i, :]
            for c in range(1, nc):
                block = block + recv[v * nc + c][0:FEATS, i, :]
            flat[0:FEATS, i * LANES : (i + 1) * LANES] = block
        gx, gy, g0, g1, g2, gh, gr, gg, gb = [flat[f : f + 1, :] for f in range(FEATS)]
        cam = [[packed[i : i + 1, j : j + 1] for j in range(3)] for i in range(2)]
        for j in range(3):
            total[j] = total[j] + cam[0][j] * gx + cam[1][j] * gy
        m = []
        for i in range(2):
            a0, a1, a2 = cam[i]
            m.append((a0 * lx + a1 * lyx + a2 * lzx, a1 * ly + a2 * lzy, a2 * lz))
        upper = m[0][0] * m[0][0] + m[0][1] * m[0][1] + m[0][2] * m[0][2] + DILATION
        cross = m[0][0] * m[1][0] + m[0][1] * m[1][1] + m[0][2] * m[1][2]
        lower = m[1][0] * m[1][0] + m[1][1] * m[1][1] + m[1][2] * m[1][2] + DILATION
        inverse = 1.0 / (upper * lower - cross * cross)
        c0, c1, c2 = lower * inverse, -cross * inverse, upper * inverse
        h1 = 0.5 * g1
        k00, k01 = g0 * c0 + h1 * c1, g0 * c1 + h1 * c2
        k10, k11 = h1 * c0 + g2 * c1, h1 * c1 + g2 * c2
        s00 = -(c0 * k00 + c1 * k10)
        s01 = -(c0 * k01 + c1 * k11)
        s11 = -(c1 * k01 + c2 * k11)
        gm = [[2.0 * (s00 * m[0][k] + s01 * m[1][k]) for k in range(3)]]
        gm.append([2.0 * (s01 * m[0][k] + s11 * m[1][k]) for k in range(3)])
        at = 3
        for i in range(3):
            for k in range(i + 1):
                total[at] = total[at] + cam[0][i] * gm[0][k] + cam[1][i] * gm[1][k]
                at += 1
        total[9] = total[9] + gh
        basis = jnp.sum(jnp.where(square, packed[0:1, :], 0.0), axis=1, keepdims=True)
        for c, g in enumerate((gr, gg, gb)):
            harmonics[c] = harmonics[c] + basis * g
    logit = row(9)
    total[9] = total[9] / (1.0 + jnp.exp(logit))
    for i in range(10):
        out_ref[i : i + 1, :] = total[i]
    for c in range(3):
        out_ref[10 + c * coefs : 10 + (c + 1) * coefs, :] = harmonics[c]


def pull_back(params, received, nv, nc, coefs):
    return pl.pallas_call(
        partial(pullback_kernel, nv=nv, nc=nc, coefs=coefs),
        in_specs=[vmem_spec()] * (1 + nv * nc),
        out_specs=vmem_spec(),
        out_shape=jax.ShapeDtypeStruct(params.shape, F32),
        scratch_shapes=[pltpu.VMEM((16, params.shape[1]), F32)],
        compiler_params=pltpu.CompilerParams(vmem_limit_bytes=40 * 1024 * 1024),
        name="pull_back",
    )(params, *received)


def hop_order(nd, first):
    return [j for j in first if j < nd] + [j for j in range(1, nd) if j not in first]


def local(
    params,
    cameras,
    view_basis,
    tile_lists,
    margin_blocks,
    depth_orders,
    tile_counts,
    requests,
    target,
    *,
    nd,
    nv,
    nc,
):
    cap = requests.shape[4]
    rows = -(-cap // LANES)
    later = (margin_blocks, depth_orders, tile_counts, tile_lists, jnp.swapaxes(target, 3, 4))
    outs = send(cameras, view_basis, params, requests, later, nd, nv, nc, cap, rows)
    packets = outs[:nd]
    index, weights, owned, blocks, orders, counts, ids, swapped = outs[nd:]
    received = list(packets)
    for j in hop_order(nd, FORTH):
        received[j] = lax.ppermute(packets[j], "dev", [(i, i ^ j) for i in range(nd)])
    prepared = tile_indices(packets[0], blocks, orders, counts, nd, cap)
    tiles, entries = margin_blocks.shape[3:]
    *returns, images = render(received[1:], prepared, ids, swapped, nd, rows, tiles, entries)
    back = list(returns)
    for j in hop_order(nd, BACK):
        back[j] = lax.ppermute(returns[j], "dev", [(i, i ^ j) for i in range(nd)])
    share = params.shape[1] // LANES // (nv * nc)
    sorted_own = owner_indices(returns[0], index, share, params.shape[1])
    shares = owner_sums(back[1:], sorted_own, weights, nd, rows, nv, nc, share)
    arrived = []
    for dv in range(nv):
        for dc in range(nc):
            pairs = [
                (v * nc + c, (v + dv) % nv * nc + (c + dc) % nc) for v in range(nv) for c in range(nc)
            ]
            piece = shares[dv * nc + dc]
            arrived.append(piece if dv + dc == 0 else lax.ppermute(piece, ("view", "chip"), pairs))
    grads = pull_back(owned, arrived, nv, nc, view_basis.shape[1])
    return (grads, jnp.swapaxes(images, 3, 4))


def solution(mesh):
    return jax.shard_map(
        partial(local, nd=mesh.shape["dev"], nv=mesh.shape["view"], nc=mesh.shape["chip"]),
        mesh=mesh,
        in_specs=(
            P(None, ("groups", "dev")),
            P(("groups", "view"), None, None),
            P(("groups", "view"), None),
            P("view", ("groups", "dev"), "chip", None),
            P("view", ("groups", "dev"), "chip", None, None),
            P("view", ("groups", "dev"), "chip", None, None),
            P("view", ("groups", "dev"), "chip", None),
            P("view", None, "chip", ("groups", "dev"), None),
            P("view", ("groups", "dev"), "chip", None, None, None),
        ),
        out_specs=(
            P(None, ("groups", "dev", "view", "chip")),
            P("view", ("groups", "dev"), "chip", None, None, None),
        ),
        check_vma=False,
    )
```

```python
from functools import partial

import jax
import jax.numpy as jnp
from jax import lax
from jax.experimental import pallas as pl
from jax.experimental.pallas import tpu as pltpu
from jax.sharding import PartitionSpec as P

SIDE = 16
TW = 16
LANES = 128
LOG2E = 1.4426950408889634
LN2 = 0.6931471805599453
DILATION = 0.3
DEAD = -1e30
F32 = jnp.float32
BF16 = jnp.bfloat16
FEATS = 9
FORTH = (1, 2, 3)
BACK = (1, 2, 3)
GROUP = 16


def lane_take(row, index):
    return jnp.take_along_axis(row, index, axis=1, mode="promise_in_bounds")


def split2(x):
    hi = x.astype(BF16)
    return hi, (x - hi.astype(F32)).astype(BF16)


def dot(a, b, ca, cb):
    return lax.dot_general(a, b, (((ca,), (cb,)), ((), ())), preferred_element_type=F32)


def send_kernel(me_ref, cam_ref, basis_ref, params_ref, req_ref, *refs, nd, cap, rows):
    outs = refs[:nd]
    idx_out, w_out, feat, w_scr = refs[nd:]
    me = me_ref[0]
    width = params_ref.shape[1]
    coefs = basis_ref.shape[-1]
    w_scr[...] = jnp.zeros_like(w_scr)
    w_scr[0:2, 0:4] = cam_ref[0]
    w_scr[2:3, 0:coefs] = basis_ref[...]
    packed = w_scr[...]
    lane8 = lax.broadcasted_iota(jnp.int32, (8, LANES), 1)
    row8 = lax.broadcasted_iota(jnp.int32, (8, LANES), 0)
    basis_row = jnp.broadcast_to(packed[2:3, :], (8, LANES))
    camera_row = jnp.where((row8 < 2), packed, 0.0)
    at10 = pltpu.roll(basis_row, 10, 1)
    w_out[...] = camera_row + jnp.where(row8 == 0, at10, 0.0)
    weights = jnp.where(lane8 < 3, camera_row, 0.0)
    weights = weights + jnp.where(row8 == 2, at10, 0.0)
    weights = weights + jnp.where(row8 == 3, pltpu.roll(basis_row, 10 + coefs, 1), 0.0)
    weights = weights + jnp.where(row8 == 4, pltpu.roll(basis_row, 10 + 2 * coefs, 1), 0.0)
    w_scr[...] = weights
    linear = lax.dot_general(
        w_scr[:, 0 : params_ref.shape[0]],
        params_ref[...],
        (((1,), (0,)), ((), ())),
        precision=lax.Precision.HIGHEST,
        preferred_element_type=F32,
    )

    def cam(i, j):
        return cam_ref[0, i : i + 1, j : j + 1]

    def row(i):
        return params_ref[i : i + 1, :]

    lx, lyx, ly, lzx, lzy, lz = [row(i) for i in range(3, 9)]
    m = []
    for i in range(2):
        a0, a1, a2 = cam(i, 0), cam(i, 1), cam(i, 2)
        m.append((a0 * lx + a1 * lyx + a2 * lzx, a1 * ly + a2 * lzy, a2 * lz))
    upper = m[0][0] * m[0][0] + m[0][1] * m[0][1] + m[0][2] * m[0][2] + DILATION
    cross = m[0][0] * m[1][0] + m[0][1] * m[1][1] + m[0][2] * m[1][2]
    lower = m[1][0] * m[1][0] + m[1][1] * m[1][1] + m[1][2] * m[1][2] + DILATION
    inverse = 1.0 / (upper * lower - cross * cross)
    logit = row(9)
    log_opacity = jnp.minimum(logit, 0.0) * LOG2E - LOG2E * jnp.log(1.0 + jnp.exp(-jnp.abs(logit)))
    feat[0:1, :] = linear[0:1, :] + cam(0, 3)
    feat[1:2, :] = linear[1:2, :] + cam(1, 3)
    feat[2:3, :] = lower * inverse * (0.5 * LOG2E)
    feat[3:4, :] = -cross * inverse * LOG2E
    feat[4:5, :] = upper * inverse * (0.5 * LOG2E)
    feat[5:6, :] = log_opacity
    for c in range(3):
        feat[6 + c : 7 + c, :] = linear[2 + c : 3 + c, :] + 0.5

    idx_out[...] = jnp.zeros_like(idx_out)
    for j in range(nd):
        dest = me ^ j
        for i in range(rows):
            size = min(LANES, cap - i * LANES)
            idx_out[j * rows + i : j * rows + i + 1, 0:size] = req_ref[
                0, dest, 0, 0:1, i * LANES : i * LANES + size
            ]
    total = nd * rows
    step = 8 if total % 8 == 0 else total
    source_rows = width // LANES
    for first in range(0, total, step):
        index = idx_out[first : first + step, :]
        low = index & (LANES - 1)
        high = index >> 7
        acc = [jnp.zeros((step, LANES), F32) for _ in range(FEATS)]
        for r in range(source_rows):
            here = high == r
            for f in range(FEATS):
                source = jnp.broadcast_to(feat[f : f + 1, r * LANES : (r + 1) * LANES], (step, LANES))
                acc[f] = jnp.where(here, lane_take(source, low), acc[f])
        for f in range(FEATS):
            for n in range(step):
                j, i = divmod(first + n, rows)
                if rows % step == 0:
                    if n == 0:
                        outs[j][f, i : i + step, :] = acc[f]
                else:
                    outs[j][f, i : i + 1, :] = acc[f][n : n + 1, :]


def vmem_spec():
    return pl.BlockSpec(memory_space=pltpu.VMEM)


def smem_spec():
    return pl.BlockSpec(memory_space=pltpu.SMEM)


def send(me, cameras, basis, params, requests, nd, cap, rows):
    return pl.pallas_call(
        partial(send_kernel, nd=nd, cap=cap, rows=rows),
        in_specs=[smem_spec()] + [vmem_spec()] * 4,
        out_specs=[vmem_spec()] * (nd + 2),
        out_shape=[jax.ShapeDtypeStruct((FEATS, rows, LANES), F32)] * nd
        + [
            jax.ShapeDtypeStruct((nd * rows, LANES), jnp.int32),
            jax.ShapeDtypeStruct((8, LANES), F32),
        ],
        scratch_shapes=[pltpu.VMEM((16, params.shape[1]), F32), pltpu.VMEM((8, LANES), F32)],
        compiler_params=pltpu.CompilerParams(vmem_limit_bytes=40 * 1024 * 1024),
        name="project_gather",
    )(me, cameras, basis, params, requests)


def fold_of(block):
    return 2 if block % 2 == 0 else 1


def fold(row, lane, block):
    wide = fold_of(block)
    height = block // wide
    inside = lax.rem(row, block)
    return lax.div(row, block) * height + lax.rem(inside, height), lax.div(inside, height) * LANES + lane


def place_hot(hot, at, column, wide):
    size = column.shape[0]
    lane = lax.broadcasted_iota(jnp.int32, (size, wide * LANES), 1)
    hot[at : at + size, :] = jnp.where(lane == column, 1.0, 0.0).astype(BF16)


def place_mask(mask, at, row):
    size = row.shape[1]
    high = lax.broadcasted_iota(jnp.int32, (mask.shape[0], size), 0)
    mask[:, at : at + size] = jnp.where(high == row, 1.0, 0.0).astype(BF16)


def place_values(spread, at, mask, values):
    height, size = mask.shape
    for f, pair in enumerate(values):
        for part, row in enumerate(pair):
            base = (part * FEATS + f) * height
            wide_row = jnp.broadcast_to(row, (height, size)).astype(BF16)
            spread[base : base + height, at : at + size] = mask * wide_row


def exact_parts(x):
    hi = x.astype(BF16).astype(F32)
    return hi, (x - hi).astype(BF16).astype(F32)


def take_rows(source, high, low, first_row, count, start):
    acc = list(start)
    for n in range(first_row, first_row + count):
        here = high == n
        for f in range(FEATS):
            value = jnp.broadcast_to(source(f, n), low.shape)
            acc[f] = jnp.where(here, lane_take(value, low), acc[f])
    return acc


def index_kernel(
    me_ref, own_ref, blocks_ref, orders_ref, counts_ref, ids_ref, high_out, low_out, live_out, centre_out, part_out, *, nd, cap
):
    me = me_ref[0]
    rows = own_ref.shape[1]
    tiles, entries = blocks_ref.shape[3:]
    chunk = entries // 8
    halves = entries // LANES

    place = lax.broadcasted_iota(jnp.int32, (tiles, entries), 1)
    rank = (place & 7) * chunk + (place >> 3)

    def take_wide(source, index):
        parts = []
        for c in range(halves):
            wanted = index[:, c * LANES : (c + 1) * LANES]
            low = wanted & (LANES - 1)
            high = wanted >> 7
            value = lane_take(source[:, 0:LANES], low)
            for h in range(1, halves):
                value = jnp.where(high == h, lane_take(source[:, h * LANES : (h + 1) * LANES], low), value)
            parts.append(value)
        return jnp.concatenate(parts, axis=1)

    order = take_wide(orders_ref[0, 0, 0], rank)
    slot = take_wide(blocks_ref[0, 0, 0], order)
    shard = jnp.zeros_like(slot)
    for i in range(1, nd):
        shard = shard + (slot >= i * cap).astype(jnp.int32)
    offset = slot - shard * cap
    slot_row = (shard ^ me) * rows + (offset >> 7)
    slot_lane = offset & (LANES - 1)
    high_out[...] = slot_row
    low_out[...] = slot_lane
    tile_id = column_of(ids_ref, tiles)
    centre_out[0] = jnp.broadcast_to(((tile_id % TW) * SIDE).astype(F32) + 0.5 * SIDE, (tiles, LANES))
    centre_out[1] = jnp.broadcast_to(((tile_id // TW) * SIDE).astype(F32) + 0.5 * SIDE, (tiles, LANES))
    live_out[...] = jnp.where(rank < column_of(counts_ref, tiles), 1.0, 0.0)
    for c in range(halves):
        columns = slice(c * LANES, (c + 1) * LANES)
        for first in range(0, tiles, 8):
            low = slot_lane[first : first + 8, columns]
            high = slot_row[first : first + 8, columns]
            start = [jnp.zeros((8, LANES), F32)] * FEATS
            acc = take_rows(lambda f, n: own_ref[f, n : n + 1, :], high, low, 0, rows, start)
            for f in range(FEATS):
                part_out[f, first : first + 8, columns] = acc[f]


def tile_indices(me, own, blocks, orders, counts, ids, nd, cap):
    rows = own.shape[1]
    tiles, entries = blocks.shape[3:]
    wide = fold_of(rows)
    return pl.pallas_call(
        partial(index_kernel, nd=nd, cap=cap),
        in_specs=[smem_spec()] + [vmem_spec()] * 5,
        out_specs=[vmem_spec()] * 5,
        out_shape=[
            jax.ShapeDtypeStruct((tiles, entries), jnp.int32),
            jax.ShapeDtypeStruct((tiles, entries), jnp.int32),
            jax.ShapeDtypeStruct((tiles, entries), F32),
            jax.ShapeDtypeStruct((2, tiles, LANES), F32),
            jax.ShapeDtypeStruct((FEATS, tiles, entries), F32),
        ],
        compiler_params=pltpu.CompilerParams(vmem_limit_bytes=40 * 1024 * 1024),
        name="prep_tiles",
    )(me, own, blocks, orders, counts, ids)


def gather_kernel(*refs, first_block):
    recv = refs[:-4]
    high_ref, low_ref, part_ref, part_out = refs[-4:]
    rows = recv[0].shape[1]
    tiles, entries = high_ref.shape
    first_row = first_block * rows
    for c in range(entries // LANES):
        columns = slice(c * LANES, (c + 1) * LANES)
        for first in range(0, tiles, 8):
            block = slice(first, first + 8)
            start = [part_ref[f, block, columns] for f in range(FEATS)]

            def source(f, n):
                n = n - first_row
                return recv[n // rows][f, n % rows : n % rows + 1, :]

            acc = take_rows(
                source, high_ref[block, columns], low_ref[block, columns], first_row, len(recv) * rows, start
            )
            for f in range(FEATS):
                part_out[f, block, columns] = acc[f]


def gather_more(received, first_block, high, low, part):
    return pl.pallas_call(
        partial(gather_kernel, first_block=first_block),
        in_specs=[vmem_spec()] * (len(received) + 3),
        out_specs=vmem_spec(),
        out_shape=jax.ShapeDtypeStruct(part.shape, F32),
        compiler_params=pltpu.CompilerParams(vmem_limit_bytes=40 * 1024 * 1024),
        name="prep_gather",
    )(*received, high, low, part)


def column_of(ref, tiles):
    square = jnp.broadcast_to(ref[0, 0].astype(F32), (tiles, tiles))
    diagonal = lax.broadcasted_iota(jnp.int32, (tiles, tiles), 0) == lax.broadcasted_iota(jnp.int32, (tiles, tiles), 1)
    return jnp.sum(jnp.where(diagonal, square, 0.0), axis=1, keepdims=True).astype(jnp.int32)


def render_kernel(*refs, nd, rows, tiles, entries):
    last_ref, high_ref, low_ref, live_ref, centre_ref, part_ref, target_ref = refs[:7]
    outs = refs[7 : nd + 7]
    (images_ref, coef, a_scr, t_scr, q_scr, whi_scr, wlo_scr, ghi_scr, glo_scr, g_rows, mom, spread, mask_ref, hot_ref) = refs[nd + 7 :]
    pixels = SIDE * SIDE
    halves = entries // LANES
    table_rows = nd * rows

    def put(ref, at, value):
        for h in range(halves):
            ref[h, at : at + value.shape[0], :] = value[:, h * LANES : (h + 1) * LANES]

    centre_x = centre_ref[0, :, 0:1]
    centre_y = centre_ref[1, :, 0:1]
    live = live_ref[...] > 0.5

    pieces = [[[] for _ in range(halves)] for _ in range(FEATS)]
    for c in range(halves):
        columns = slice(c * LANES, (c + 1) * LANES)
        for first in range(0, tiles, 8):
            low = low_ref[first : first + 8, columns]
            high = high_ref[first : first + 8, columns]
            start = [part_ref[f, first : first + 8, columns] for f in range(FEATS)]
            acc = take_rows(
                lambda f, n: last_ref[f, n % rows : n % rows + 1, :], high, low, table_rows - rows, rows, start
            )
            for f in range(FEATS):
                pieces[f][c].append(acc[f])
    pieces = [[jnp.concatenate(p, axis=0) for p in both] for both in pieces]
    mean_x, mean_y, con_a, con_b, con_c, log_op, red, green, blue = [jnp.concatenate(p, axis=1) for p in pieces]
    mean_x = mean_x - centre_x
    mean_y = mean_y - centre_y
    bx = con_a * mean_x
    by = con_c * mean_y
    constant = log_op - (bx * mean_x + con_b * mean_x * mean_y + by * mean_y)
    constant = jnp.where(live, constant, DEAD)
    poly = [constant, 2.0 * bx + con_b * mean_y, 2.0 * by + con_b * mean_x, -con_a, -con_b, -con_c]
    for i, value in enumerate(poly):
        rest = value
        for part in range(3):
            piece = rest.astype(BF16).astype(F32)
            rest = rest - piece
            at = (6 * part + i) * tiles
            put(coef, at, piece)
    for i, value in enumerate((red, green, blue)):
        first = value.astype(BF16).astype(F32)
        second = (value - first).astype(BF16).astype(F32)
        for block, piece in enumerate((first, first, second, second)):
            at = (18 + 3 * block + i) * tiles
            put(coef, at, piece)
    coef[:, 30 * tiles : 32 * tiles, :] = jnp.zeros((halves, 2 * tiles, LANES), F32)

    pixel = lax.broadcasted_iota(jnp.int32, (1, pixels), 1)
    px = (pixel & (SIDE - 1)).astype(F32) + (0.5 - 0.5 * SIDE)
    py = (pixel >> 4).astype(F32) + (0.5 - 0.5 * SIDE)
    one = jnp.ones((1, pixels), F32)
    monomials = [one, px, py, px * px, px * py, py * py]
    zero = jnp.zeros((1, pixels), F32)
    basis_scr = g_rows.at[0]
    for part in range(3):
        for i in range(6):
            basis_scr[6 * part + i : 6 * part + i + 1, :] = monomials[i]
    basis_scr[18:32, :] = jnp.zeros((14, pixels), F32)
    basis = basis_scr[...].astype(BF16)
    moment_basis = jnp.concatenate(monomials + [zero, zero], axis=0).astype(BF16)
    g_rows[...] = jnp.zeros_like(g_rows)

    sub_e = lax.broadcasted_iota(jnp.int32, (8, entries), 0)
    own_chunk = jnp.where(sub_e == (lax.broadcasted_iota(jnp.int32, (8, entries), 1) & 7), 1.0, 0.0)
    sub_p = lax.broadcasted_iota(jnp.int32, (8, pixels), 0)

    def down(x, by, fill):
        return jnp.where(sub_p >= by, pltpu.roll(x, by, 0), fill)

    def up(x, by, fill):
        return jnp.where(sub_p < 8 - by, pltpu.roll(x, 8 - by, 0), fill)

    def group(step, carry):
        lanes = range(GROUP)
        ts = [step * GROUP + u for u in lanes]
        tables, lhs = [], []
        for u in lanes:
            table = [coef[h, pl.ds(ts[u], 32, stride=tiles), :] for h in range(halves)]
            tables.append(jnp.concatenate(table, axis=1))
            lhs.append(tables[u].T.astype(BF16))
            a_scr[u] = jnp.exp2(jnp.minimum(dot(lhs[u], basis, 1, 0), 0.0))
        trans = [jnp.ones((8, pixels), F32) for _ in lanes]
        for jj in range(entries // 16):
            for u in lanes:
                w = []
                for h in range(2):
                    at = slice(16 * jj + 8 * h, 16 * jj + 8 * h + 8)
                    t_scr[u, at, :] = trans[u]
                    value = trans[u] * a_scr[u, at, :]
                    trans[u] = trans[u] - value
                    w.append(value)
                at = slice(16 * jj, 16 * jj + 16)
                whi_scr[u, at, :], wlo_scr[u, at, :] = split2(jnp.concatenate(w, axis=0))
        befores, tints, behinds = [], [], []
        for u in lanes:
            table, t = tables[u], ts[u]
            colour = [own_chunk * table[18 + i : 19 + i, :] for i in range(3)]
            colour = colour + [own_chunk * table[24 + i : 25 + i, :] for i in range(3)]
            colour = jnp.concatenate(colour, axis=0).astype(BF16)
            local = dot(colour, whi_scr[u], 1, 0) + dot(colour, wlo_scr[u], 1, 0)
            local = [local[8 * i : 8 * i + 8, :] + local[24 + 8 * i : 32 + 8 * i, :] for i in range(3)]
            before = down(trans[u], 1, 1.0)
            for by in (1, 2, 4):
                before = before * down(before, by, 1.0)
            tinted = []
            inner = jnp.zeros((8, pixels), F32)
            for i in range(3):
                image = jnp.sum(before * local[i], axis=0, keepdims=True)
                images_ref[0, 0, 0, i, pl.ds(t, 1), :] = image
                residual = image - target_ref[0, 0, 0, i, pl.ds(t, 1), :]
                first = residual.astype(BF16).astype(F32)
                second = (residual - first).astype(BF16).astype(F32)
                g_rows[u, 18 + i : 19 + i, :] = first
                g_rows[u, 21 + i : 22 + i, :] = second
                g_rows[u, 24 + i : 25 + i, :] = first
                g_rows[u, 27 + i : 28 + i, :] = second
                tinted.append(before * residual)
                inner = inner + residual * local[i]
            q_scr[u] = dot(lhs[u], g_rows[u].astype(BF16), 1, 0)
            tinted_hi, tinted_lo = split2(jnp.concatenate(tinted, axis=0))
            tints.append(jnp.concatenate([tinted_hi.astype(F32), tinted_lo.astype(F32)], axis=0).astype(BF16))
            add = up(inner, 1, 0.0)
            scale = up(trans[u], 1, 0.0)
            for by in (1, 2, 4):
                add = add + scale * up(add, by, 0.0)
                scale = scale * up(scale, by, 0.0)
            behinds.append(add)
            befores.append(before)
        rows_out = []
        for u in lanes:
            colour_grad = dot(tints[u], whi_scr[u], 1, 1) + dot(tints[u], wlo_scr[u], 1, 1)
            for i in range(3):
                both = colour_grad[8 * i : 8 * i + 8, :] + colour_grad[24 + 8 * i : 32 + 8 * i, :]
                rows_out.append(jnp.sum(own_chunk * both, axis=0, keepdims=True))
        for jj in reversed(range(entries // 16)):
            for u in lanes:
                g = [None, None]
                for h in (1, 0):
                    at = slice(16 * jj + 8 * h, 16 * jj + 8 * h + 8)
                    moved = a_scr[u, at, :] * (q_scr[u, at, :] - behinds[u])
                    behinds[u] = behinds[u] + moved
                    g[h] = (t_scr[u, at, :] * befores[u]) * moved
                at = slice(16 * jj, 16 * jj + 16)
                ghi_scr[u, at, :], glo_scr[u, at, :] = split2(jnp.concatenate(g, axis=0))
        for u in lanes:
            moments = dot(moment_basis, ghi_scr[u], 1, 1) + dot(moment_basis, glo_scr[u], 1, 1)
            for h in range(halves):
                columns = slice(h * LANES, (h + 1) * LANES)
                mom[h, pl.ds(ts[u], 8, stride=tiles), :] = moments[:, columns]
                for i in range(3):
                    mom[h, pl.ds((8 + i) * tiles + ts[u], 1), :] = rows_out[3 * u + i][:, columns]
        return carry

    if tiles == GROUP:
        group(0, 0)
    else:
        lax.fori_loop(0, tiles // GROUP, group, 0)

    def got(i):
        return jnp.concatenate([mom[h, i * tiles : (i + 1) * tiles, :] for h in range(halves)], axis=1)

    m0, m1, m2, m3, m4, m5 = [got(i) for i in range(6)]
    su = m1 - mean_x * m0
    sv = m2 - mean_y * m0
    suu = m3 - mean_x * (m1 + su)
    suv = m4 - mean_x * m2 - mean_y * su
    svv = m5 - mean_y * (m2 + sv)
    grads = [
        LN2 * (2.0 * con_a * su + con_b * sv),
        LN2 * (con_b * su + 2.0 * con_c * sv),
        -0.5 * suu,
        -suv,
        -0.5 * svv,
        m0,
    ] + [got(8 + i) for i in range(3)]
    key_high, key_low = fold(high_ref[...], low_ref[...], rows)
    key_columns = key_low.astype(F32).T.astype(jnp.int32)
    for t in range(tiles):
        place_mask(mask_ref, t * entries, key_high[t : t + 1, :])
        place_hot(hot_ref, t * entries, key_columns[:, t : t + 1], fold_of(rows))
    parts = [exact_parts(g) for g in grads]
    for t in range(tiles):
        at = t * entries
        values = [[x[t : t + 1, :] for x in pair] for pair in parts]
        place_values(spread, at, mask_ref[:, at : at + entries], values)
    summed = dot(spread[...], hot_ref[...], 1, 0)
    wide = fold_of(rows)
    height = rows // wide
    total = table_rows // wide
    for f in range(FEATS):
        both = summed[f * total : (f + 1) * total, :] + summed[(FEATS + f) * total : (FEATS + f + 1) * total, :]
        for j in range(nd):
            for h in range(wide):
                outs[j][f, h * height : (h + 1) * height, :] = both[
                    j * height : (j + 1) * height, h * LANES : (h + 1) * LANES
                ]


def render(last, prepared, target, nd, rows, tiles, entries):
    pixels = SIDE * SIDE
    return pl.pallas_call(
        partial(render_kernel, nd=nd, rows=rows, tiles=tiles, entries=entries),
        in_specs=[vmem_spec()] * 7,
        out_specs=[vmem_spec()] * (nd + 1),
        out_shape=[jax.ShapeDtypeStruct((FEATS, rows, LANES), F32)] * nd
        + [jax.ShapeDtypeStruct(target.shape, F32)],
        scratch_shapes=[
            pltpu.VMEM((entries // LANES, 32 * tiles, LANES), F32),
            pltpu.VMEM((GROUP, entries, pixels), F32),
            pltpu.VMEM((GROUP, entries, pixels), F32),
            pltpu.VMEM((GROUP, entries, pixels), F32),
            pltpu.VMEM((GROUP, entries, pixels), BF16),
            pltpu.VMEM((GROUP, entries, pixels), BF16),
            pltpu.VMEM((GROUP, entries, pixels), BF16),
            pltpu.VMEM((GROUP, entries, pixels), BF16),
            pltpu.VMEM((GROUP, 32, pixels), F32),
            pltpu.VMEM((entries // LANES, 11 * tiles, LANES), F32),
            pltpu.VMEM((2 * FEATS * nd * rows // fold_of(rows), tiles * entries), BF16),
            pltpu.VMEM((nd * rows // fold_of(rows), tiles * entries), BF16),
            pltpu.VMEM((tiles * entries, fold_of(rows) * LANES), BF16),
        ],
        compiler_params=pltpu.CompilerParams(vmem_limit_bytes=48 * 1024 * 1024),
        name="render_tiles",
    )(last, *prepared, target)


def owner_index_kernel(own_ref, next_ref, idx_ref, mask_out, hot_low, hot_high, sum_out, spread, *, share):
    middle = idx_ref.shape[0] // 2
    rows = own_ref.shape[1]
    index = idx_ref[...]
    key_high, key_low = fold(index >> 7, index & (LANES - 1), share)
    key_columns = key_low.astype(F32).T.astype(jnp.int32)
    wide = fold_of(share)
    for n in range(idx_ref.shape[0]):
        place_mask(mask_out, n * LANES, key_high[n : n + 1, :])
        place_hot(hot_low if n < middle else hot_high, n % middle * LANES, key_columns[:, n : n + 1], wide)
    for j, ref in enumerate((own_ref, next_ref)):
        parts = [exact_parts(ref[f]) for f in range(FEATS)]
        for i in range(rows):
            at = (j * rows + i) * LANES
            values = [[x[i : i + 1, :] for x in pair] for pair in parts]
            place_values(spread, at, mask_out[:, at : at + LANES], values)
    sum_out[...] = dot(spread[...], hot_low[0 : 2 * rows * LANES, :], 1, 0)


def owner_indices(own, following, index, share, width):
    rows = own.shape[1]
    wide = fold_of(share)
    height = width // LANES // wide
    slots = index.shape[0] * LANES
    return pl.pallas_call(
        partial(owner_index_kernel, share=share),
        in_specs=[vmem_spec()] * 3,
        out_specs=[vmem_spec()] * 4,
        out_shape=[
            jax.ShapeDtypeStruct((height, slots), BF16),
            jax.ShapeDtypeStruct((slots // 2, wide * LANES), BF16),
            jax.ShapeDtypeStruct((slots // 2, wide * LANES), BF16),
            jax.ShapeDtypeStruct((2 * FEATS * height, wide * LANES), F32),
        ],
        scratch_shapes=[pltpu.VMEM((2 * FEATS * height, 2 * rows * LANES), BF16)],
        compiler_params=pltpu.CompilerParams(vmem_limit_bytes=40 * 1024 * 1024),
        name="prep_owner",
    )(own, following, index)


def owner_kernel(me_ref, *refs, nd, rows, parts, nv, nc, share):
    recv = refs[: nd - 2]
    mask_ref, hot_low, hot_high, sum_ref, w_ref = refs[nd - 2 : nd + 3]
    outs = refs[nd + 3 : nd + 3 + parts]
    spread, summed = refs[nd + 3 + parts :]
    my_view = me_ref[1]
    my_chip = me_ref[2]
    skip = 2 * rows * LANES
    for j in range(nd - 2):
        pairs = [exact_parts(recv[j][f]) for f in range(FEATS)]
        for i in range(rows):
            at = (j * rows + i) * LANES
            values = [[x[i : i + 1, :] for x in pair] for pair in pairs]
            place_values(spread, at, mask_ref[:, skip + at : skip + at + LANES], values)
    middle = hot_low.shape[0] - skip
    result = sum_ref[...] + dot(spread[:, middle:], hot_high[...], 1, 0)
    if middle > 0:
        result = result + dot(spread[:, 0:middle], hot_low[skip:, :], 1, 0)
    wide = fold_of(share)
    height = share // wide
    total = parts * height
    for f in range(FEATS):
        both = result[f * total : (f + 1) * total, :] + result[(FEATS + f) * total : (FEATS + f + 1) * total, :]
        for p in range(parts):
            for h in range(wide):
                summed[p, f, h * height : (h + 1) * height, :] = both[
                    p * height : (p + 1) * height, h * LANES : (h + 1) * LANES
                ]
    for p in range(parts):
        summed[p, FEATS] = w_ref[0:share, :]
    for dv in range(nv):
        for dc in range(nc):
            where = lax.rem(my_view + dv, nv) * nc + lax.rem(my_chip + dc, nc)
            outs[dv * nc + dc][...] = summed[where]


def owner_sums(me, received, prepared, weights, nd, rows, nv, nc, share):
    parts = nv * nc
    height, slots = prepared[0].shape
    return pl.pallas_call(
        partial(owner_kernel, nd=nd, rows=rows, parts=parts, nv=nv, nc=nc, share=share),
        in_specs=[smem_spec()] + [vmem_spec()] * (nd + 3),
        out_specs=[vmem_spec()] * parts,
        out_shape=[jax.ShapeDtypeStruct((FEATS + 1, share, LANES), F32)] * parts,
        scratch_shapes=[
            pltpu.VMEM((2 * FEATS * height, slots - 2 * rows * LANES), BF16),
            pltpu.VMEM((parts, FEATS + 1, share, LANES), F32),
        ],
        compiler_params=pltpu.CompilerParams(vmem_limit_bytes=40 * 1024 * 1024),
        name="owner_sums",
    )(me, *received, *prepared, weights)


def pullback_kernel(at_ref, params_ref, *refs, nv, nc, coefs):
    recv = refs[: nv * nc]
    out_ref, flat = refs[nv * nc :]
    share = recv[0].shape[1]
    columns = share * LANES

    def row(i):
        return params_ref[i : i + 1, :]

    lx, lyx, ly, lzx, lzy, lz = [row(i) for i in range(3, 9)]
    total = [jnp.zeros((1, columns), F32) for _ in range(10)]
    harmonics = [jnp.zeros((coefs, columns), F32) for _ in range(3)]
    square = lax.broadcasted_iota(jnp.int32, (coefs, LANES), 1) == lax.broadcasted_iota(
        jnp.int32, (coefs, LANES), 0
    ) + 10
    for v in range(nv):
        packed = recv[v * nc][FEATS]
        for i in range(share):
            block = recv[v * nc][0:FEATS, i, :]
            for c in range(1, nc):
                block = block + recv[v * nc + c][0:FEATS, i, :]
            flat[0:FEATS, i * LANES : (i + 1) * LANES] = block
        gx, gy, g0, g1, g2, gh, gr, gg, gb = [flat[f : f + 1, :] for f in range(FEATS)]
        cam = [[packed[i : i + 1, j : j + 1] for j in range(3)] for i in range(2)]
        for j in range(3):
            total[j] = total[j] + cam[0][j] * gx + cam[1][j] * gy
        m = []
        for i in range(2):
            a0, a1, a2 = cam[i]
            m.append((a0 * lx + a1 * lyx + a2 * lzx, a1 * ly + a2 * lzy, a2 * lz))
        upper = m[0][0] * m[0][0] + m[0][1] * m[0][1] + m[0][2] * m[0][2] + DILATION
        cross = m[0][0] * m[1][0] + m[0][1] * m[1][1] + m[0][2] * m[1][2]
        lower = m[1][0] * m[1][0] + m[1][1] * m[1][1] + m[1][2] * m[1][2] + DILATION
        inverse = 1.0 / (upper * lower - cross * cross)
        c0, c1, c2 = lower * inverse, -cross * inverse, upper * inverse
        h1 = 0.5 * g1
        k00, k01 = g0 * c0 + h1 * c1, g0 * c1 + h1 * c2
        k10, k11 = h1 * c0 + g2 * c1, h1 * c1 + g2 * c2
        s00 = -(c0 * k00 + c1 * k10)
        s01 = -(c0 * k01 + c1 * k11)
        s11 = -(c1 * k01 + c2 * k11)
        gm = [[2.0 * (s00 * m[0][k] + s01 * m[1][k]) for k in range(3)]]
        gm.append([2.0 * (s01 * m[0][k] + s11 * m[1][k]) for k in range(3)])
        at = 3
        for i in range(3):
            for k in range(i + 1):
                total[at] = total[at] + cam[0][i] * gm[0][k] + cam[1][i] * gm[1][k]
                at += 1
        total[9] = total[9] + gh
        basis = jnp.sum(jnp.where(square, packed[0:1, :], 0.0), axis=1, keepdims=True)
        for c, g in enumerate((gr, gg, gb)):
            harmonics[c] = harmonics[c] + basis * g
    logit = row(9)
    total[9] = total[9] / (1.0 + jnp.exp(logit))
    for i in range(10):
        out_ref[i : i + 1, :] = total[i]
    for c in range(3):
        out_ref[10 + c * coefs : 10 + (c + 1) * coefs, :] = harmonics[c]


def pull_back(at, params, received, nv, nc, coefs):
    parts = nv * nc
    columns = params.shape[1] // parts
    block = received[0].shape
    return pl.pallas_call(
        partial(pullback_kernel, nv=nv, nc=nc, coefs=coefs),
        grid_spec=pltpu.PrefetchScalarGridSpec(
            num_scalar_prefetch=1,
            grid=(1,),
            in_specs=[pl.BlockSpec((params.shape[0], columns), lambda i, at_ref: (0, at_ref[0]))]
            + [pl.BlockSpec(block, lambda i, at_ref: (0, 0, 0))] * parts,
            out_specs=pl.BlockSpec((params.shape[0], columns), lambda i, at_ref: (0, 0)),
            scratch_shapes=[pltpu.VMEM((16, columns), F32)],
        ),
        out_shape=jax.ShapeDtypeStruct((params.shape[0], columns), F32),
        compiler_params=pltpu.CompilerParams(vmem_limit_bytes=40 * 1024 * 1024),
        name="pull_back",
    )(at, params, *received)


def hop_order(nd, first):
    return [j for j in first if j < nd] + [j for j in range(1, nd) if j not in first]


def local(
    params,
    cameras,
    view_basis,
    tile_lists,
    margin_blocks,
    depth_orders,
    tile_counts,
    requests,
    target,
    *,
    nd,
    nv,
    nc,
):
    cap = requests.shape[4]
    rows = -(-cap // LANES)
    my_view = lax.axis_index("view")
    my_chip = lax.axis_index("chip")
    me = jnp.stack([lax.axis_index("dev"), my_view, my_chip]).astype(jnp.int32)
    at = (my_view * nc + my_chip).astype(jnp.int32).reshape(1)

    *packets, index, weights = send(me, cameras, view_basis, params, requests, nd, cap, rows)
    received = list(packets)
    for j in hop_order(nd, FORTH):
        received[j] = lax.ppermute(packets[j], "dev", [(i, i ^ j) for i in range(nd)])
    prepared = tile_indices(
        me, packets[0], margin_blocks, depth_orders, tile_counts, tile_lists, nd, cap
    )
    tiles, entries = margin_blocks.shape[3:]
    swapped = jnp.swapaxes(target, 3, 4)
    *prepared, part = prepared
    part = gather_more(received[1 : nd - 1], 1, prepared[0], prepared[1], part)
    *returns, images = render(received[nd - 1], (*prepared, part), swapped, nd, rows, tiles, entries)
    back = list(returns)
    for j in hop_order(nd, BACK):
        back[j] = lax.ppermute(returns[j], "dev", [(i, i ^ j) for i in range(nd)])
    share = params.shape[1] // LANES // (nv * nc)
    sorted_own = owner_indices(returns[0], back[1], index, share, params.shape[1])
    shares = owner_sums(me, back[2:], sorted_own, weights, nd, rows, nv, nc, share)
    arrived = []
    for dv in range(nv):
        for dc in range(nc):
            pairs = [
                (v * nc + c, (v + dv) % nv * nc + (c + dc) % nc) for v in range(nv) for c in range(nc)
            ]
            piece = shares[dv * nc + dc]
            arrived.append(piece if dv + dc == 0 else lax.ppermute(piece, ("view", "chip"), pairs))
    grads = pull_back(at, params, arrived, nv, nc, view_basis.shape[1])
    return (grads, jnp.swapaxes(images, 3, 4))


def solution(mesh):
    return jax.shard_map(
        partial(local, nd=mesh.shape["dev"], nv=mesh.shape["view"], nc=mesh.shape["chip"]),
        mesh=mesh,
        in_specs=(
            P(None, ("groups", "dev")),
            P(("groups", "view"), None, None),
            P(("groups", "view"), None),
            P("view", ("groups", "dev"), "chip", None),
            P("view", ("groups", "dev"), "chip", None, None),
            P("view", ("groups", "dev"), "chip", None, None),
            P("view", ("groups", "dev"), "chip", None),
            P("view", None, "chip", ("groups", "dev"), None),
            P("view", ("groups", "dev"), "chip", None, None, None),
        ),
        out_specs=(
            P(None, ("groups", "dev", "view", "chip")),
            P("view", ("groups", "dev"), "chip", None, None, None),
        ),
        check_vma=False,
    )
```

```python
from functools import partial

import jax
import jax.numpy as jnp
from jax import lax
from jax.experimental import pallas as pl
from jax.experimental.pallas import tpu as pltpu
from jax.sharding import PartitionSpec as P

SIDE = 16
TW = 16
LANES = 128
LOG2E = 1.4426950408889634
LN2 = 0.6931471805599453
DILATION = 0.3
DEAD = -1e30
F32 = jnp.float32
BF16 = jnp.bfloat16
FEATS = 9
FORTH = (1, 2, 3)
BACK = (1, 2, 3)
GROUP = 8


def lane_take(row, index):
    return jnp.take_along_axis(row, index, axis=1, mode="promise_in_bounds")


def split2(x):
    hi = x.astype(BF16)
    return hi, (x - hi.astype(F32)).astype(BF16)


def dot(a, b, ca, cb):
    return lax.dot_general(a, b, (((ca,), (cb,)), ((), ())), preferred_element_type=F32)


def send_kernel(me_ref, cam_ref, basis_ref, params_ref, req_ref, *refs, nd, cap, rows):
    outs = refs[: nd - 1]
    idx_out, w_out, feat, w_scr = refs[nd - 1 :]
    me = me_ref[0]
    width = params_ref.shape[1]
    coefs = basis_ref.shape[-1]
    w_scr[...] = jnp.zeros_like(w_scr)
    w_scr[0:2, 0:4] = cam_ref[0]
    w_scr[2:3, 0:coefs] = basis_ref[...]
    packed = w_scr[...]
    lane8 = lax.broadcasted_iota(jnp.int32, (8, LANES), 1)
    row8 = lax.broadcasted_iota(jnp.int32, (8, LANES), 0)
    basis_row = jnp.broadcast_to(packed[2:3, :], (8, LANES))
    camera_row = jnp.where((row8 < 2), packed, 0.0)
    at10 = pltpu.roll(basis_row, 10, 1)
    w_out[...] = camera_row + jnp.where(row8 == 0, at10, 0.0)
    weights = jnp.where(lane8 < 3, camera_row, 0.0)
    weights = weights + jnp.where(row8 == 2, at10, 0.0)
    weights = weights + jnp.where(row8 == 3, pltpu.roll(basis_row, 10 + coefs, 1), 0.0)
    weights = weights + jnp.where(row8 == 4, pltpu.roll(basis_row, 10 + 2 * coefs, 1), 0.0)
    columns = weights.T
    last = params_ref.shape[0]

    def weighted(c, low, high):
        first, end = low // 8 * 8, min(-(-high // 8) * 8, last)
        return jnp.sum(params_ref[first:end, :] * columns[first:end, c : c + 1], axis=0, keepdims=True)

    linear = [weighted(0, 0, 3), weighted(1, 0, 3)]
    for c in range(3):
        linear.append(weighted(2 + c, 10 + c * coefs, 10 + (c + 1) * coefs))

    def cam(i, j):
        return cam_ref[0, i : i + 1, j : j + 1]

    def row(i):
        return params_ref[i : i + 1, :]

    lx, lyx, ly, lzx, lzy, lz = [row(i) for i in range(3, 9)]
    m = []
    for i in range(2):
        a0, a1, a2 = cam(i, 0), cam(i, 1), cam(i, 2)
        m.append((a0 * lx + a1 * lyx + a2 * lzx, a1 * ly + a2 * lzy, a2 * lz))
    upper = m[0][0] * m[0][0] + m[0][1] * m[0][1] + m[0][2] * m[0][2] + DILATION
    cross = m[0][0] * m[1][0] + m[0][1] * m[1][1] + m[0][2] * m[1][2]
    lower = m[1][0] * m[1][0] + m[1][1] * m[1][1] + m[1][2] * m[1][2] + DILATION
    inverse = 1.0 / (upper * lower - cross * cross)
    logit = row(9)
    log_opacity = jnp.minimum(logit, 0.0) * LOG2E - LOG2E * jnp.log(1.0 + jnp.exp(-jnp.abs(logit)))
    feat[0:1, :] = linear[0] + cam(0, 3)
    feat[1:2, :] = linear[1] + cam(1, 3)
    feat[2:3, :] = lower * inverse * (0.5 * LOG2E)
    feat[3:4, :] = -cross * inverse * LOG2E
    feat[4:5, :] = upper * inverse * (0.5 * LOG2E)
    feat[5:6, :] = log_opacity
    for c in range(3):
        feat[6 + c : 7 + c, :] = linear[2 + c] + 0.5

    idx_out[...] = jnp.zeros_like(idx_out)
    for j in range(nd):
        dest = me ^ j
        for i in range(rows):
            size = min(LANES, cap - i * LANES)
            idx_out[j * rows + i : j * rows + i + 1, 0:size] = req_ref[
                0, dest, 0, 0:1, i * LANES : i * LANES + size
            ]
    total = nd * rows
    step = 8 if rows % 8 == 0 else total - rows
    for first in range(rows, total, step):
        gathered = gather_features(feat, idx_out[first : first + step, :])
        for f in range(FEATS):
            for n in range(0, step, rows if step > rows else step):
                j, i = divmod(first + n, rows)
                size = min(rows, step)
                outs[j - 1][f, i : i + size, :] = gathered[f][n : n + size, :]


def gather_features(feat, index):
    low = index & (LANES - 1)
    high = index >> 7
    acc = [jnp.zeros(index.shape, F32) for _ in range(FEATS)]
    for r in range(feat.shape[1] // LANES):
        here = high == r
        for f in range(FEATS):
            source = jnp.broadcast_to(feat[f : f + 1, r * LANES : (r + 1) * LANES], index.shape)
            acc[f] = jnp.where(here, lane_take(source, low), acc[f])
    return acc


def vmem_spec():
    return pl.BlockSpec(memory_space=pltpu.VMEM)


def smem_spec():
    return pl.BlockSpec(memory_space=pltpu.SMEM)


def send(me, cameras, basis, params, requests, nd, cap, rows):
    return pl.pallas_call(
        partial(send_kernel, nd=nd, cap=cap, rows=rows),
        in_specs=[smem_spec()] + [vmem_spec()] * 4,
        out_specs=[vmem_spec()] * (nd + 2),
        out_shape=[jax.ShapeDtypeStruct((FEATS, rows, LANES), F32)] * (nd - 1)
        + [
            jax.ShapeDtypeStruct((nd * rows, LANES), jnp.int32),
            jax.ShapeDtypeStruct((8, LANES), F32),
            jax.ShapeDtypeStruct((16, params.shape[1]), F32),
        ],
        scratch_shapes=[pltpu.VMEM((8, LANES), F32)],
        compiler_params=pltpu.CompilerParams(vmem_limit_bytes=40 * 1024 * 1024),
        name="project_gather",
    )(me, cameras, basis, params, requests)


def fold_of(block):
    return 2 if block % 2 == 0 else 1


def fold(row, lane, block):
    wide = fold_of(block)
    height = block // wide
    inside = lax.rem(row, block)
    return lax.div(row, block) * height + lax.rem(inside, height), lax.div(inside, height) * LANES + lane


def place_hot(hot, at, column, wide):
    size = column.shape[0]
    lane = lax.broadcasted_iota(jnp.int32, (size, wide * LANES), 1)
    hot[at : at + size, :] = jnp.where(lane == column, 1.0, 0.0).astype(BF16)


def place_mask(mask, at, row):
    size = row.shape[1]
    high = lax.broadcasted_iota(jnp.int32, (mask.shape[0], size), 0)
    mask[:, at : at + size] = jnp.where(high == row, 1.0, 0.0).astype(BF16)


def place_values(spread, at, mask, values):
    height, size = mask.shape
    for f, pair in enumerate(values):
        for part, row in enumerate(pair):
            base = (part * FEATS + f) * height
            wide_row = jnp.broadcast_to(row, (height, size)).astype(BF16)
            spread[base : base + height, at : at + size] = mask * wide_row


def exact_parts(x):
    hi = x.astype(BF16).astype(F32)
    return hi, (x - hi).astype(BF16).astype(F32)


def take_rows(source, high, low, first_row, count, start):
    acc = list(start)
    for n in range(first_row, first_row + count):
        here = high == n
        for f in range(FEATS):
            value = jnp.broadcast_to(source(f, n), low.shape)
            acc[f] = jnp.where(here, lane_take(value, low), acc[f])
    return acc


def index_kernel(
    me_ref, feat_ref, idx_ref, blocks_ref, orders_ref, counts_ref, ids_ref, high_out, low_out, live_out, centre_out, part_out, own_ref, *, nd, cap
):
    me = me_ref[0]
    rows = own_ref.shape[1]
    own = gather_features(feat_ref, idx_ref[0 : max(rows, 8), :])
    for f in range(FEATS):
        own_ref[f] = own[f][0:rows, :]
    tiles, entries = blocks_ref.shape[3:]
    chunk = entries // 8
    halves = entries // LANES

    place = lax.broadcasted_iota(jnp.int32, (tiles, entries), 1)
    rank = (place & 7) * chunk + (place >> 3)

    def take_wide(source, index):
        parts = []
        for c in range(halves):
            wanted = index[:, c * LANES : (c + 1) * LANES]
            low = wanted & (LANES - 1)
            high = wanted >> 7
            value = lane_take(source[:, 0:LANES], low)
            for h in range(1, halves):
                value = jnp.where(high == h, lane_take(source[:, h * LANES : (h + 1) * LANES], low), value)
            parts.append(value)
        return jnp.concatenate(parts, axis=1)

    order = take_wide(orders_ref[0, 0, 0], rank)
    slot = take_wide(blocks_ref[0, 0, 0], order)
    shard = jnp.zeros_like(slot)
    for i in range(1, nd):
        shard = shard + (slot >= i * cap).astype(jnp.int32)
    offset = slot - shard * cap
    slot_row = (shard ^ me) * rows + (offset >> 7)
    slot_lane = offset & (LANES - 1)
    high_out[...] = slot_row
    low_out[...] = slot_lane
    tile_id = column_of(ids_ref, tiles)
    centre_out[0] = jnp.broadcast_to(((tile_id % TW) * SIDE).astype(F32) + 0.5 * SIDE, (tiles, LANES))
    centre_out[1] = jnp.broadcast_to(((tile_id // TW) * SIDE).astype(F32) + 0.5 * SIDE, (tiles, LANES))
    live_out[...] = jnp.where(rank < column_of(counts_ref, tiles), 1.0, 0.0)
    for c in range(halves):
        columns = slice(c * LANES, (c + 1) * LANES)
        for first in range(0, tiles, 8):
            low = slot_lane[first : first + 8, columns]
            high = slot_row[first : first + 8, columns]
            start = [jnp.zeros((8, LANES), F32)] * FEATS
            acc = take_rows(lambda f, n: own_ref[f, n : n + 1, :], high, low, 0, rows, start)
            for f in range(FEATS):
                part_out[f, first : first + 8, columns] = acc[f]


def tile_indices(me, features, index, blocks, orders, counts, ids, nd, cap):
    rows = index.shape[0] // nd
    tiles, entries = blocks.shape[3:]
    wide = fold_of(rows)
    return pl.pallas_call(
        partial(index_kernel, nd=nd, cap=cap),
        in_specs=[smem_spec()] + [vmem_spec()] * 6,
        out_specs=[vmem_spec()] * 5,
        out_shape=[
            jax.ShapeDtypeStruct((tiles, entries), jnp.int32),
            jax.ShapeDtypeStruct((tiles, entries), jnp.int32),
            jax.ShapeDtypeStruct((tiles, entries), F32),
            jax.ShapeDtypeStruct((2, tiles, LANES), F32),
            jax.ShapeDtypeStruct((FEATS, tiles, entries), F32),
        ],
        scratch_shapes=[pltpu.VMEM((FEATS, rows, LANES), F32)],
        compiler_params=pltpu.CompilerParams(vmem_limit_bytes=40 * 1024 * 1024),
        name="prep_tiles",
    )(me, features, index, blocks, orders, counts, ids)


def gather_kernel(*refs, first_block):
    recv = refs[:-4]
    high_ref, low_ref, part_ref, part_out = refs[-4:]
    rows = recv[0].shape[1]
    tiles, entries = high_ref.shape
    first_row = first_block * rows
    for c in range(entries // LANES):
        columns = slice(c * LANES, (c + 1) * LANES)
        for first in range(0, tiles, 8):
            block = slice(first, first + 8)
            start = [part_ref[f, block, columns] for f in range(FEATS)]

            def source(f, n):
                n = n - first_row
                return recv[n // rows][f, n % rows : n % rows + 1, :]

            acc = take_rows(
                source, high_ref[block, columns], low_ref[block, columns], first_row, len(recv) * rows, start
            )
            for f in range(FEATS):
                part_out[f, block, columns] = acc[f]


def gather_more(received, first_block, high, low, part):
    return pl.pallas_call(
        partial(gather_kernel, first_block=first_block),
        in_specs=[vmem_spec()] * (len(received) + 3),
        out_specs=vmem_spec(),
        out_shape=jax.ShapeDtypeStruct(part.shape, F32),
        compiler_params=pltpu.CompilerParams(vmem_limit_bytes=40 * 1024 * 1024),
        name="prep_gather",
    )(*received, high, low, part)


def column_of(ref, tiles):
    square = jnp.broadcast_to(ref[0, 0].astype(F32), (tiles, tiles))
    diagonal = lax.broadcasted_iota(jnp.int32, (tiles, tiles), 0) == lax.broadcasted_iota(jnp.int32, (tiles, tiles), 1)
    return jnp.sum(jnp.where(diagonal, square, 0.0), axis=1, keepdims=True).astype(jnp.int32)


def render_kernel(*refs, nd, rows, tiles, entries):
    last_ref, high_ref, low_ref, live_ref, centre_ref, part_ref, target_ref = refs[:7]
    outs = refs[7 : nd + 7]
    (images_ref, coef, a_scr, t_scr, q_scr, whi_scr, wlo_scr, ghi_scr, glo_scr, g_rows, mom, spread, mask_ref, hot_ref) = refs[nd + 7 :]
    pixels = SIDE * SIDE
    halves = entries // LANES
    table_rows = nd * rows

    def put(ref, at, value):
        for h in range(halves):
            ref[h, at : at + value.shape[0], :] = value[:, h * LANES : (h + 1) * LANES]

    centre_x = centre_ref[0, :, 0:1]
    centre_y = centre_ref[1, :, 0:1]
    live = live_ref[...] > 0.5

    pieces = [[[] for _ in range(halves)] for _ in range(FEATS)]
    for c in range(halves):
        columns = slice(c * LANES, (c + 1) * LANES)
        for first in range(0, tiles, 8):
            low = low_ref[first : first + 8, columns]
            high = high_ref[first : first + 8, columns]
            start = [part_ref[f, first : first + 8, columns] for f in range(FEATS)]
            acc = take_rows(
                lambda f, n: last_ref[f, n % rows : n % rows + 1, :], high, low, table_rows - rows, rows, start
            )
            for f in range(FEATS):
                pieces[f][c].append(acc[f])
    pieces = [[jnp.concatenate(p, axis=0) for p in both] for both in pieces]
    mean_x, mean_y, con_a, con_b, con_c, log_op, red, green, blue = [jnp.concatenate(p, axis=1) for p in pieces]
    mean_x = mean_x - centre_x
    mean_y = mean_y - centre_y
    bx = con_a * mean_x
    by = con_c * mean_y
    constant = log_op - (bx * mean_x + con_b * mean_x * mean_y + by * mean_y)
    constant = jnp.where(live, constant, DEAD)
    poly = [constant, 2.0 * bx + con_b * mean_y, 2.0 * by + con_b * mean_x, -con_a, -con_b, -con_c]
    for i, value in enumerate(poly):
        rest = value
        for part in range(3):
            piece = rest.astype(BF16).astype(F32)
            rest = rest - piece
            at = (6 * part + i) * tiles
            put(coef, at, piece)
    for i, value in enumerate((red, green, blue)):
        first = value.astype(BF16).astype(F32)
        second = (value - first).astype(BF16).astype(F32)
        for block, piece in enumerate((first, first, second, second)):
            at = (18 + 3 * block + i) * tiles
            put(coef, at, piece)
    coef[:, 30 * tiles : 32 * tiles, :] = jnp.zeros((halves, 2 * tiles, LANES), F32)

    pixel = lax.broadcasted_iota(jnp.int32, (1, pixels), 1)
    px = (pixel & (SIDE - 1)).astype(F32) + (0.5 - 0.5 * SIDE)
    py = (pixel >> 4).astype(F32) + (0.5 - 0.5 * SIDE)
    one = jnp.ones((1, pixels), F32)
    monomials = [one, px, py, px * px, px * py, py * py]
    zero = jnp.zeros((1, pixels), F32)
    basis_scr = g_rows.at[0]
    for part in range(3):
        for i in range(6):
            basis_scr[6 * part + i : 6 * part + i + 1, :] = monomials[i]
    basis_scr[18:32, :] = jnp.zeros((14, pixels), F32)
    basis = basis_scr[...].astype(BF16)
    moment_basis = jnp.concatenate(monomials + [zero, zero], axis=0).astype(BF16)
    g_rows[...] = jnp.zeros_like(g_rows)

    sub_e = lax.broadcasted_iota(jnp.int32, (8, entries), 0)
    own_chunk = jnp.where(sub_e == (lax.broadcasted_iota(jnp.int32, (8, entries), 1) & 7), 1.0, 0.0)
    sub_p = lax.broadcasted_iota(jnp.int32, (8, pixels), 0)

    def down(x, by, fill):
        return jnp.where(sub_p >= by, pltpu.roll(x, by, 0), fill)

    def up(x, by, fill):
        return jnp.where(sub_p < 8 - by, pltpu.roll(x, 8 - by, 0), fill)

    def group(step, carry):
        lanes = range(GROUP)
        ts = [step * GROUP + u for u in lanes]
        tables, lhs = [], []
        for u in lanes:
            table = [coef[h, pl.ds(ts[u], 32, stride=tiles), :] for h in range(halves)]
            tables.append(jnp.concatenate(table, axis=1))
            lhs.append(tables[u].T.astype(BF16))
            a_scr[u] = jnp.exp2(jnp.minimum(dot(lhs[u], basis, 1, 0), 0.0))
        trans = [jnp.ones((8, pixels), F32) for _ in lanes]
        for jj in range(entries // 16):
            for u in lanes:
                w = []
                for h in range(2):
                    at = slice(16 * jj + 8 * h, 16 * jj + 8 * h + 8)
                    t_scr[u, at, :] = trans[u]
                    value = trans[u] * a_scr[u, at, :]
                    trans[u] = trans[u] - value
                    w.append(value)
                at = slice(16 * jj, 16 * jj + 16)
                whi_scr[u, at, :], wlo_scr[u, at, :] = split2(jnp.concatenate(w, axis=0))
        befores, tints, behinds = [], [], []
        for u in lanes:
            table, t = tables[u], ts[u]
            colour = [own_chunk * table[18 + i : 19 + i, :] for i in range(3)]
            colour = colour + [own_chunk * table[24 + i : 25 + i, :] for i in range(3)]
            colour = jnp.concatenate(colour, axis=0).astype(BF16)
            local = dot(colour, whi_scr[u], 1, 0) + dot(colour, wlo_scr[u], 1, 0)
            local = [local[8 * i : 8 * i + 8, :] + local[24 + 8 * i : 32 + 8 * i, :] for i in range(3)]
            before = down(trans[u], 1, 1.0)
            for by in (1, 2, 4):
                before = before * down(before, by, 1.0)
            tinted = []
            inner = jnp.zeros((8, pixels), F32)
            for i in range(3):
                image = jnp.sum(before * local[i], axis=0, keepdims=True)
                images_ref[0, 0, 0, i, pl.ds(t, 1), :] = image
                residual = image - target_ref[0, 0, 0, i, pl.ds(t, 1), :]
                first = residual.astype(BF16).astype(F32)
                second = (residual - first).astype(BF16).astype(F32)
                g_rows[u, 18 + i : 19 + i, :] = first
                g_rows[u, 21 + i : 22 + i, :] = second
                g_rows[u, 24 + i : 25 + i, :] = first
                g_rows[u, 27 + i : 28 + i, :] = second
                tinted.append(before * residual)
                inner = inner + residual * local[i]
            q_scr[u] = dot(lhs[u], g_rows[u].astype(BF16), 1, 0)
            tinted_hi, tinted_lo = split2(jnp.concatenate(tinted, axis=0))
            tints.append(jnp.concatenate([tinted_hi.astype(F32), tinted_lo.astype(F32)], axis=0).astype(BF16))
            add = up(inner, 1, 0.0)
            scale = up(trans[u], 1, 0.0)
            for by in (1, 2, 4):
                add = add + scale * up(add, by, 0.0)
                scale = scale * up(scale, by, 0.0)
            behinds.append(add)
            befores.append(before)
        rows_out = []
        for u in lanes:
            colour_grad = (dot(whi_scr[u], tints[u], 1, 1) + dot(wlo_scr[u], tints[u], 1, 1)).T
            for i in range(3):
                both = colour_grad[8 * i : 8 * i + 8, :] + colour_grad[24 + 8 * i : 32 + 8 * i, :]
                rows_out.append(jnp.sum(own_chunk * both, axis=0, keepdims=True))
        for jj in reversed(range(entries // 16)):
            for u in lanes:
                g = [None, None]
                for h in (1, 0):
                    at = slice(16 * jj + 8 * h, 16 * jj + 8 * h + 8)
                    moved = a_scr[u, at, :] * (q_scr[u, at, :] - behinds[u])
                    behinds[u] = behinds[u] + moved
                    g[h] = (t_scr[u, at, :] * befores[u]) * moved
                at = slice(16 * jj, 16 * jj + 16)
                ghi_scr[u, at, :], glo_scr[u, at, :] = split2(jnp.concatenate(g, axis=0))
        for u in lanes:
            moments = dot(moment_basis, ghi_scr[u], 1, 1) + dot(moment_basis, glo_scr[u], 1, 1)
            for h in range(halves):
                columns = slice(h * LANES, (h + 1) * LANES)
                mom[h, pl.ds(ts[u], 8, stride=tiles), :] = moments[:, columns]
                for i in range(3):
                    mom[h, pl.ds((8 + i) * tiles + ts[u], 1), :] = rows_out[3 * u + i][:, columns]
        return carry

    for step in range(tiles // GROUP):
        group(step, 0)

    def got(i):
        return jnp.concatenate([mom[h, i * tiles : (i + 1) * tiles, :] for h in range(halves)], axis=1)

    m0, m1, m2, m3, m4, m5 = [got(i) for i in range(6)]
    su = m1 - mean_x * m0
    sv = m2 - mean_y * m0
    suu = m3 - mean_x * (m1 + su)
    suv = m4 - mean_x * m2 - mean_y * su
    svv = m5 - mean_y * (m2 + sv)
    grads = [
        LN2 * (2.0 * con_a * su + con_b * sv),
        LN2 * (con_b * su + 2.0 * con_c * sv),
        -0.5 * suu,
        -suv,
        -0.5 * svv,
        m0,
    ] + [got(8 + i) for i in range(3)]
    key_high, key_low = fold(high_ref[...], low_ref[...], rows)
    key_columns = key_low.astype(F32).T.astype(jnp.int32)
    for t in range(tiles):
        place_mask(mask_ref, t * entries, key_high[t : t + 1, :])
        place_hot(hot_ref, t * entries, key_columns[:, t : t + 1], fold_of(rows))
    parts = [exact_parts(g) for g in grads]
    for t in range(tiles):
        at = t * entries
        values = [[x[t : t + 1, :] for x in pair] for pair in parts]
        place_values(spread, at, mask_ref[:, at : at + entries], values)
    summed = dot(spread[...], hot_ref[...], 1, 0)
    wide = fold_of(rows)
    height = rows // wide
    total = table_rows // wide
    for f in range(FEATS):
        both = summed[f * total : (f + 1) * total, :] + summed[(FEATS + f) * total : (FEATS + f + 1) * total, :]
        for j in range(nd):
            for h in range(wide):
                outs[j][f, h * height : (h + 1) * height, :] = both[
                    j * height : (j + 1) * height, h * LANES : (h + 1) * LANES
                ]


def render(last, prepared, target, nd, rows, tiles, entries):
    pixels = SIDE * SIDE
    return pl.pallas_call(
        partial(render_kernel, nd=nd, rows=rows, tiles=tiles, entries=entries),
        in_specs=[vmem_spec()] * 7,
        out_specs=[vmem_spec()] * (nd + 1),
        out_shape=[jax.ShapeDtypeStruct((FEATS, rows, LANES), F32)] * nd
        + [jax.ShapeDtypeStruct(target.shape, F32)],
        scratch_shapes=[
            pltpu.VMEM((entries // LANES, 32 * tiles, LANES), F32),
            pltpu.VMEM((GROUP, entries, pixels), F32),
            pltpu.VMEM((GROUP, entries, pixels), F32),
            pltpu.VMEM((GROUP, entries, pixels), F32),
            pltpu.VMEM((GROUP, entries, pixels), BF16),
            pltpu.VMEM((GROUP, entries, pixels), BF16),
            pltpu.VMEM((GROUP, entries, pixels), BF16),
            pltpu.VMEM((GROUP, entries, pixels), BF16),
            pltpu.VMEM((GROUP, 32, pixels), F32),
            pltpu.VMEM((entries // LANES, 11 * tiles, LANES), F32),
            pltpu.VMEM((2 * FEATS * nd * rows // fold_of(rows), tiles * entries), BF16),
            pltpu.VMEM((nd * rows // fold_of(rows), tiles * entries), BF16),
            pltpu.VMEM((tiles * entries, fold_of(rows) * LANES), BF16),
        ],
        compiler_params=pltpu.CompilerParams(vmem_limit_bytes=48 * 1024 * 1024),
        name="render_tiles",
    )(last, *prepared, target)


def owner_index_kernel(own_ref, next_ref, idx_ref, mask_out, hot_low, hot_high, sum_out, spread, *, share):
    middle = idx_ref.shape[0] // 2
    rows = own_ref.shape[1]
    index = idx_ref[...]
    key_high, key_low = fold(index >> 7, index & (LANES - 1), share)
    key_columns = key_low.astype(F32).T.astype(jnp.int32)
    wide = fold_of(share)
    for n in range(idx_ref.shape[0]):
        place_mask(mask_out, n * LANES, key_high[n : n + 1, :])
        place_hot(hot_low if n < middle else hot_high, n % middle * LANES, key_columns[:, n : n + 1], wide)
    for j, ref in enumerate((own_ref, next_ref)):
        parts = [exact_parts(ref[f]) for f in range(FEATS)]
        for i in range(rows):
            at = (j * rows + i) * LANES
            values = [[x[i : i + 1, :] for x in pair] for pair in parts]
            place_values(spread, at, mask_out[:, at : at + LANES], values)
    sum_out[...] = dot(spread[...], hot_low[0 : 2 * rows * LANES, :], 1, 0)


def owner_indices(own, following, index, share, width):
    rows = own.shape[1]
    wide = fold_of(share)
    height = width // LANES // wide
    slots = index.shape[0] * LANES
    return pl.pallas_call(
        partial(owner_index_kernel, share=share),
        in_specs=[vmem_spec()] * 3,
        out_specs=[vmem_spec()] * 4,
        out_shape=[
            jax.ShapeDtypeStruct((height, slots), BF16),
            jax.ShapeDtypeStruct((slots // 2, wide * LANES), BF16),
            jax.ShapeDtypeStruct((slots // 2, wide * LANES), BF16),
            jax.ShapeDtypeStruct((2 * FEATS * height, wide * LANES), F32),
        ],
        scratch_shapes=[pltpu.VMEM((2 * FEATS * height, 2 * rows * LANES), BF16)],
        compiler_params=pltpu.CompilerParams(vmem_limit_bytes=40 * 1024 * 1024),
        name="prep_owner",
    )(own, following, index)


def owner_kernel(me_ref, *refs, nd, rows, parts, nv, nc, share):
    recv = refs[: nd - 2]
    mask_ref, hot_low, hot_high, sum_ref, w_ref = refs[nd - 2 : nd + 3]
    outs = refs[nd + 3 : nd + 3 + parts]
    spread, summed = refs[nd + 3 + parts :]
    my_view = me_ref[1]
    my_chip = me_ref[2]
    skip = 2 * rows * LANES
    for j in range(nd - 2):
        pairs = [exact_parts(recv[j][f]) for f in range(FEATS)]
        for i in range(rows):
            at = (j * rows + i) * LANES
            values = [[x[i : i + 1, :] for x in pair] for pair in pairs]
            place_values(spread, at, mask_ref[:, skip + at : skip + at + LANES], values)
    middle = hot_low.shape[0] - skip
    result = sum_ref[...] + dot(spread[:, middle:], hot_high[...], 1, 0)
    if middle > 0:
        result = result + dot(spread[:, 0:middle], hot_low[skip:, :], 1, 0)
    wide = fold_of(share)
    height = share // wide
    total = parts * height
    for f in range(FEATS):
        both = result[f * total : (f + 1) * total, :] + result[(FEATS + f) * total : (FEATS + f + 1) * total, :]
        for p in range(parts):
            for h in range(wide):
                summed[p, f, h * height : (h + 1) * height, :] = both[
                    p * height : (p + 1) * height, h * LANES : (h + 1) * LANES
                ]
    for p in range(parts):
        summed[p, FEATS] = w_ref[0:share, :]
    for dv in range(nv):
        for dc in range(nc):
            where = lax.rem(my_view + dv, nv) * nc + lax.rem(my_chip + dc, nc)
            outs[dv * nc + dc][...] = summed[where]


def owner_sums(me, received, prepared, weights, nd, rows, nv, nc, share):
    parts = nv * nc
    height, slots = prepared[0].shape
    return pl.pallas_call(
        partial(owner_kernel, nd=nd, rows=rows, parts=parts, nv=nv, nc=nc, share=share),
        in_specs=[smem_spec()] + [vmem_spec()] * (nd + 3),
        out_specs=[vmem_spec()] * parts,
        out_shape=[jax.ShapeDtypeStruct((FEATS + 1, share, LANES), F32)] * parts,
        scratch_shapes=[
            pltpu.VMEM((2 * FEATS * height, slots - 2 * rows * LANES), BF16),
            pltpu.VMEM((parts, FEATS + 1, share, LANES), F32),
        ],
        compiler_params=pltpu.CompilerParams(vmem_limit_bytes=40 * 1024 * 1024),
        name="owner_sums",
    )(me, *received, *prepared, weights)


def pulled(recv, params_ref, flat, out_ref, before_ref, *, nc, coefs):
    nv = len(recv) // nc
    share = recv[0].shape[1]
    columns = share * LANES

    def row(i):
        return params_ref[i : i + 1, :]

    lx, lyx, ly, lzx, lzy, lz = [row(i) for i in range(3, 9)]
    total = [jnp.zeros((1, columns), F32) for _ in range(10)]
    harmonics = [jnp.zeros((coefs, columns), F32) for _ in range(3)]
    square = lax.broadcasted_iota(jnp.int32, (coefs, LANES), 1) == lax.broadcasted_iota(
        jnp.int32, (coefs, LANES), 0
    ) + 10
    for v in range(nv):
        packed = recv[v * nc][FEATS]
        for i in range(share):
            block = recv[v * nc][0:FEATS, i, :]
            for c in range(1, nc):
                block = block + recv[v * nc + c][0:FEATS, i, :]
            flat[0:FEATS, i * LANES : (i + 1) * LANES] = block
        gx, gy, g0, g1, g2, gh, gr, gg, gb = [flat[f : f + 1, :] for f in range(FEATS)]
        cam = [[packed[i : i + 1, j : j + 1] for j in range(3)] for i in range(2)]
        for j in range(3):
            total[j] = total[j] + cam[0][j] * gx + cam[1][j] * gy
        m = []
        for i in range(2):
            a0, a1, a2 = cam[i]
            m.append((a0 * lx + a1 * lyx + a2 * lzx, a1 * ly + a2 * lzy, a2 * lz))
        upper = m[0][0] * m[0][0] + m[0][1] * m[0][1] + m[0][2] * m[0][2] + DILATION
        cross = m[0][0] * m[1][0] + m[0][1] * m[1][1] + m[0][2] * m[1][2]
        lower = m[1][0] * m[1][0] + m[1][1] * m[1][1] + m[1][2] * m[1][2] + DILATION
        inverse = 1.0 / (upper * lower - cross * cross)
        c0, c1, c2 = lower * inverse, -cross * inverse, upper * inverse
        h1 = 0.5 * g1
        k00, k01 = g0 * c0 + h1 * c1, g0 * c1 + h1 * c2
        k10, k11 = h1 * c0 + g2 * c1, h1 * c1 + g2 * c2
        s00 = -(c0 * k00 + c1 * k10)
        s01 = -(c0 * k01 + c1 * k11)
        s11 = -(c1 * k01 + c2 * k11)
        gm = [[2.0 * (s00 * m[0][k] + s01 * m[1][k]) for k in range(3)]]
        gm.append([2.0 * (s01 * m[0][k] + s11 * m[1][k]) for k in range(3)])
        at = 3
        for i in range(3):
            for k in range(i + 1):
                total[at] = total[at] + cam[0][i] * gm[0][k] + cam[1][i] * gm[1][k]
                at += 1
        total[9] = total[9] + gh
        basis = jnp.sum(jnp.where(square, packed[0:1, :], 0.0), axis=1, keepdims=True)
        for c, g in enumerate((gr, gg, gb)):
            harmonics[c] = harmonics[c] + basis * g
    logit = row(9)
    total[9] = total[9] / (1.0 + jnp.exp(logit))
    for i in range(10):
        out_ref[i : i + 1, :] = total[i] if before_ref is None else total[i] + before_ref[i : i + 1, :]
    for c in range(3):
        at = slice(10 + c * coefs, 10 + (c + 1) * coefs)
        out_ref[at, :] = harmonics[c] if before_ref is None else harmonics[c] + before_ref[at, :]


def pull_own_kernel(at_ref, params_ref, *refs, nc, coefs):
    out_ref, geometry_out, flat = refs[nc:]
    geometry_out[...] = params_ref[0:16, :]
    pulled(refs[:nc], params_ref, flat, out_ref, None, nc=nc, coefs=coefs)


def pull_own(at, params, received, parts, coefs):
    columns = params.shape[1] // parts
    block = received[0].shape
    count = params.shape[0]
    return pl.pallas_call(
        partial(pull_own_kernel, nc=len(received), coefs=coefs),
        grid_spec=pltpu.PrefetchScalarGridSpec(
            num_scalar_prefetch=1,
            grid=(1,),
            in_specs=[pl.BlockSpec((count, columns), lambda i, at_ref: (0, at_ref[0]))]
            + [pl.BlockSpec(block, lambda i, at_ref: (0, 0, 0))] * len(received),
            out_specs=[
                pl.BlockSpec((count, columns), lambda i, at_ref: (0, 0)),
                pl.BlockSpec((16, columns), lambda i, at_ref: (0, 0)),
            ],
            scratch_shapes=[pltpu.VMEM((16, columns), F32)],
        ),
        out_shape=[
            jax.ShapeDtypeStruct((count, columns), F32),
            jax.ShapeDtypeStruct((16, columns), F32),
        ],
        compiler_params=pltpu.CompilerParams(vmem_limit_bytes=40 * 1024 * 1024),
        name="prep_pull",
    )(at, params, *received)


def pull_rest_kernel(before_ref, geometry_ref, *refs, nc, coefs):
    out_ref, flat = refs[-2:]
    pulled(refs[:-2], geometry_ref, flat, out_ref, before_ref, nc=nc, coefs=coefs)


def pull_rest(before, geometry, received, nc, coefs):
    return pl.pallas_call(
        partial(pull_rest_kernel, nc=nc, coefs=coefs),
        in_specs=[vmem_spec()] * (2 + len(received)),
        out_specs=vmem_spec(),
        out_shape=jax.ShapeDtypeStruct(before.shape, F32),
        scratch_shapes=[pltpu.VMEM((16, before.shape[1]), F32)],
        compiler_params=pltpu.CompilerParams(vmem_limit_bytes=40 * 1024 * 1024),
        name="pull_back",
    )(before, geometry, *received)


def hop_order(nd, first):
    return [j for j in first if j < nd] + [j for j in range(1, nd) if j not in first]


def local(
    params,
    cameras,
    view_basis,
    tile_lists,
    margin_blocks,
    depth_orders,
    tile_counts,
    requests,
    target,
    *,
    nd,
    nv,
    nc,
):
    cap = requests.shape[4]
    rows = -(-cap // LANES)
    my_view = lax.axis_index("view")
    my_chip = lax.axis_index("chip")
    me = jnp.stack([lax.axis_index("dev"), my_view, my_chip]).astype(jnp.int32)
    at = (my_view * nc + my_chip).astype(jnp.int32).reshape(1)

    *packets, index, weights, features = send(me, cameras, view_basis, params, requests, nd, cap, rows)
    received = [None, *packets]
    for j in hop_order(nd, FORTH):
        received[j] = lax.ppermute(packets[j - 1], "dev", [(i, i ^ j) for i in range(nd)])
    prepared = tile_indices(
        me, features, index, margin_blocks, depth_orders, tile_counts, tile_lists, nd, cap
    )
    tiles, entries = margin_blocks.shape[3:]
    swapped = jnp.swapaxes(target, 3, 4)
    *prepared, part = prepared
    part = gather_more(received[1 : nd - 1], 1, prepared[0], prepared[1], part)
    *returns, images = render(received[nd - 1], (*prepared, part), swapped, nd, rows, tiles, entries)
    back = list(returns)
    for j in hop_order(nd, BACK):
        back[j] = lax.ppermute(returns[j], "dev", [(i, i ^ j) for i in range(nd)])
    share = params.shape[1] // LANES // (nv * nc)
    sorted_own = owner_indices(returns[0], back[1], index, share, params.shape[1])
    shares = owner_sums(me, back[2:], sorted_own, weights, nd, rows, nv, nc, share)
    arrived = []
    for dv in range(nv):
        for dc in range(nc):
            pairs = [
                (v * nc + c, (v + dv) % nv * nc + (c + dc) % nc) for v in range(nv) for c in range(nc)
            ]
            piece = shares[dv * nc + dc]
            arrived.append(piece if dv + dc == 0 else lax.ppermute(piece, ("view", "chip"), pairs))
    coefs = view_basis.shape[1]
    before, geometry = pull_own(at, params, arrived[:nc], nv * nc, coefs)
    grads = pull_rest(before, geometry, arrived[nc:], nc, coefs)
    return (grads, jnp.swapaxes(images, 3, 4))


def solution(mesh):
    return jax.shard_map(
        partial(local, nd=mesh.shape["dev"], nv=mesh.shape["view"], nc=mesh.shape["chip"]),
        mesh=mesh,
        in_specs=(
            P(None, ("groups", "dev")),
            P(("groups", "view"), None, None),
            P(("groups", "view"), None),
            P("view", ("groups", "dev"), "chip", None),
            P("view", ("groups", "dev"), "chip", None, None),
            P("view", ("groups", "dev"), "chip", None, None),
            P("view", ("groups", "dev"), "chip", None),
            P("view", None, "chip", ("groups", "dev"), None),
            P("view", ("groups", "dev"), "chip", None, None, None),
        ),
        out_specs=(
            P(None, ("groups", "dev", "view", "chip")),
            P("view", ("groups", "dev"), "chip", None, None, None),
        ),
        check_vma=False,
    )
```

```python
from functools import partial

import jax
import jax.numpy as jnp
from jax import lax
from jax.experimental import pallas as pl
from jax.experimental.pallas import tpu as pltpu
from jax.sharding import PartitionSpec as P

SIDE = 16
TW = 16
LANES = 128
LOG2E = 1.4426950408889634
LN2 = 0.6931471805599453
DILATION = 0.3
DEAD = -1e30
F32 = jnp.float32
BF16 = jnp.bfloat16
FEATS = 9
FORTH = (3, 2, 1)
BACK = (1, 2, 3)
GROUP = 8


def lane_take(row, index):
    return jnp.take_along_axis(row, index, axis=1, mode="promise_in_bounds")


def split2(x):
    hi = x.astype(BF16)
    return hi, (x - hi.astype(F32)).astype(BF16)


def dot(a, b, ca, cb):
    return lax.dot_general(a, b, (((ca,), (cb,)), ((), ())), preferred_element_type=F32)


def send_kernel(me_ref, cam_ref, basis_ref, params_ref, req_ref, *refs, nd, cap, rows):
    far_out, idx_out, w_out, feat, w_scr = refs
    me = me_ref[0]
    width = params_ref.shape[1]
    coefs = basis_ref.shape[-1]
    w_scr[...] = jnp.zeros_like(w_scr)
    w_scr[0:2, 0:4] = cam_ref[0]
    w_scr[2:3, 0:coefs] = basis_ref[...]
    packed = w_scr[...]
    lane8 = lax.broadcasted_iota(jnp.int32, (8, LANES), 1)
    row8 = lax.broadcasted_iota(jnp.int32, (8, LANES), 0)
    basis_row = jnp.broadcast_to(packed[2:3, :], (8, LANES))
    camera_row = jnp.where((row8 < 2), packed, 0.0)
    at10 = pltpu.roll(basis_row, 10, 1)
    w_out[...] = camera_row + jnp.where(row8 == 0, at10, 0.0)
    weights = jnp.where(lane8 < 3, camera_row, 0.0)
    weights = weights + jnp.where(row8 == 2, at10, 0.0)
    weights = weights + jnp.where(row8 == 3, pltpu.roll(basis_row, 10 + coefs, 1), 0.0)
    weights = weights + jnp.where(row8 == 4, pltpu.roll(basis_row, 10 + 2 * coefs, 1), 0.0)
    columns = weights.T
    last = params_ref.shape[0]

    def weighted(c, low, high):
        first, end = low // 8 * 8, min(-(-high // 8) * 8, last)
        return jnp.sum(params_ref[first:end, :] * columns[first:end, c : c + 1], axis=0, keepdims=True)

    linear = [weighted(0, 0, 3), weighted(1, 0, 3)]
    for c in range(3):
        linear.append(weighted(2 + c, 10 + c * coefs, 10 + (c + 1) * coefs))

    def cam(i, j):
        return cam_ref[0, i : i + 1, j : j + 1]

    def row(i):
        return params_ref[i : i + 1, :]

    lx, lyx, ly, lzx, lzy, lz = [row(i) for i in range(3, 9)]
    m = []
    for i in range(2):
        a0, a1, a2 = cam(i, 0), cam(i, 1), cam(i, 2)
        m.append((a0 * lx + a1 * lyx + a2 * lzx, a1 * ly + a2 * lzy, a2 * lz))
    upper = m[0][0] * m[0][0] + m[0][1] * m[0][1] + m[0][2] * m[0][2] + DILATION
    cross = m[0][0] * m[1][0] + m[0][1] * m[1][1] + m[0][2] * m[1][2]
    lower = m[1][0] * m[1][0] + m[1][1] * m[1][1] + m[1][2] * m[1][2] + DILATION
    inverse = 1.0 / (upper * lower - cross * cross)
    logit = row(9)
    log_opacity = jnp.minimum(logit, 0.0) * LOG2E - LOG2E * jnp.log(1.0 + jnp.exp(-jnp.abs(logit)))
    feat[0:1, :] = linear[0] + cam(0, 3)
    feat[1:2, :] = linear[1] + cam(1, 3)
    feat[2:3, :] = lower * inverse * (0.5 * LOG2E)
    feat[3:4, :] = -cross * inverse * LOG2E
    feat[4:5, :] = upper * inverse * (0.5 * LOG2E)
    feat[5:6, :] = log_opacity
    for c in range(3):
        feat[6 + c : 7 + c, :] = linear[2 + c] + 0.5

    idx_out[...] = jnp.zeros_like(idx_out)
    for j in range(nd):
        dest = me ^ j
        for i in range(rows):
            size = min(LANES, cap - i * LANES)
            idx_out[j * rows + i : j * rows + i + 1, 0:size] = req_ref[
                0, dest, 0, 0:1, i * LANES : i * LANES + size
            ]
    far = (nd - 1) * rows
    size = max(rows, 8)
    gathered = gather_features(feat, idx_out[nd * rows - size :, :])
    for f in range(FEATS):
        far_out[f] = gathered[f][far - nd * rows + size :, :]


def near_kernel(feat_ref, idx_ref, *outs):
    rows = outs[0].shape[1]
    total = len(outs) * rows
    step = 8 if rows % 8 == 0 else total
    for first in range(0, total, step):
        gathered = gather_features(feat_ref, idx_ref[rows + first : rows + first + step, :])
        size = min(rows, step)
        for f in range(FEATS):
            for n in range(0, step, size):
                j, i = divmod(first + n, rows)
                outs[j][f, i : i + size, :] = gathered[f][n : n + size, :]


def gather_near(features, index, nd, rows):
    return pl.pallas_call(
        near_kernel,
        in_specs=[vmem_spec()] * 2,
        out_specs=[vmem_spec()] * (nd - 2),
        out_shape=[jax.ShapeDtypeStruct((FEATS, rows, LANES), F32)] * (nd - 2),
        compiler_params=pltpu.CompilerParams(vmem_limit_bytes=40 * 1024 * 1024),
        name="prep_near",
    )(features, index)


def gather_features(feat, index):
    low = index & (LANES - 1)
    high = index >> 7
    acc = [jnp.zeros(index.shape, F32) for _ in range(FEATS)]
    for r in range(feat.shape[1] // LANES):
        here = high == r
        for f in range(FEATS):
            source = jnp.broadcast_to(feat[f : f + 1, r * LANES : (r + 1) * LANES], index.shape)
            acc[f] = jnp.where(here, lane_take(source, low), acc[f])
    return acc


def vmem_spec():
    return pl.BlockSpec(memory_space=pltpu.VMEM)


def smem_spec():
    return pl.BlockSpec(memory_space=pltpu.SMEM)


def send(me, cameras, basis, params, requests, nd, cap, rows):
    return pl.pallas_call(
        partial(send_kernel, nd=nd, cap=cap, rows=rows),
        in_specs=[smem_spec()] + [vmem_spec()] * 4,
        out_specs=[vmem_spec()] * 4,
        out_shape=[
            jax.ShapeDtypeStruct((FEATS, rows, LANES), F32),
            jax.ShapeDtypeStruct((nd * rows, LANES), jnp.int32),
            jax.ShapeDtypeStruct((8, LANES), F32),
            jax.ShapeDtypeStruct((16, params.shape[1]), F32),
        ],
        scratch_shapes=[pltpu.VMEM((8, LANES), F32)],
        compiler_params=pltpu.CompilerParams(vmem_limit_bytes=40 * 1024 * 1024),
        name="project_gather",
    )(me, cameras, basis, params, requests)


def fold_of(block):
    return 2 if block % 2 == 0 else 1


def fold(row, lane, block):
    wide = fold_of(block)
    height = block // wide
    inside = lax.rem(row, block)
    return lax.div(row, block) * height + lax.rem(inside, height), lax.div(inside, height) * LANES + lane


def place_hot(hot, at, column, wide):
    size = column.shape[0]
    lane = lax.broadcasted_iota(jnp.int32, (size, wide * LANES), 1)
    hot[at : at + size, :] = jnp.where(lane == column, 1.0, 0.0).astype(BF16)


def place_mask(mask, at, row):
    size = row.shape[1]
    high = lax.broadcasted_iota(jnp.int32, (mask.shape[0], size), 0)
    mask[:, at : at + size] = jnp.where(high == row, 1.0, 0.0).astype(BF16)


def place_values(spread, at, mask, values):
    height, size = mask.shape
    for f, pair in enumerate(values):
        for part, row in enumerate(pair):
            base = (part * FEATS + f) * height
            wide_row = jnp.broadcast_to(row, (height, size)).astype(BF16)
            spread[base : base + height, at : at + size] = mask * wide_row


def exact_parts(x):
    hi = x.astype(BF16).astype(F32)
    return hi, (x - hi).astype(BF16).astype(F32)


def take_rows(source, high, low, first_row, count, start):
    acc = list(start)
    for n in range(first_row, first_row + count):
        here = high == n
        for f in range(FEATS):
            value = jnp.broadcast_to(source(f, n), low.shape)
            acc[f] = jnp.where(here, lane_take(value, low), acc[f])
    return acc


def index_kernel(
    me_ref, feat_ref, idx_ref, blocks_ref, orders_ref, counts_ref, ids_ref, high_out, low_out, live_out, centre_out, part_out, own_ref, *, nd, cap
):
    me = me_ref[0]
    rows = own_ref.shape[1]
    own = gather_features(feat_ref, idx_ref[0 : max(rows, 8), :])
    for f in range(FEATS):
        own_ref[f] = own[f][0:rows, :]
    tiles, entries = blocks_ref.shape[3:]
    chunk = entries // 8
    halves = entries // LANES

    place = lax.broadcasted_iota(jnp.int32, (tiles, entries), 1)
    rank = (place & 7) * chunk + (place >> 3)

    def take_wide(source, index):
        parts = []
        for c in range(halves):
            wanted = index[:, c * LANES : (c + 1) * LANES]
            low = wanted & (LANES - 1)
            high = wanted >> 7
            value = lane_take(source[:, 0:LANES], low)
            for h in range(1, halves):
                value = jnp.where(high == h, lane_take(source[:, h * LANES : (h + 1) * LANES], low), value)
            parts.append(value)
        return jnp.concatenate(parts, axis=1)

    order = take_wide(orders_ref[0, 0, 0], rank)
    slot = take_wide(blocks_ref[0, 0, 0], order)
    shard = jnp.zeros_like(slot)
    for i in range(1, nd):
        shard = shard + (slot >= i * cap).astype(jnp.int32)
    offset = slot - shard * cap
    slot_row = (shard ^ me) * rows + (offset >> 7)
    slot_lane = offset & (LANES - 1)
    high_out[...] = slot_row
    low_out[...] = slot_lane
    tile_id = column_of(ids_ref, tiles)
    centre_out[0] = jnp.broadcast_to(((tile_id % TW) * SIDE).astype(F32) + 0.5 * SIDE, (tiles, LANES))
    centre_out[1] = jnp.broadcast_to(((tile_id // TW) * SIDE).astype(F32) + 0.5 * SIDE, (tiles, LANES))
    live_out[...] = jnp.where(rank < column_of(counts_ref, tiles), 1.0, 0.0)
    for c in range(halves):
        columns = slice(c * LANES, (c + 1) * LANES)
        for first in range(0, tiles, 8):
            low = slot_lane[first : first + 8, columns]
            high = slot_row[first : first + 8, columns]
            start = [jnp.zeros((8, LANES), F32)] * FEATS
            acc = take_rows(lambda f, n: own_ref[f, n : n + 1, :], high, low, 0, rows, start)
            for f in range(FEATS):
                part_out[f, first : first + 8, columns] = acc[f]


def tile_indices(me, features, index, blocks, orders, counts, ids, nd, cap):
    rows = index.shape[0] // nd
    tiles, entries = blocks.shape[3:]
    wide = fold_of(rows)
    return pl.pallas_call(
        partial(index_kernel, nd=nd, cap=cap),
        in_specs=[smem_spec()] + [vmem_spec()] * 6,
        out_specs=[vmem_spec()] * 5,
        out_shape=[
            jax.ShapeDtypeStruct((tiles, entries), jnp.int32),
            jax.ShapeDtypeStruct((tiles, entries), jnp.int32),
            jax.ShapeDtypeStruct((tiles, entries), F32),
            jax.ShapeDtypeStruct((2, tiles, LANES), F32),
            jax.ShapeDtypeStruct((FEATS, tiles, entries), F32),
        ],
        scratch_shapes=[pltpu.VMEM((FEATS, rows, LANES), F32)],
        compiler_params=pltpu.CompilerParams(vmem_limit_bytes=40 * 1024 * 1024),
        name="prep_tiles",
    )(me, features, index, blocks, orders, counts, ids)


def gather_kernel(*refs, first_block):
    recv = refs[:-4]
    high_ref, low_ref, part_ref, part_out = refs[-4:]
    rows = recv[0].shape[1]
    tiles, entries = high_ref.shape
    first_row = first_block * rows
    for c in range(entries // LANES):
        columns = slice(c * LANES, (c + 1) * LANES)
        for first in range(0, tiles, 8):
            block = slice(first, first + 8)
            start = [part_ref[f, block, columns] for f in range(FEATS)]

            def source(f, n):
                n = n - first_row
                return recv[n // rows][f, n % rows : n % rows + 1, :]

            acc = take_rows(
                source, high_ref[block, columns], low_ref[block, columns], first_row, len(recv) * rows, start
            )
            for f in range(FEATS):
                part_out[f, block, columns] = acc[f]


def gather_more(received, first_block, high, low, part):
    return pl.pallas_call(
        partial(gather_kernel, first_block=first_block),
        in_specs=[vmem_spec()] * (len(received) + 3),
        out_specs=vmem_spec(),
        out_shape=jax.ShapeDtypeStruct(part.shape, F32),
        compiler_params=pltpu.CompilerParams(vmem_limit_bytes=40 * 1024 * 1024),
        name="prep_gather",
    )(*received, high, low, part)


def column_of(ref, tiles):
    square = jnp.broadcast_to(ref[0, 0].astype(F32), (tiles, tiles))
    diagonal = lax.broadcasted_iota(jnp.int32, (tiles, tiles), 0) == lax.broadcasted_iota(jnp.int32, (tiles, tiles), 1)
    return jnp.sum(jnp.where(diagonal, square, 0.0), axis=1, keepdims=True).astype(jnp.int32)


def render_kernel(*refs, nd, rows, tiles, entries):
    last_ref, high_ref, low_ref, live_ref, centre_ref, part_ref, target_ref = refs[:7]
    outs = refs[7 : nd + 7]
    (images_ref, coef, a_scr, t_scr, q_scr, whi_scr, wlo_scr, ghi_scr, glo_scr, g_rows, mom, spread, mask_ref, hot_ref) = refs[nd + 7 :]
    pixels = SIDE * SIDE
    halves = entries // LANES
    table_rows = nd * rows

    def put(ref, at, value):
        for h in range(halves):
            ref[h, at : at + value.shape[0], :] = value[:, h * LANES : (h + 1) * LANES]

    centre_x = centre_ref[0, :, 0:1]
    centre_y = centre_ref[1, :, 0:1]
    live = live_ref[...] > 0.5

    pieces = [[[] for _ in range(halves)] for _ in range(FEATS)]
    for c in range(halves):
        columns = slice(c * LANES, (c + 1) * LANES)
        for first in range(0, tiles, 8):
            low = low_ref[first : first + 8, columns]
            high = high_ref[first : first + 8, columns]
            start = [part_ref[f, first : first + 8, columns] for f in range(FEATS)]
            acc = take_rows(
                lambda f, n: last_ref[f, n % rows : n % rows + 1, :], high, low, table_rows - rows, rows, start
            )
            for f in range(FEATS):
                pieces[f][c].append(acc[f])
    pieces = [[jnp.concatenate(p, axis=0) for p in both] for both in pieces]
    mean_x, mean_y, con_a, con_b, con_c, log_op, red, green, blue = [jnp.concatenate(p, axis=1) for p in pieces]
    mean_x = mean_x - centre_x
    mean_y = mean_y - centre_y
    bx = con_a * mean_x
    by = con_c * mean_y
    constant = log_op - (bx * mean_x + con_b * mean_x * mean_y + by * mean_y)
    constant = jnp.where(live, constant, DEAD)
    poly = [constant, 2.0 * bx + con_b * mean_y, 2.0 * by + con_b * mean_x, -con_a, -con_b, -con_c]
    for i, value in enumerate(poly):
        rest = value
        for part in range(3):
            piece = rest.astype(BF16).astype(F32)
            rest = rest - piece
            at = (6 * part + i) * tiles
            put(coef, at, piece)
    for i, value in enumerate((red, green, blue)):
        first = value.astype(BF16).astype(F32)
        second = (value - first).astype(BF16).astype(F32)
        for block, piece in enumerate((first, first, second, second)):
            at = (18 + 3 * block + i) * tiles
            put(coef, at, piece)
    coef[:, 30 * tiles : 32 * tiles, :] = jnp.zeros((halves, 2 * tiles, LANES), F32)

    pixel = lax.broadcasted_iota(jnp.int32, (1, pixels), 1)
    px = (pixel & (SIDE - 1)).astype(F32) + (0.5 - 0.5 * SIDE)
    py = (pixel >> 4).astype(F32) + (0.5 - 0.5 * SIDE)
    one = jnp.ones((1, pixels), F32)
    monomials = [one, px, py, px * px, px * py, py * py]
    zero = jnp.zeros((1, pixels), F32)
    basis_scr = g_rows.at[0]
    for part in range(3):
        for i in range(6):
            basis_scr[6 * part + i : 6 * part + i + 1, :] = monomials[i]
    basis_scr[18:32, :] = jnp.zeros((14, pixels), F32)
    basis = basis_scr[...].astype(BF16)
    moment_basis = jnp.concatenate(monomials + [zero, zero], axis=0).astype(BF16)
    g_rows[...] = jnp.zeros_like(g_rows)

    sub_e = lax.broadcasted_iota(jnp.int32, (8, entries), 0)
    own_chunk = jnp.where(sub_e == (lax.broadcasted_iota(jnp.int32, (8, entries), 1) & 7), 1.0, 0.0)
    sub_p = lax.broadcasted_iota(jnp.int32, (8, pixels), 0)

    def down(x, by, fill):
        return jnp.where(sub_p >= by, pltpu.roll(x, by, 0), fill)

    def up(x, by, fill):
        return jnp.where(sub_p < 8 - by, pltpu.roll(x, 8 - by, 0), fill)

    def group(step, carry):
        lanes = range(GROUP)
        ts = [step * GROUP + u for u in lanes]
        tables, lhs = [], []
        for u in lanes:
            table = [coef[h, pl.ds(ts[u], 32, stride=tiles), :] for h in range(halves)]
            tables.append(jnp.concatenate(table, axis=1))
            lhs.append(tables[u].T.astype(BF16))
            a_scr[u] = jnp.exp2(jnp.minimum(dot(lhs[u], basis, 1, 0), 0.0))
        trans = [jnp.ones((8, pixels), F32) for _ in lanes]
        for jj in range(entries // 16):
            for u in lanes:
                w = []
                for h in range(2):
                    at = slice(16 * jj + 8 * h, 16 * jj + 8 * h + 8)
                    t_scr[u, at, :] = trans[u]
                    value = trans[u] * a_scr[u, at, :]
                    trans[u] = trans[u] - value
                    w.append(value)
                at = slice(16 * jj, 16 * jj + 16)
                whi_scr[u, at, :], wlo_scr[u, at, :] = split2(jnp.concatenate(w, axis=0))
        befores, tints, behinds = [], [], []
        for u in lanes:
            table, t = tables[u], ts[u]
            colour = [own_chunk * table[18 + i : 19 + i, :] for i in range(3)]
            colour = colour + [own_chunk * table[24 + i : 25 + i, :] for i in range(3)]
            colour = jnp.concatenate(colour, axis=0).astype(BF16)
            local = dot(colour, whi_scr[u], 1, 0) + dot(colour, wlo_scr[u], 1, 0)
            local = [local[8 * i : 8 * i + 8, :] + local[24 + 8 * i : 32 + 8 * i, :] for i in range(3)]
            before = down(trans[u], 1, 1.0)
            for by in (1, 2, 4):
                before = before * down(before, by, 1.0)
            tinted = []
            inner = jnp.zeros((8, pixels), F32)
            for i in range(3):
                image = jnp.sum(before * local[i], axis=0, keepdims=True)
                images_ref[0, 0, 0, i, pl.ds(t, 1), :] = image
                residual = image - target_ref[0, 0, 0, i, pl.ds(t, 1), :]
                first = residual.astype(BF16).astype(F32)
                second = (residual - first).astype(BF16).astype(F32)
                g_rows[u, 18 + i : 19 + i, :] = first
                g_rows[u, 21 + i : 22 + i, :] = second
                g_rows[u, 24 + i : 25 + i, :] = first
                g_rows[u, 27 + i : 28 + i, :] = second
                tinted.append(before * residual)
                inner = inner + residual * local[i]
            q_scr[u] = dot(lhs[u], g_rows[u].astype(BF16), 1, 0)
            tinted_hi, tinted_lo = split2(jnp.concatenate(tinted, axis=0))
            tints.append(jnp.concatenate([tinted_hi.astype(F32), tinted_lo.astype(F32)], axis=0).astype(BF16))
            add = up(inner, 1, 0.0)
            scale = up(trans[u], 1, 0.0)
            for by in (1, 2, 4):
                add = add + scale * up(add, by, 0.0)
                scale = scale * up(scale, by, 0.0)
            behinds.append(add)
            befores.append(before)
        rows_out = []
        for u in lanes:
            colour_grad = (dot(whi_scr[u], tints[u], 1, 1) + dot(wlo_scr[u], tints[u], 1, 1)).T
            for i in range(3):
                both = colour_grad[8 * i : 8 * i + 8, :] + colour_grad[24 + 8 * i : 32 + 8 * i, :]
                rows_out.append(jnp.sum(own_chunk * both, axis=0, keepdims=True))
        for jj in reversed(range(entries // 16)):
            for u in lanes:
                g = [None, None]
                for h in (1, 0):
                    at = slice(16 * jj + 8 * h, 16 * jj + 8 * h + 8)
                    moved = a_scr[u, at, :] * (q_scr[u, at, :] - behinds[u])
                    behinds[u] = behinds[u] + moved
                    g[h] = (t_scr[u, at, :] * befores[u]) * moved
                at = slice(16 * jj, 16 * jj + 16)
                ghi_scr[u, at, :], glo_scr[u, at, :] = split2(jnp.concatenate(g, axis=0))
        for u in lanes:
            moments = dot(moment_basis, ghi_scr[u], 1, 1) + dot(moment_basis, glo_scr[u], 1, 1)
            for h in range(halves):
                columns = slice(h * LANES, (h + 1) * LANES)
                mom[h, pl.ds(ts[u], 8, stride=tiles), :] = moments[:, columns]
                for i in range(3):
                    mom[h, pl.ds((8 + i) * tiles + ts[u], 1), :] = rows_out[3 * u + i][:, columns]
        return carry

    for step in range(tiles // GROUP):
        group(step, 0)

    def got(i):
        return jnp.concatenate([mom[h, i * tiles : (i + 1) * tiles, :] for h in range(halves)], axis=1)

    m0, m1, m2, m3, m4, m5 = [got(i) for i in range(6)]
    su = m1 - mean_x * m0
    sv = m2 - mean_y * m0
    suu = m3 - mean_x * (m1 + su)
    suv = m4 - mean_x * m2 - mean_y * su
    svv = m5 - mean_y * (m2 + sv)
    grads = [
        LN2 * (2.0 * con_a * su + con_b * sv),
        LN2 * (con_b * su + 2.0 * con_c * sv),
        -0.5 * suu,
        -suv,
        -0.5 * svv,
        m0,
    ] + [got(8 + i) for i in range(3)]
    key_high, key_low = fold(high_ref[...], low_ref[...], rows)
    key_columns = key_low.astype(F32).T.astype(jnp.int32)
    for t in range(tiles):
        place_mask(mask_ref, t * entries, key_high[t : t + 1, :])
        place_hot(hot_ref, t * entries, key_columns[:, t : t + 1], fold_of(rows))
    parts = [exact_parts(g) for g in grads]
    for t in range(tiles):
        at = t * entries
        values = [[x[t : t + 1, :] for x in pair] for pair in parts]
        place_values(spread, at, mask_ref[:, at : at + entries], values)
    summed = dot(spread[...], hot_ref[...], 1, 0)
    wide = fold_of(rows)
    height = rows // wide
    total = table_rows // wide
    for f in range(FEATS):
        both = summed[f * total : (f + 1) * total, :] + summed[(FEATS + f) * total : (FEATS + f + 1) * total, :]
        for j in range(nd):
            for h in range(wide):
                outs[j][f, h * height : (h + 1) * height, :] = both[
                    j * height : (j + 1) * height, h * LANES : (h + 1) * LANES
                ]


def render(last, prepared, target, nd, rows, tiles, entries):
    pixels = SIDE * SIDE
    return pl.pallas_call(
        partial(render_kernel, nd=nd, rows=rows, tiles=tiles, entries=entries),
        in_specs=[vmem_spec()] * 7,
        out_specs=[vmem_spec()] * (nd + 1),
        out_shape=[jax.ShapeDtypeStruct((FEATS, rows, LANES), F32)] * nd
        + [jax.ShapeDtypeStruct(target.shape, F32)],
        scratch_shapes=[
            pltpu.VMEM((entries // LANES, 32 * tiles, LANES), F32),
            pltpu.VMEM((GROUP, entries, pixels), F32),
            pltpu.VMEM((GROUP, entries, pixels), F32),
            pltpu.VMEM((GROUP, entries, pixels), F32),
            pltpu.VMEM((GROUP, entries, pixels), BF16),
            pltpu.VMEM((GROUP, entries, pixels), BF16),
            pltpu.VMEM((GROUP, entries, pixels), BF16),
            pltpu.VMEM((GROUP, entries, pixels), BF16),
            pltpu.VMEM((GROUP, 32, pixels), F32),
            pltpu.VMEM((entries // LANES, 11 * tiles, LANES), F32),
            pltpu.VMEM((2 * FEATS * nd * rows // fold_of(rows), tiles * entries), BF16),
            pltpu.VMEM((nd * rows // fold_of(rows), tiles * entries), BF16),
            pltpu.VMEM((tiles * entries, fold_of(rows) * LANES), BF16),
        ],
        compiler_params=pltpu.CompilerParams(vmem_limit_bytes=48 * 1024 * 1024),
        name="render_tiles",
    )(last, *prepared, target)


def owner_index_kernel(own_ref, next_ref, idx_ref, mask_out, hot_low, hot_high, sum_out, spread, *, share):
    middle = idx_ref.shape[0] // 2
    rows = own_ref.shape[1]
    index = idx_ref[...]
    key_high, key_low = fold(index >> 7, index & (LANES - 1), share)
    key_columns = key_low.astype(F32).T.astype(jnp.int32)
    wide = fold_of(share)
    for n in range(idx_ref.shape[0]):
        place_mask(mask_out, n * LANES, key_high[n : n + 1, :])
        place_hot(hot_low if n < middle else hot_high, n % middle * LANES, key_columns[:, n : n + 1], wide)
    for j, ref in enumerate((own_ref, next_ref)):
        parts = [exact_parts(ref[f]) for f in range(FEATS)]
        for i in range(rows):
            at = (j * rows + i) * LANES
            values = [[x[i : i + 1, :] for x in pair] for pair in parts]
            place_values(spread, at, mask_out[:, at : at + LANES], values)
    sum_out[...] = dot(spread[...], hot_low[0 : 2 * rows * LANES, :], 1, 0)


def owner_indices(own, following, index, share, width):
    rows = own.shape[1]
    wide = fold_of(share)
    height = width // LANES // wide
    slots = index.shape[0] * LANES
    return pl.pallas_call(
        partial(owner_index_kernel, share=share),
        in_specs=[vmem_spec()] * 3,
        out_specs=[vmem_spec()] * 4,
        out_shape=[
            jax.ShapeDtypeStruct((height, slots), BF16),
            jax.ShapeDtypeStruct((slots // 2, wide * LANES), BF16),
            jax.ShapeDtypeStruct((slots // 2, wide * LANES), BF16),
            jax.ShapeDtypeStruct((2 * FEATS * height, wide * LANES), F32),
        ],
        scratch_shapes=[pltpu.VMEM((2 * FEATS * height, 2 * rows * LANES), BF16)],
        compiler_params=pltpu.CompilerParams(vmem_limit_bytes=40 * 1024 * 1024),
        name="prep_owner",
    )(own, following, index)


def owner_kernel(me_ref, *refs, nd, rows, parts, nv, nc, share):
    recv = refs[: nd - 2]
    mask_ref, hot_low, hot_high, sum_ref, w_ref = refs[nd - 2 : nd + 3]
    outs = refs[nd + 3 : nd + 3 + parts]
    spread, summed = refs[nd + 3 + parts :]
    my_view = me_ref[1]
    my_chip = me_ref[2]
    skip = 2 * rows * LANES
    for j in range(nd - 2):
        pairs = [exact_parts(recv[j][f]) for f in range(FEATS)]
        for i in range(rows):
            at = (j * rows + i) * LANES
            values = [[x[i : i + 1, :] for x in pair] for pair in pairs]
            place_values(spread, at, mask_ref[:, skip + at : skip + at + LANES], values)
    middle = hot_low.shape[0] - skip
    result = sum_ref[...] + dot(spread[:, middle:], hot_high[...], 1, 0)
    if middle > 0:
        result = result + dot(spread[:, 0:middle], hot_low[skip:, :], 1, 0)
    wide = fold_of(share)
    height = share // wide
    total = parts * height
    for f in range(FEATS):
        both = result[f * total : (f + 1) * total, :] + result[(FEATS + f) * total : (FEATS + f + 1) * total, :]
        for p in range(parts):
            for h in range(wide):
                summed[p, f, h * height : (h + 1) * height, :] = both[
                    p * height : (p + 1) * height, h * LANES : (h + 1) * LANES
                ]
    for p in range(parts):
        summed[p, FEATS] = w_ref[0:share, :]
    for dv in range(nv):
        for dc in range(nc):
            where = lax.rem(my_view + dv, nv) * nc + lax.rem(my_chip + dc, nc)
            outs[dv * nc + dc][...] = summed[where]


def owner_sums(me, received, prepared, weights, nd, rows, nv, nc, share):
    parts = nv * nc
    height, slots = prepared[0].shape
    return pl.pallas_call(
        partial(owner_kernel, nd=nd, rows=rows, parts=parts, nv=nv, nc=nc, share=share),
        in_specs=[smem_spec()] + [vmem_spec()] * (nd + 3),
        out_specs=[vmem_spec()] * parts,
        out_shape=[jax.ShapeDtypeStruct((FEATS + 1, share, LANES), F32)] * parts,
        scratch_shapes=[
            pltpu.VMEM((2 * FEATS * height, slots - 2 * rows * LANES), BF16),
            pltpu.VMEM((parts, FEATS + 1, share, LANES), F32),
        ],
        compiler_params=pltpu.CompilerParams(vmem_limit_bytes=40 * 1024 * 1024),
        name="owner_sums",
    )(me, *received, *prepared, weights)


def pulled(recv, params_ref, flat, out_ref, before_ref, *, nc, coefs):
    nv = len(recv) // nc
    share = recv[0].shape[1]
    columns = share * LANES

    def row(i):
        return params_ref[i : i + 1, :]

    lx, lyx, ly, lzx, lzy, lz = [row(i) for i in range(3, 9)]
    total = [jnp.zeros((1, columns), F32) for _ in range(10)]
    harmonics = [jnp.zeros((coefs, columns), F32) for _ in range(3)]
    square = lax.broadcasted_iota(jnp.int32, (coefs, LANES), 1) == lax.broadcasted_iota(
        jnp.int32, (coefs, LANES), 0
    ) + 10
    for v in range(nv):
        packed = recv[v * nc][FEATS]
        for i in range(share):
            block = recv[v * nc][0:FEATS, i, :]
            for c in range(1, nc):
                block = block + recv[v * nc + c][0:FEATS, i, :]
            flat[0:FEATS, i * LANES : (i + 1) * LANES] = block
        gx, gy, g0, g1, g2, gh, gr, gg, gb = [flat[f : f + 1, :] for f in range(FEATS)]
        cam = [[packed[i : i + 1, j : j + 1] for j in range(3)] for i in range(2)]
        for j in range(3):
            total[j] = total[j] + cam[0][j] * gx + cam[1][j] * gy
        m = []
        for i in range(2):
            a0, a1, a2 = cam[i]
            m.append((a0 * lx + a1 * lyx + a2 * lzx, a1 * ly + a2 * lzy, a2 * lz))
        upper = m[0][0] * m[0][0] + m[0][1] * m[0][1] + m[0][2] * m[0][2] + DILATION
        cross = m[0][0] * m[1][0] + m[0][1] * m[1][1] + m[0][2] * m[1][2]
        lower = m[1][0] * m[1][0] + m[1][1] * m[1][1] + m[1][2] * m[1][2] + DILATION
        inverse = 1.0 / (upper * lower - cross * cross)
        c0, c1, c2 = lower * inverse, -cross * inverse, upper * inverse
        h1 = 0.5 * g1
        k00, k01 = g0 * c0 + h1 * c1, g0 * c1 + h1 * c2
        k10, k11 = h1 * c0 + g2 * c1, h1 * c1 + g2 * c2
        s00 = -(c0 * k00 + c1 * k10)
        s01 = -(c0 * k01 + c1 * k11)
        s11 = -(c1 * k01 + c2 * k11)
        gm = [[2.0 * (s00 * m[0][k] + s01 * m[1][k]) for k in range(3)]]
        gm.append([2.0 * (s01 * m[0][k] + s11 * m[1][k]) for k in range(3)])
        at = 3
        for i in range(3):
            for k in range(i + 1):
                total[at] = total[at] + cam[0][i] * gm[0][k] + cam[1][i] * gm[1][k]
                at += 1
        total[9] = total[9] + gh
        basis = jnp.sum(jnp.where(square, packed[0:1, :], 0.0), axis=1, keepdims=True)
        for c, g in enumerate((gr, gg, gb)):
            harmonics[c] = harmonics[c] + basis * g
    logit = row(9)
    total[9] = total[9] / (1.0 + jnp.exp(logit))
    for i in range(10):
        out_ref[i : i + 1, :] = total[i] if before_ref is None else total[i] + before_ref[i : i + 1, :]
    for c in range(3):
        at = slice(10 + c * coefs, 10 + (c + 1) * coefs)
        out_ref[at, :] = harmonics[c] if before_ref is None else harmonics[c] + before_ref[at, :]


def pull_own_kernel(at_ref, params_ref, *refs, nc, coefs):
    out_ref, geometry_out, flat = refs[nc:]
    geometry_out[...] = params_ref[0:16, :]
    pulled(refs[:nc], params_ref, flat, out_ref, None, nc=nc, coefs=coefs)


def pull_own(at, params, received, parts, coefs):
    columns = params.shape[1] // parts
    block = received[0].shape
    count = params.shape[0]
    return pl.pallas_call(
        partial(pull_own_kernel, nc=len(received), coefs=coefs),
        grid_spec=pltpu.PrefetchScalarGridSpec(
            num_scalar_prefetch=1,
            grid=(1,),
            in_specs=[pl.BlockSpec((count, columns), lambda i, at_ref: (0, at_ref[0]))]
            + [pl.BlockSpec(block, lambda i, at_ref: (0, 0, 0))] * len(received),
            out_specs=[
                pl.BlockSpec((count, columns), lambda i, at_ref: (0, 0)),
                pl.BlockSpec((16, columns), lambda i, at_ref: (0, 0)),
            ],
            scratch_shapes=[pltpu.VMEM((16, columns), F32)],
        ),
        out_shape=[
            jax.ShapeDtypeStruct((count, columns), F32),
            jax.ShapeDtypeStruct((16, columns), F32),
        ],
        compiler_params=pltpu.CompilerParams(vmem_limit_bytes=40 * 1024 * 1024),
        name="prep_pull",
    )(at, params, *received)


def pull_rest_kernel(before_ref, geometry_ref, *refs, nc, coefs):
    out_ref, flat = refs[-2:]
    pulled(refs[:-2], geometry_ref, flat, out_ref, before_ref, nc=nc, coefs=coefs)


def pull_rest(before, geometry, received, nc, coefs):
    return pl.pallas_call(
        partial(pull_rest_kernel, nc=nc, coefs=coefs),
        in_specs=[vmem_spec()] * (2 + len(received)),
        out_specs=vmem_spec(),
        out_shape=jax.ShapeDtypeStruct(before.shape, F32),
        scratch_shapes=[pltpu.VMEM((16, before.shape[1]), F32)],
        compiler_params=pltpu.CompilerParams(vmem_limit_bytes=40 * 1024 * 1024),
        name="pull_back",
    )(before, geometry, *received)


def hop_order(nd, first):
    return [j for j in first if j < nd] + [j for j in range(1, nd) if j not in first]


def local(
    params,
    cameras,
    view_basis,
    tile_lists,
    margin_blocks,
    depth_orders,
    tile_counts,
    requests,
    target,
    *,
    nd,
    nv,
    nc,
):
    cap = requests.shape[4]
    rows = -(-cap // LANES)
    my_view = lax.axis_index("view")
    my_chip = lax.axis_index("chip")
    me = jnp.stack([lax.axis_index("dev"), my_view, my_chip]).astype(jnp.int32)
    at = (my_view * nc + my_chip).astype(jnp.int32).reshape(1)

    far, index, weights, features = send(me, cameras, view_basis, params, requests, nd, cap, rows)
    packets = [*gather_near(features, index, nd, rows), far]
    received = [None, *packets]
    for j in hop_order(nd, FORTH):
        received[j] = lax.ppermute(packets[j - 1], "dev", [(i, i ^ j) for i in range(nd)])
    prepared = tile_indices(
        me, features, index, margin_blocks, depth_orders, tile_counts, tile_lists, nd, cap
    )
    tiles, entries = margin_blocks.shape[3:]
    swapped = jnp.swapaxes(target, 3, 4)
    *prepared, part = prepared
    part = gather_more(received[1 : nd - 1], 1, prepared[0], prepared[1], part)
    *returns, images = render(received[nd - 1], (*prepared, part), swapped, nd, rows, tiles, entries)
    back = list(returns)
    for j in hop_order(nd, BACK):
        back[j] = lax.ppermute(returns[j], "dev", [(i, i ^ j) for i in range(nd)])
    share = params.shape[1] // LANES // (nv * nc)
    sorted_own = owner_indices(returns[0], back[1], index, share, params.shape[1])
    shares = owner_sums(me, back[2:], sorted_own, weights, nd, rows, nv, nc, share)
    arrived = []
    for dv in range(nv):
        for dc in range(nc):
            pairs = [
                (v * nc + c, (v + dv) % nv * nc + (c + dc) % nc) for v in range(nv) for c in range(nc)
            ]
            piece = shares[dv * nc + dc]
            arrived.append(piece if dv + dc == 0 else lax.ppermute(piece, ("view", "chip"), pairs))
    coefs = view_basis.shape[1]
    before, geometry = pull_own(at, params, arrived[:nc], nv * nc, coefs)
    grads = pull_rest(before, geometry, arrived[nc:], nc, coefs)
    return (grads, jnp.swapaxes(images, 3, 4))


def solution(mesh):
    return jax.shard_map(
        partial(local, nd=mesh.shape["dev"], nv=mesh.shape["view"], nc=mesh.shape["chip"]),
        mesh=mesh,
        in_specs=(
            P(None, ("groups", "dev")),
            P(("groups", "view"), None, None),
            P(("groups", "view"), None),
            P("view", ("groups", "dev"), "chip", None),
            P("view", ("groups", "dev"), "chip", None, None),
            P("view", ("groups", "dev"), "chip", None, None),
            P("view", ("groups", "dev"), "chip", None),
            P("view", None, "chip", ("groups", "dev"), None),
            P("view", ("groups", "dev"), "chip", None, None, None),
        ),
        out_specs=(
            P(None, ("groups", "dev", "view", "chip")),
            P("view", ("groups", "dev"), "chip", None, None, None),
        ),
        check_vma=False,
    )
```
